32 devices in a mesh: tensor: 2 (over x), context: 16 (over z, y, core).
Axes of the slice: x: 2, y: 2, z: 4, core: 2. Of those that a mesh axis runs over, the one named last changes fastest.
Arguments:
- q_proj: bfloat16 [4096, 8192], P('context', 'tensor'), may hold values from -6 to 6
- k_proj: bfloat16 [4096, 8192], P('context', 'tensor'), may hold values from -6 to 6
- v_proj: bfloat16 [4096, 8192], P('context', 'tensor'), may hold values from -6 to 6
- short_filter: bfloat16 [3, 3, 512], P(None, None, 'tensor'), may hold values from -3.5 to 3.5
- residue: float32 [16, 8192], P(None, 'tensor'), may hold values from -1.5 to 1.5
- decay_rate: float32 [16, 8192], P(None, 'tensor'), may hold values from 0.5 to 128
- out_weight: bfloat16 [4096, 8192], P('context', 'tensor'), may hold values from -0.0625 to 0.0625
Outputs:
- projected: bfloat16 [4096, 4096], P('tensor', 'context')
The draws below stay inside these ranges and needn't reach their ends.
All inputs are finite; a program needn't handle non-finite values.
Results may differ from the reference program's by a relative error of at most 0.02.
Values may be sent and summed in bfloat16 or wider, within the bound.
No kernel may reach another device: no remote copies, remote signals or barrier semaphores. Data moves between devices by JAX's collectives and lax.ppermute only.
A program may use at most 256 MiB of HBM per device.

```python
import math
import jax
import jax.numpy as jnp
from jax import lax

D = 8192
DOUT = 4096
GROUP = 16
STAPS = 3
MODES = 16
TOKENS = 4096
GROUPS = 512
N_TENSOR = 2


def levels(rng, shape, shards, smallest, top_value):
    level = 1.0
    for dim, shards_of in shards:
        draws = jax.random.uniform(jax.random.fold_in(jax.random.fold_in(rng, 6), dim), (shards_of,), jnp.float32, smallest / len(shards), top_value / len(shards))
        level = level * jnp.repeat(jnp.exp(draws), shape[dim] // shards_of).reshape((-1,) + (1,) * (len(shape) - 1 - dim))
    return level


def normal_values(own_key, dims, deviation, limit, split=(), kind=jnp.bfloat16):
    drawn = deviation * jax.random.normal(own_key, dims, jnp.float32)
    if split:
        drawn = drawn * levels(own_key, dims, split, -0.22, 0.18)
    return jnp.clip(drawn, -limit, limit).astype(kind)


def setup_inputs(seed: int = 0) -> dict:
    arg_keys = jax.random.split(jax.random.key(seed), 8)
    q_proj = normal_values(arg_keys[0], (TOKENS, D), 1.0, 6.0, ((0, 16), (1, 2)))
    k_proj = normal_values(arg_keys[1], (TOKENS, D), 1.0, 6.0, ((0, 16), (1, 2)))
    v_proj = normal_values(arg_keys[2], (TOKENS, D), 1.0, 6.0, ((0, 16), (1, 2)))
    short_filter = normal_values(arg_keys[3], (3, STAPS, GROUPS), STAPS ** -0.5, 3.5, ((2, 2),))
    residue = normal_values(arg_keys[4], (MODES, D), 0.25, 1.5, ((1, 2),), jnp.float32)
    decay_rate = jnp.clip(jnp.exp(math.log(128.0) - 5.5451774 * jax.random.uniform(arg_keys[5], (MODES, D), jnp.float32) ** levels(arg_keys[5], (MODES, D), ((1, 2),), -0.2, 0.2)), 0.5, 128.0)
    out_weight = normal_values(arg_keys[6], (DOUT, D), D ** -0.5, 0.0625, ((0, 16), (1, 2)))
    return dict(q_proj=q_proj, k_proj=k_proj, v_proj=v_proj, short_filter=short_filter, residue=residue, decay_rate=decay_rate, out_weight=out_weight)


def causal_taps(signal, filters):
    tap_count = filters.shape[0]
    length_rows = signal.shape[0]
    padded = jnp.pad(signal, ((tap_count - 1, 0), (0, 0)))
    running = jnp.zeros_like(signal)
    for offset in range(tap_count):
        begin = tap_count - 1 - offset
        running = running + filters[offset] * padded[begin:begin + length_rows]
    return running

def reference(q_proj, k_proj, v_proj, short_filter, residue, decay_rate, out_weight):
    chan_count = q_proj.shape[1]
    chan_block = math.gcd(chan_count, 256)
    block_total = chan_count // chan_block
    short_wide = jnp.repeat(short_filter.astype(jnp.float32), GROUP, axis=2)
    decay_step = decay_rate / TOKENS
    mode_scale = residue * jnp.sqrt(2.0 * decay_step)
    positions = jnp.arange(TOKENS).astype(jnp.float32)
    fft_length = 2 * TOKENS

    def one_block(block_index):
        first_chan = (block_index * chan_block).astype(jnp.int32)

        def columns(source, along_dim):
            return lax.dynamic_slice_in_dim(source, first_chan, chan_block, along_dim)
        q_feat = causal_taps(columns(q_proj, 1).astype(jnp.float32), columns(short_wide[0], 1)).astype(jnp.bfloat16)
        k_feat = causal_taps(columns(k_proj, 1).astype(jnp.float32), columns(short_wide[1], 1)).astype(jnp.bfloat16)
        v_feat = causal_taps(columns(v_proj, 1).astype(jnp.float32), columns(short_wide[2], 1)).astype(jnp.bfloat16)
        product = (k_feat.astype(jnp.float32) * v_feat.astype(jnp.float32)).astype(jnp.bfloat16)
        steps_block = columns(decay_step, 1)
        scale_block = columns(mode_scale, 1)
        response = jnp.zeros((TOKENS, chan_block), jnp.float32)
        for mode_index in range(MODES):
            response = response + scale_block[mode_index] * jnp.exp(-steps_block[mode_index] * positions[:, None])
        spectrum = jnp.fft.rfft(product.astype(jnp.float32), n=fft_length, axis=0) * jnp.fft.rfft(response, n=fft_length, axis=0)
        mixed = jnp.fft.irfft(spectrum, n=fft_length, axis=0)[:TOKENS].astype(jnp.float32)
        return (q_feat.astype(jnp.float32) * mixed).astype(jnp.bfloat16)
    stacked = lax.map(one_block, jnp.arange(block_total).astype(jnp.int32))
    gated = jnp.transpose(stacked, (1, 0, 2)).reshape(TOKENS, chan_count)
    shard_chans = chan_count // N_TENSOR
    running = jnp.zeros((DOUT, TOKENS), jnp.float32)
    for shard_index in range(N_TENSOR):
        low_chan = shard_index * shard_chans
        partial_term = lax.dot_general(out_weight[:, low_chan:low_chan + shard_chans], gated[:, low_chan:low_chan + shard_chans], (((1,), (1,)), ((), ())), preferred_element_type=jnp.float32)
        rounded = lax.optimization_barrier(partial_term.astype(jnp.bfloat16))
        running = running + rounded.astype(jnp.float32)
    return running.astype(jnp.bfloat16)
```

```python
import functools

import jax
import jax.numpy as jnp
from jax import lax
from jax.experimental import pallas as pl
from jax.experimental.pallas import tpu as pltpu
from jax.sharding import PartitionSpec as P

LANES = 128
SEGS = 8
CREW = 4
PLANES = 4
F32 = jnp.float32
BF16 = jnp.bfloat16


def lane_block(chan_count):
    return 512 if chan_count % 512 == 0 else LANES


def tree_sum(terms):
    terms = list(terms)
    while len(terms) > 1:
        paired = [terms[i] + terms[i + 1] for i in range(0, len(terms) - 1, 2)]
        if len(terms) % 2:
            paired.append(terms[-1])
        terms = paired
    return terms[0]


def spread(row):
    return jnp.broadcast_to(row, (SEGS, LANES))


def local_kernel(
    total, q_ref, k_ref, v_ref, rim_ref, taps_ref, decay_ref, residue_ref,
    qf_ref, y_ref, carry_ref, end_ref, shifted, signal,
):
    rows, width = q_ref.shape
    modes = decay_ref.shape[0]
    length = rows // SEGS
    tap_count = taps_ref.shape[0] // 3
    lead = tap_count - 1

    def short_pass(which, ref, lanes):
        pad = shifted.at[which]
        pad[SEGS : SEGS + rows, :] = ref[:, lanes].astype(F32)
        pad[SEGS - lead : SEGS, :] = rim_ref[which * lead : (which + 1) * lead, lanes]
        running = None
        for offset in range(tap_count):
            row = which * tap_count + offset
            term = taps_ref[row : row + 1, lanes] * pad[SEGS - offset : SEGS - offset + rows, :]
            running = term if running is None else running + term
        return running.astype(BF16)

    for block in range(width // LANES):
        lanes = slice(block * LANES, (block + 1) * LANES)
        qf_ref[:, lanes] = short_pass(0, q_ref, lanes)
        k_feat = short_pass(1, k_ref, lanes).astype(F32)
        v_feat = short_pass(2, v_ref, lanes).astype(F32)
        signal[block] = (k_feat * v_feat).astype(BF16).astype(F32)

    seg = lax.broadcasted_iota(jnp.int32, (SEGS, LANES), 0)
    for block in range(width // LANES):
        lanes = slice(block * LANES, (block + 1) * LANES)
        steps = decay_ref[:, lanes] / total
        decays = jnp.exp(-steps)
        scales = residue_ref[:, lanes] * jnp.sqrt(2.0 * steps)
        decay = [spread(decays[m : m + 1]) for m in range(modes)]
        scale = [spread(scales[m : m + 1]) for m in range(modes)]

        def advance(i, state):
            x = signal[block, pl.ds(i, SEGS, stride=length), :]
            state = tuple(d * s + x for d, s in zip(decay, state))
            y_ref[i, :, lanes] = tree_sum(c * s for c, s in zip(scale, state))
            return state

        zero = jnp.zeros((SEGS, LANES), F32)
        state = lax.fori_loop(0, length, advance, (zero,) * modes, unroll=4)
        for m in range(modes):
            ends = state[m]
            for hop in (1, 2, 4):
                factor = spread(jnp.exp(-steps[m : m + 1] * float(length * hop)))
                ends = ends + factor * jnp.where(seg >= hop, pltpu.roll(ends, hop, 0), 0.0)
            end_ref[m : m + 1, lanes] = ends[SEGS - 1 : SEGS]
            carry_ref[m, :, lanes] = jnp.where(seg >= 1, pltpu.roll(ends, 1, 0), 0.0)


def gate_kernel(
    total, qf_ref, y_ref, carry_ref, incoming_ref, decay_ref, residue_ref, out_ref, mixed
):
    rows, width = qf_ref.shape
    modes = decay_ref.shape[0]
    length = rows // SEGS
    begin = (lax.broadcasted_iota(jnp.int32, (SEGS, LANES), 0) * length).astype(F32)
    for block in range(width // LANES):
        lanes = slice(block * LANES, (block + 1) * LANES)
        steps = decay_ref[:, lanes] / total
        decays = jnp.exp(-steps)
        weights = residue_ref[:, lanes] * jnp.sqrt(2.0 * steps) * decays
        decay = [spread(decays[m : m + 1]) for m in range(modes)]
        tail = []
        for m in range(modes):
            reach = jnp.exp(-spread(steps[m : m + 1]) * begin)
            held = carry_ref[m, :, lanes] + reach * spread(incoming_ref[m : m + 1, lanes])
            tail.append(spread(weights[m : m + 1]) * held)

        def advance(i, tail):
            mixed[block, pl.ds(i, SEGS, stride=length), :] = y_ref[i, :, lanes] + tree_sum(tail)
            return tuple(d * s for d, s in zip(decay, tail))

        lax.fori_loop(0, length, advance, tuple(tail), unroll=4)
    for block in range(width // LANES):
        lanes = slice(block * LANES, (block + 1) * LANES)
        out_ref[:, lanes] = (qf_ref[:, lanes].astype(F32) * mixed[block]).astype(BF16)


def local_pass(q_proj, k_proj, v_proj, rims, taps, decay_rate, residue, total):
    rows, chan_count = q_proj.shape
    modes = decay_rate.shape[0]
    width = lane_block(chan_count)
    length = rows // SEGS

    def cols(height):
        return pl.BlockSpec((height, width), lambda c: (0, c))

    return pl.pallas_call(
        functools.partial(local_kernel, total),
        grid=(chan_count // width,),
        in_specs=[
            cols(rows), cols(rows), cols(rows), cols(rims.shape[0]), cols(taps.shape[0]),
            cols(modes), cols(modes),
        ],
        out_specs=[
            cols(rows),
            pl.BlockSpec((length, SEGS, width), lambda c: (0, 0, c)),
            pl.BlockSpec((modes, SEGS, width), lambda c: (0, 0, c)),
            cols(modes),
        ],
        out_shape=[
            jax.ShapeDtypeStruct((rows, chan_count), BF16),
            jax.ShapeDtypeStruct((length, SEGS, chan_count), F32),
            jax.ShapeDtypeStruct((modes, SEGS, chan_count), F32),
            jax.ShapeDtypeStruct((modes, chan_count), F32),
        ],
        scratch_shapes=[
            pltpu.VMEM((3, rows + SEGS, LANES), F32),
            pltpu.VMEM((width // LANES, rows, LANES), F32),
        ],
        compiler_params=pltpu.CompilerParams(vmem_limit_bytes=32 * 2**20),
        name="local_pass",
    )(q_proj, k_proj, v_proj, rims, taps, decay_rate, residue)


def gate_pass(q_feat, y_local, carry, incoming, decay_rate, residue, total):
    rows, chan_count = q_feat.shape
    modes = decay_rate.shape[0]
    width = lane_block(chan_count)
    length = rows // SEGS

    def cols(height):
        return pl.BlockSpec((height, width), lambda c: (0, c))

    return pl.pallas_call(
        functools.partial(gate_kernel, total),
        grid=(chan_count // width,),
        in_specs=[
            cols(rows),
            pl.BlockSpec((length, SEGS, width), lambda c: (0, 0, c)),
            pl.BlockSpec((modes, SEGS, width), lambda c: (0, 0, c)),
            cols(modes), cols(modes), cols(modes),
        ],
        out_specs=cols(rows),
        out_shape=jax.ShapeDtypeStruct((rows, chan_count), BF16),
        scratch_shapes=[pltpu.VMEM((width // LANES, rows, LANES), F32)],
        compiler_params=pltpu.CompilerParams(vmem_limit_bytes=32 * 2**20),
        name="gate_pass",
    )(q_feat, y_local, carry, incoming, decay_rate, residue)


def product_kernel(slot_count, pick_ref, *refs):
    pairs = [refs[2 * s : 2 * s + 2] for s in range(slot_count)]
    tokens = refs[2 * slot_count : 2 * slot_count + CREW]
    out_ref, total = refs[2 * slot_count + CREW :]
    feat = pairs[0][0].shape[0]
    step = pl.program_id(0)

    @pl.when(step == 0)
    def _():
        total[...] = jnp.zeros_like(total)

    for s, (one, other) in enumerate(pairs):
        for first, source in ((1, one), (0, other)):

            @pl.when(pick_ref[s] == first)
            def _():
                weights = source[...]
                for j in range(CREW):
                    total[j, s * feat : (s + 1) * feat, :] += lax.dot_general(
                        weights, tokens[j][...], (((1,), (1,)), ((), ())),
                        preferred_element_type=F32,
                    )

    @pl.when(step == pl.num_programs(0) - 1)
    def _():
        out_ref[...] = total[...].astype(BF16)


def project(pairs, picks, tokens):
    feat, depth = pairs[0][0].shape
    rows = tokens[0].shape[0]
    slot_count = len(pairs)
    width = 1024 if depth % 1024 == 0 else LANES
    flat = [array for pair in pairs for array in pair]
    out_rows = slot_count * feat
    return pl.pallas_call(
        functools.partial(product_kernel, slot_count),
        grid_spec=pltpu.PrefetchScalarGridSpec(
            num_scalar_prefetch=1,
            grid=(depth // width,),
            in_specs=[pl.BlockSpec((feat, width), lambda c, _: (0, c)) for _ in flat]
            + [pl.BlockSpec((rows, width), lambda c, _: (0, c)) for _ in tokens],
            out_specs=pl.BlockSpec((CREW, out_rows, rows), lambda c, _: (0, 0, 0)),
            scratch_shapes=[pltpu.VMEM((CREW, out_rows, rows), F32)],
        ),
        out_shape=jax.ShapeDtypeStruct((CREW, out_rows, rows), BF16),
        compiler_params=pltpu.CompilerParams(vmem_limit_bytes=48 * 2**20),
        name="project",
    )(jnp.stack(picks).astype(jnp.int32), *flat, *tokens)


def assemble_kernel(place_ref, *refs):
    near, third, fourth, out_ref = refs[:CREW], refs[CREW : 2 * CREW], refs[2 * CREW : -1], refs[-1]
    feat = third[0].shape[0]
    half = out_ref.shape[0] // 2
    same, low, seat = place_ref[0], place_ref[1], place_ref[2]
    for j in range(CREW):
        within = (seat ^ j) * feat
        first = pl.multiple_of(low * half + within, feat)
        second = pl.multiple_of((1 - low) * half + within, feat)

        @pl.when(same == 1)
        def _():
            out_ref[pl.ds(first, feat), :] = near[j][:feat, :]
            out_ref[pl.ds(second, feat), :] = near[j][feat:, :]

        @pl.when(same == 0)
        def _():
            out_ref[pl.ds(first, feat), :] = third[j][...]
            out_ref[pl.ds(second, feat), :] = fourth[j][...]


def assemble(place, near, third, fourth):
    feat, rows = third[0].shape
    vmem = pl.BlockSpec(memory_space=pltpu.VMEM)
    return pl.pallas_call(
        assemble_kernel,
        in_specs=[pl.BlockSpec(memory_space=pltpu.SMEM)] + [vmem] * (3 * CREW),
        out_specs=vmem,
        out_shape=jax.ShapeDtypeStruct((2 * CREW * feat, rows), BF16),
        name="assemble",
    )(place, *near, *third, *fourth)


def widen_taps(short_filter, chan_count):
    kinds, tap_count, groups = short_filter.shape
    return jnp.repeat(
        short_filter.astype(F32).reshape(kinds * tap_count, groups), chan_count // groups, axis=1
    )


def gather_rims(q_proj, k_proj, v_proj, lead):
    size = lax.axis_size("context")
    tails = jnp.concatenate([a[a.shape[0] - lead :] for a in (q_proj, k_proj, v_proj)], axis=0)
    rims = lax.ppermute(tails, "context", [(i, i + 1) for i in range(size - 1)])
    return jnp.pad(rims.astype(F32), ((0, -rims.shape[0] % SEGS), (0, 0)))


def per_device(q_proj, k_proj, v_proj, short_filter, residue, decay_rate, out_weight):
    rows, chan_count = q_proj.shape
    size = lax.axis_size("context")
    total = float(rows * size)
    place = lax.axis_index("context")
    rims = gather_rims(q_proj, k_proj, v_proj, short_filter.shape[1] - 1)
    taps = widen_taps(short_filter, chan_count)
    q_feat, y_local, carry, ends = local_pass(
        q_proj, k_proj, v_proj, rims, taps, decay_rate, residue, total
    )
    gathered = lax.all_gather(ends, "context")
    gaps = (place - 1 - jnp.arange(size))[:, None, None]
    reach = jnp.exp(-(decay_rate / total)[None] * (gaps * rows).astype(F32))
    incoming = jnp.sum(jnp.where(gaps >= 0, reach * gathered, 0.0), axis=0)
    gated = gate_pass(q_feat, y_local, carry, incoming, decay_rate, residue, total)
    partial_terms = lax.dot_general(
        lax.all_gather(out_weight, "context", axis=0, tiled=True),
        gated,
        (((1,), (1,)), ((), ())),
        preferred_element_type=F32,
    )
    return lax.psum_scatter(
        partial_terms.astype(BF16), "tensor", scatter_dimension=0, tiled=True
    )


def swap(block, mask):
    size = lax.axis_size("context")
    return lax.ppermute(block, "context", [(i, i ^ mask) for i in range(size)])


def shift(block, distance):
    size = lax.axis_size("context")
    moves = [(i, i + distance) for i in range(size) if 0 <= i + distance < size]
    return lax.ppermute(block, "context", moves)


def exchange_states(ends, steps, rows, place):
    chan_count = ends.shape[1]
    quarter = chan_count // CREW
    seat = place % CREW

    def part(array, owner):
        return lax.dynamic_slice_in_dim(array, owner * quarter, quarter, 1)

    own_steps = part(steps, seat)

    def reach(count):
        return jnp.exp(-own_steps * (rows * count).astype(F32))

    blocks = [part(ends, seat)] + [swap(part(ends, seat ^ j), j) for j in range(1, CREW)]
    plane = sum(reach(CREW - 1 - (seat ^ j)) * blocks[j] for j in range(CREW))
    before = jnp.zeros_like(plane)
    for hop in range(1, PLANES):
        arrived = shift(plane, hop * CREW)
        before = before + jnp.exp(-own_steps * float(rows * CREW * (hop - 1))) * arrived

    def for_seat(target):
        state = reach(target) * before
        for j in range(CREW):
            gap = target - 1 - (seat ^ j)
            state = state + jnp.where(gap >= 0, reach(jnp.maximum(gap, 0)) * blocks[j], 0.0)
        return state

    mine = [for_seat(seat)] + [swap(for_seat(seat ^ j), j) for j in range(1, CREW)]
    odd, high = seat % 2 == 1, seat >= 2
    ordered = [jnp.where(odd, mine[j ^ 1], mine[j]) for j in range(CREW)]
    ordered = [jnp.where(high, ordered[j ^ 2], ordered[j]) for j in range(CREW)]
    return jnp.concatenate(ordered, axis=1)


def per_device_planes(q_proj, k_proj, v_proj, short_filter, residue, decay_rate, out_weight):
    rows, chan_count = q_proj.shape
    size = lax.axis_size("context")
    total = float(rows * size)
    place = lax.axis_index("context")
    side = lax.axis_index("tensor")
    plane, seat = place // CREW, place % CREW
    low = plane % 2
    same = (side == plane // 2).astype(jnp.int32)

    up1, down1 = shift(out_weight, CREW), shift(out_weight, -CREW)
    rims = gather_rims(q_proj, k_proj, v_proj, short_filter.shape[1] - 1)
    taps = widen_taps(short_filter, chan_count)
    q_feat, y_local, carry, ends = local_pass(
        q_proj, k_proj, v_proj, rims, taps, decay_rate, residue, total
    )
    incoming = exchange_states(ends, decay_rate / total, rows, place)
    gated = gate_pass(q_feat, y_local, carry, incoming, decay_rate, residue, total)

    def hops(block, moves):
        return lax.ppermute(
            block, "context",
            [(a * CREW + s, b * CREW + s) for a, b in moves for s in range(CREW)],
        )

    up2 = hops(up1, [(1, 2), (2, 3)])
    down2 = hops(down1, [(2, 1), (1, 0)])
    up3 = hops(up2, [(2, 3)])
    down3 = hops(down2, [(1, 0)])

    tokens = [gated, swap(gated, 1), swap(gated, 2)]
    tokens.append(swap(tokens[2], 1))

    def cross(block, from_same):
        moves = []
        for p in range(PLANES):
            for s in range(CREW):
                keeper = p // 2 if not from_same else 1 - p // 2
                moves.append(((1 - keeper) * size + p * CREW + s, keeper * size + p * CREW + s))
        return lax.ppermute(block, ("tensor", "context"), moves)

    def deal(block, mask, to_same):
        moves = []
        for p in range(PLANES):
            keeper = p // 2 if to_same else 1 - p // 2
            for s in range(CREW):
                at = keeper * size + p * CREW
                moves.append((at + s, at + (s ^ mask)))
        return lax.ppermute(block, ("tensor", "context"), moves)

    def finish(partials, to_same):
        arrived = cross(partials, not to_same)
        summed = [
            (partials[j].astype(F32) + arrived[j].astype(F32)).astype(BF16) for j in range(CREW)
        ]
        return [summed[0]] + [deal(summed[j], j, to_same) for j in range(1, CREW)]

    edge = (plane == 0) | (plane == PLANES - 1)
    near = project([(out_weight, out_weight), (up1, down1)], [low * 0 + 1, low], tokens)
    near = finish(near, True)
    third = project([(up2, down2)], [plane >= 2], tokens)
    third = finish(third, False)
    middle = jnp.where(plane == 1, down1, up1)
    outer = jnp.where(plane == 0, down3, up3)
    fourth = project([(outer, middle)], [edge], tokens)
    fourth = finish(fourth, False)
    return assemble(jnp.stack([same, low, seat]).astype(jnp.int32), near, third, fourth)


def solution(mesh):
    planes = mesh.shape["tensor"] == 2 and mesh.shape["context"] == CREW * PLANES
    return jax.shard_map(
        per_device_planes if planes else per_device,
        mesh=mesh,
        in_specs=(
            P("context", "tensor"),
            P("context", "tensor"),
            P("context", "tensor"),
            P(None, None, "tensor"),
            P(None, "tensor"),
            P(None, "tensor"),
            P("context", "tensor"),
        ),
        out_specs=P("tensor", "context"),
        check_vma=False,
    )
```

```python
import functools

import jax
import jax.numpy as jnp
from jax import lax
from jax.experimental import pallas as pl
from jax.experimental.pallas import tpu as pltpu
from jax.sharding import PartitionSpec as P

LANES = 128
SEGS = 8
CREW = 4
LEAD = 2
PLANES = 4
VMEM_GRANT = 56 * 2**20
F32 = jnp.float32
BF16 = jnp.bfloat16


def lane_block(chan_count):
    return 512 if chan_count % 512 == 0 else LANES


def tree_sum(terms):
    terms = list(terms)
    while len(terms) > 1:
        paired = [terms[i] + terms[i + 1] for i in range(0, len(terms) - 1, 2)]
        if len(terms) % 2:
            paired.append(terms[-1])
        terms = paired
    return terms[0]


def spread(row):
    return jnp.broadcast_to(row, (SEGS, LANES))


def local_kernel(
    total, q_ref, k_ref, v_ref, rim_ref, filter_ref, decay_ref, residue_ref,
    qf_ref, y_ref, carry_ref, end_ref, shifted, signal,
):
    rows, width = q_ref.shape
    modes = decay_ref.shape[0]
    length = rows // SEGS
    kinds, tap_count, groups = filter_ref.shape
    group_width = pl.num_programs(0) * width // groups
    chan = pl.program_id(0) * width + lax.broadcasted_iota(jnp.int32, (groups, width), 1)
    first = lax.broadcasted_iota(jnp.int32, (groups, width), 0) * group_width
    member = ((chan >= first) & (chan < first + group_width)).astype(BF16)
    taps = [
        jnp.dot(filter_ref[kind], member, preferred_element_type=F32) for kind in range(kinds)
    ]
    lead = LEAD

    def short_pass(which, ref, lanes):
        pad = shifted.at[which]
        pad[SEGS : SEGS + rows, :] = ref[:, lanes].astype(F32)
        pad[SEGS - lead : SEGS, :] = rim_ref[which * lead : (which + 1) * lead, lanes]
        running = None
        for offset in range(tap_count):
            tap = taps[which][offset : offset + 1, lanes]
            term = tap * pad[SEGS - offset : SEGS - offset + rows, :]
            running = term if running is None else running + term
        return running.astype(BF16)

    for block in range(width // LANES):
        lanes = slice(block * LANES, (block + 1) * LANES)
        qf_ref[:, lanes] = short_pass(0, q_ref, lanes)
        k_feat = short_pass(1, k_ref, lanes).astype(F32)
        v_feat = short_pass(2, v_ref, lanes).astype(F32)
        signal[block] = (k_feat * v_feat).astype(BF16).astype(F32)

    seg = lax.broadcasted_iota(jnp.int32, (SEGS, LANES), 0)
    for block in range(width // LANES):
        lanes = slice(block * LANES, (block + 1) * LANES)
        steps = decay_ref[:, lanes] / total
        decays = jnp.exp(-steps)
        scales = residue_ref[:, lanes] * jnp.sqrt(2.0 * steps)
        decay = [spread(decays[m : m + 1]) for m in range(modes)]
        scale = [spread(scales[m : m + 1]) for m in range(modes)]

        def advance(i, state):
            x = signal[block, pl.ds(i, SEGS, stride=length), :]
            state = tuple(d * s + x for d, s in zip(decay, state))
            y_ref[i, :, lanes] = tree_sum(c * s for c, s in zip(scale, state))
            return state

        zero = jnp.zeros((SEGS, LANES), F32)
        state = lax.fori_loop(0, length, advance, (zero,) * modes, unroll=4)
        for m in range(modes):
            ends = state[m]
            for hop in (1, 2, 4):
                factor = spread(jnp.exp(-steps[m : m + 1] * float(length * hop)))
                ends = ends + factor * jnp.where(seg >= hop, pltpu.roll(ends, hop, 0), 0.0)
            end_ref[m : m + 1, lanes] = ends[SEGS - 1 : SEGS]
            carry_ref[m, :, lanes] = jnp.where(seg >= 1, pltpu.roll(ends, 1, 0), 0.0)


def gate_kernel(
    total, qf_ref, y_ref, carry_ref, incoming_ref, decay_ref, residue_ref, out_ref, mixed
):
    rows, width = qf_ref.shape
    modes = decay_ref.shape[0]
    length = rows // SEGS
    begin = (lax.broadcasted_iota(jnp.int32, (SEGS, LANES), 0) * length).astype(F32)
    for block in range(width // LANES):
        lanes = slice(block * LANES, (block + 1) * LANES)
        steps = decay_ref[:, lanes] / total
        decays = jnp.exp(-steps)
        weights = residue_ref[:, lanes] * jnp.sqrt(2.0 * steps) * decays
        decay = [spread(decays[m : m + 1]) for m in range(modes)]
        tail = []
        for m in range(modes):
            reach = jnp.exp(-spread(steps[m : m + 1]) * begin)
            held = carry_ref[m, :, lanes] + reach * spread(incoming_ref[m : m + 1, lanes])
            tail.append(spread(weights[m : m + 1]) * held)

        def advance(i, tail):
            mixed[block, pl.ds(i, SEGS, stride=length), :] = y_ref[i, :, lanes] + tree_sum(tail)
            return tuple(d * s for d, s in zip(decay, tail))

        lax.fori_loop(0, length, advance, tuple(tail), unroll=4)
    for block in range(width // LANES):
        lanes = slice(block * LANES, (block + 1) * LANES)
        gated = qf_ref[:, lanes].astype(F32) * mixed[block]
        out_ref[lanes, :] = jnp.transpose(gated).astype(BF16)


def local_pass(q_proj, k_proj, v_proj, rims, short_filter, decay_rate, residue, total):
    rows, chan_count = q_proj.shape
    modes = decay_rate.shape[0]
    width = lane_block(chan_count)
    length = rows // SEGS

    def cols(height):
        return pl.BlockSpec((height, width), lambda c: (0, c))

    return pl.pallas_call(
        functools.partial(local_kernel, total),
        grid=(chan_count // width,),
        in_specs=[
            cols(rows), cols(rows), cols(rows), cols(rims.shape[0]),
            pl.BlockSpec(short_filter.shape, lambda c: (0, 0, 0)),
            cols(modes), cols(modes),
        ],
        out_specs=[
            cols(rows),
            pl.BlockSpec((length, SEGS, width), lambda c: (0, 0, c)),
            pl.BlockSpec((modes, SEGS, width), lambda c: (0, 0, c)),
            cols(modes),
        ],
        out_shape=[
            jax.ShapeDtypeStruct((rows, chan_count), BF16),
            jax.ShapeDtypeStruct((length, SEGS, chan_count), F32),
            jax.ShapeDtypeStruct((modes, SEGS, chan_count), F32),
            jax.ShapeDtypeStruct((modes, chan_count), F32),
        ],
        scratch_shapes=[
            pltpu.VMEM((3, rows + SEGS, LANES), F32),
            pltpu.VMEM((width // LANES, rows, LANES), F32),
        ],
        compiler_params=pltpu.CompilerParams(vmem_limit_bytes=VMEM_GRANT),
        name="local_pass",
    )(q_proj, k_proj, v_proj, rims, short_filter, decay_rate, residue)


def gate_pass(q_feat, y_local, carry, incoming, decay_rate, residue, total):
    rows, chan_count = q_feat.shape
    modes = decay_rate.shape[0]
    width = lane_block(chan_count)
    length = rows // SEGS

    def cols(height):
        return pl.BlockSpec((height, width), lambda c: (0, c))

    return pl.pallas_call(
        functools.partial(gate_kernel, total),
        grid=(chan_count // width,),
        in_specs=[
            cols(rows),
            pl.BlockSpec((length, SEGS, width), lambda c: (0, 0, c)),
            pl.BlockSpec((modes, SEGS, width), lambda c: (0, 0, c)),
            cols(modes), cols(modes), cols(modes),
        ],
        out_specs=pl.BlockSpec((width, rows), lambda c: (c, 0)),
        out_shape=jax.ShapeDtypeStruct((chan_count, rows), BF16),
        scratch_shapes=[pltpu.VMEM((width // LANES, rows, LANES), F32)],
        compiler_params=pltpu.CompilerParams(vmem_limit_bytes=VMEM_GRANT),
        name="gate_pass",
    )(q_feat, y_local, carry, incoming, decay_rate, residue)


def product_kernel(weight_count, weight_refs, token_refs, out_ref, total):
    step = pl.program_id(0)

    @pl.when(step == 0)
    def _():
        total[...] = jnp.zeros_like(total)

    for j, tokens in enumerate(token_refs):
        begin = 0
        for s in range(weight_count):
            end = begin + weight_refs[s].shape[0]
            total[j, begin:end, :] += jnp.dot(
                weight_refs[s][...], tokens[...], preferred_element_type=F32
            )
            begin = end

    @pl.when(step == pl.num_programs(0) - 1)
    def _():
        out_ref[...] = total[...].astype(BF16)


def plain_product(weight_count, *refs):
    tokens = refs[weight_count : weight_count + CREW]
    product_kernel(weight_count, refs[:weight_count], tokens, *refs[weight_count + CREW :])


def picked_product(pick_ref, one_ref, other_ref, *refs):
    for first, source in ((1, one_ref), (0, other_ref)):

        @pl.when(pick_ref[0] == first)
        def _():
            product_kernel(1, [source], refs[:CREW], *refs[CREW:])


def project(weights, tokens, pick=None):
    depth, rows = tokens[0].shape
    width = 1024 if depth % 1024 == 0 else LANES
    out_rows = sum(w.shape[0] for w in weights) if pick is None else weights[0].shape[0]
    prefetch = [] if pick is None else [pick.astype(jnp.int32).reshape(1)]
    body = functools.partial(plain_product, len(weights)) if pick is None else picked_product
    return pl.pallas_call(
        body,
        grid_spec=pltpu.PrefetchScalarGridSpec(
            num_scalar_prefetch=len(prefetch),
            grid=(depth // width,),
            in_specs=[pl.BlockSpec((w.shape[0], width), lambda c, *_: (0, c)) for w in weights]
            + [pl.BlockSpec((width, rows), lambda c, *_: (c, 0)) for _ in tokens],
            out_specs=pl.BlockSpec((CREW, out_rows, rows), lambda c, *_: (0, 0, 0)),
            scratch_shapes=[pltpu.VMEM((CREW, out_rows, rows), F32)],
        ),
        out_shape=jax.ShapeDtypeStruct((CREW, out_rows, rows), BF16),
        compiler_params=pltpu.CompilerParams(vmem_limit_bytes=VMEM_GRANT),
        name="project",
    )(*prefetch, *weights, *tokens)


def assemble_kernel(place_ref, *refs):
    near, third, fourth = (refs[i * CREW : (i + 1) * CREW] for i in range(3))
    last, out_ref = refs[3 * CREW : 4 * CREW], refs[-1]
    feat, part = third[0].shape[0], fourth[0].shape[0]
    half = out_ref.shape[0] // 2
    same, low, seat = place_ref[0], place_ref[1], place_ref[2]
    for j in range(CREW):
        within = (seat ^ j) * feat
        first = pl.multiple_of(low * half + within, feat)
        second = pl.multiple_of((1 - low) * half + within, feat)
        split = pl.multiple_of(second + part, part)

        @pl.when(same == 1)
        def _():
            out_ref[pl.ds(first, feat), :] = near[j][:feat, :]
            out_ref[pl.ds(second, feat), :] = near[j][feat:, :]

        @pl.when(same == 0)
        def _():
            out_ref[pl.ds(first, feat), :] = third[j][...]
            out_ref[pl.ds(second, part), :] = fourth[j][...]
            out_ref[pl.ds(split, feat - part), :] = last[j][...]


def assemble(place, near, third, fourth, last):
    feat, rows = third[0].shape
    vmem = pl.BlockSpec(memory_space=pltpu.VMEM)
    return pl.pallas_call(
        assemble_kernel,
        in_specs=[pl.BlockSpec(memory_space=pltpu.SMEM)] + [vmem] * (4 * CREW),
        out_specs=vmem,
        out_shape=jax.ShapeDtypeStruct((2 * CREW * feat, rows), BF16),
        compiler_params=pltpu.CompilerParams(vmem_limit_bytes=VMEM_GRANT),
        name="assemble",
    )(place, *near, *third, *fourth, *last)


def tails_kernel(q_ref, k_ref, v_ref, out_ref):
    lead = LEAD
    for which, ref in enumerate((q_ref, k_ref, v_ref)):
        rows = ref[...].astype(F32)
        out_ref[which * lead : (which + 1) * lead, :] = rows[rows.shape[0] - lead :]
    out_ref[3 * lead :, :] = jnp.zeros((out_ref.shape[0] - 3 * lead, out_ref.shape[1]), F32)


def gather_rims(q_proj, k_proj, v_proj):
    size = lax.axis_size("context")
    rows, chan_count = q_proj.shape
    last = pl.BlockSpec((16, chan_count), lambda i: (rows // 16 - 1, 0))
    tails = pl.pallas_call(
        tails_kernel,
        grid=(1,),
        in_specs=[last] * 3,
        out_specs=pl.BlockSpec((SEGS, chan_count), lambda i: (0, 0)),
        out_shape=jax.ShapeDtypeStruct((SEGS, chan_count), F32),
        compiler_params=pltpu.CompilerParams(vmem_limit_bytes=VMEM_GRANT),
        name="tails",
    )(q_proj, k_proj, v_proj)
    return lax.ppermute(tails, "context", [(i, i + 1) for i in range(size - 1)])


def per_device(q_proj, k_proj, v_proj, short_filter, residue, decay_rate, out_weight):
    rows, chan_count = q_proj.shape
    size = lax.axis_size("context")
    total = float(rows * size)
    place = lax.axis_index("context")
    rims = gather_rims(q_proj, k_proj, v_proj)
    q_feat, y_local, carry, ends = local_pass(
        q_proj, k_proj, v_proj, rims, short_filter, decay_rate, residue, total
    )
    gathered = lax.all_gather(ends, "context")
    gaps = (place - 1 - jnp.arange(size))[:, None, None]
    reach = jnp.exp(-(decay_rate / total)[None] * (gaps * rows).astype(F32))
    incoming = jnp.sum(jnp.where(gaps >= 0, reach * gathered, 0.0), axis=0)
    gated = gate_pass(q_feat, y_local, carry, incoming, decay_rate, residue, total)
    partial_terms = lax.dot_general(
        lax.all_gather(out_weight, "context", axis=0, tiled=True),
        gated,
        (((1,), (0,)), ((), ())),
        preferred_element_type=F32,
    )
    return lax.psum_scatter(
        partial_terms.astype(BF16), "tensor", scatter_dimension=0, tiled=True
    )


def swap(block, mask):
    size = lax.axis_size("context")
    return lax.ppermute(block, "context", [(i, i ^ mask) for i in range(size)])


def shift(block, distance):
    size = lax.axis_size("context")
    moves = [(i, i + distance) for i in range(size) if 0 <= i + distance < size]
    return lax.ppermute(block, "context", moves)


def exchange_states(ends, steps, rows, place):
    chan_count = ends.shape[1]
    quarter = chan_count // CREW
    seat = place % CREW

    def part(array, owner):
        return lax.dynamic_slice_in_dim(array, owner * quarter, quarter, 1)

    own_steps = part(steps, seat)

    def reach(count):
        return jnp.exp(-own_steps * (rows * count).astype(F32))

    blocks = [part(ends, seat)] + [swap(part(ends, seat ^ j), j) for j in range(1, CREW)]
    plane = sum(reach(CREW - 1 - (seat ^ j)) * blocks[j] for j in range(CREW))
    before = jnp.zeros_like(plane)
    for hop in range(1, PLANES):
        arrived = shift(plane, hop * CREW)
        before = before + jnp.exp(-own_steps * float(rows * CREW * (hop - 1))) * arrived

    def for_seat(target):
        state = reach(target) * before
        for j in range(CREW):
            gap = target - 1 - (seat ^ j)
            state = state + jnp.where(gap >= 0, reach(jnp.maximum(gap, 0)) * blocks[j], 0.0)
        return state

    mine = [for_seat(seat)] + [swap(for_seat(seat ^ j), j) for j in range(1, CREW)]
    odd, high = seat % 2 == 1, seat >= 2
    ordered = [jnp.where(odd, mine[j ^ 1], mine[j]) for j in range(CREW)]
    ordered = [jnp.where(high, ordered[j ^ 2], ordered[j]) for j in range(CREW)]
    return jnp.concatenate(ordered, axis=1)


def per_device_planes(q_proj, k_proj, v_proj, short_filter, residue, decay_rate, out_weight):
    rows, chan_count = q_proj.shape
    size = lax.axis_size("context")
    total = float(rows * size)
    place = lax.axis_index("context")
    side = lax.axis_index("tensor")
    plane, seat = place // CREW, place % CREW
    low = plane % 2
    same = (side == plane // 2).astype(jnp.int32)

    up1, down1 = shift(out_weight, CREW), shift(out_weight, -CREW)
    rims = gather_rims(q_proj, k_proj, v_proj)
    q_feat, y_local, carry, ends = local_pass(
        q_proj, k_proj, v_proj, rims, short_filter, decay_rate, residue, total
    )
    incoming = exchange_states(ends, decay_rate / total, rows, place)
    incoming, up1, down1 = lax.optimization_barrier((incoming, up1, down1))

    def hops(block, moves):
        return lax.ppermute(
            block, "context",
            [(a * CREW + s, b * CREW + s) for a, b in moves for s in range(CREW)],
        )

    up2 = hops(up1, [(1, 2), (2, 3)])
    down2 = hops(down1, [(2, 1), (1, 0)])
    gated = gate_pass(q_feat, y_local, carry, incoming, decay_rate, residue, total)
    half = out_weight.shape[0] // 2
    parts = [slice(0, half), slice(half, None)]
    outer = [hops(up2[p], [(2, 3)]) + hops(down2[p], [(1, 0)]) for p in parts]

    tokens = [gated, swap(gated, 1), swap(gated, 2)]
    tokens.append(swap(tokens[2], 1))

    def cross(block, from_same):
        moves = []
        for p in range(PLANES):
            for s in range(CREW):
                keeper = p // 2 if not from_same else 1 - p // 2
                moves.append(((1 - keeper) * size + p * CREW + s, keeper * size + p * CREW + s))
        return lax.ppermute(block, ("tensor", "context"), moves)

    def deal(block, mask, to_same):
        moves = []
        for p in range(PLANES):
            keeper = p // 2 if to_same else 1 - p // 2
            for s in range(CREW):
                at = keeper * size + p * CREW
                moves.append((at + s, at + (s ^ mask)))
        return lax.ppermute(block, ("tensor", "context"), moves)

    def finish(partials, to_same):
        arrived = cross(partials, not to_same)
        summed = [
            (partials[j].astype(F32) + arrived[j].astype(F32)).astype(BF16) for j in range(CREW)
        ]
        return [summed[0]] + [deal(summed[j], j, to_same) for j in range(1, CREW)]

    edge = (plane == 0) | (plane == PLANES - 1)
    beside = project([up1, down1], tokens, low)
    near = finish(jnp.concatenate([project([out_weight], tokens), beside], axis=1), True)
    third = finish(project([up2, down2], tokens, plane >= 2), False)
    inner = jnp.where(plane == 1, down1, up1)
    fourth = finish(project([outer[0], inner[:half]], tokens, edge), False)
    last = finish(project([outer[1], inner[half:]], tokens, edge), False)
    return assemble(jnp.stack([same, low, seat]).astype(jnp.int32), near, third, fourth, last)


def solution(mesh):
    planes = mesh.shape["tensor"] == 2 and mesh.shape["context"] == CREW * PLANES
    return jax.shard_map(
        per_device_planes if planes else per_device,
        mesh=mesh,
        in_specs=(
            P("context", "tensor"),
            P("context", "tensor"),
            P("context", "tensor"),
            P(None, None, "tensor"),
            P(None, "tensor"),
            P(None, "tensor"),
            P("context", "tensor"),
        ),
        out_specs=P("tensor", "context"),
        check_vma=False,
    )
```

```python
import functools

import jax
import jax.numpy as jnp
from jax import lax
from jax.experimental import pallas as pl
from jax.experimental.pallas import tpu as pltpu
from jax.sharding import PartitionSpec as P

LANES = 128
SEGS = 8
CREW = 4
LEAD = 2
PLANES = 4
NEAR = (0, 1)
ACROSS_Y = 2
FAR = (4, 5)
VMEM_GRANT = 56 * 2**20
F32 = jnp.float32
BF16 = jnp.bfloat16


def lane_block(chan_count):
    return 512 if chan_count % 512 == 0 else LANES


def tree_sum(terms):
    terms = list(terms)
    while len(terms) > 1:
        paired = [terms[i] + terms[i + 1] for i in range(0, len(terms) - 1, 2)]
        if len(terms) % 2:
            paired.append(terms[-1])
        terms = paired
    return terms[0]


def spread(row):
    return jnp.broadcast_to(row, (SEGS, LANES))


def rounded(value):
    return value.astype(BF16).astype(F32)


def strided(ref, block, begin, length):
    return ref[block, pl.ds(begin, SEGS, stride=length), :]


def group_taps(filter_ref, kind, width):
    groups = filter_ref.shape[2]
    group_width = pl.num_programs(0) * width // groups
    chan = pl.program_id(0) * width + lax.broadcasted_iota(jnp.int32, (groups, width), 1)
    first = lax.broadcasted_iota(jnp.int32, (groups, width), 0) * group_width
    member = ((chan >= first) & (chan < first + group_width)).astype(BF16)
    return jnp.dot(filter_ref[kind], member, preferred_element_type=F32)


def lead_values(ref, block, length, rim_ref, kind, lanes):
    seg = lax.broadcasted_iota(jnp.int32, (SEGS, LANES), 0)
    values = []
    for back in range(1, LEAD + 1):
        ends = pltpu.roll(strided(ref, block, length - back, length), 1, 0)
        row = kind * LEAD + LEAD - back
        values.append(jnp.where(seg == 0, spread(rim_ref[row : row + 1, lanes]), ends))
    return values


def filtered(taps, now, earlier):
    running = taps[0] * now
    for tap, value in zip(taps[1:], earlier):
        running = running + tap * value
    return rounded(running)


def ends_kernel(
    total, k_ref, v_ref, rim_ref, filter_ref, decay_ref,
    signal_ref, carry_ref, end_ref, k_wide, v_wide,
):
    rows, width = k_ref.shape
    modes = decay_ref.shape[0]
    length = rows // SEGS
    tap_count = filter_ref.shape[1]
    k_taps = group_taps(filter_ref, 1, width)
    v_taps = group_taps(filter_ref, 2, width)
    seg = lax.broadcasted_iota(jnp.int32, (SEGS, LANES), 0)
    for block in range(width // LANES):
        lanes = slice(block * LANES, (block + 1) * LANES)
        k_wide[block] = k_ref[:, lanes].astype(F32)
        v_wide[block] = v_ref[:, lanes].astype(F32)
    for block in range(width // LANES):
        lanes = slice(block * LANES, (block + 1) * LANES)
        steps = decay_ref[:, lanes] / total
        decays = jnp.exp(-steps)
        decay = [spread(decays[m : m + 1]) for m in range(modes)]
        k_tap = [spread(k_taps[o : o + 1, lanes]) for o in range(tap_count)]
        v_tap = [spread(v_taps[o : o + 1, lanes]) for o in range(tap_count)]

        def advance(i, held):
            k_back, v_back, state = held
            k_now = strided(k_wide, block, i, length)
            v_now = strided(v_wide, block, i, length)
            x = rounded(filtered(k_tap, k_now, k_back) * filtered(v_tap, v_now, v_back))
            signal_ref[i, :, lanes] = x
            state = tuple(d * s + x for d, s in zip(decay, state))
            return (k_now,) + k_back[:-1], (v_now,) + v_back[:-1], state

        zero = jnp.zeros((SEGS, LANES), F32)
        held = (
            tuple(lead_values(k_wide, block, length, rim_ref, 1, lanes)),
            tuple(lead_values(v_wide, block, length, rim_ref, 2, lanes)),
            (zero,) * modes,
        )
        state = lax.fori_loop(0, length, advance, held, unroll=4)[2]
        for m in range(modes):
            ends = state[m]
            for hop in (1, 2, 4):
                factor = spread(jnp.exp(-steps[m : m + 1] * float(length * hop)))
                ends = ends + factor * jnp.where(seg >= hop, pltpu.roll(ends, hop, 0), 0.0)
            end_ref[m : m + 1, lanes] = ends[SEGS - 1 : SEGS]
            carry_ref[m, :, lanes] = jnp.where(seg >= 1, pltpu.roll(ends, 1, 0), 0.0)


def local_kernel(
    total, q_ref, rim_ref, filter_ref, decay_ref, residue_ref, signal_ref, qf_ref, y_ref, q_wide
):
    rows, width = q_ref.shape
    modes = decay_ref.shape[0]
    length = rows // SEGS
    q_taps = group_taps(filter_ref, 0, width)
    for block in range(width // LANES):
        q_wide[block] = q_ref[:, block * LANES : (block + 1) * LANES].astype(F32)
    for block in range(width // LANES):
        lanes = slice(block * LANES, (block + 1) * LANES)
        steps = decay_ref[:, lanes] / total
        decays = jnp.exp(-steps)
        scales = residue_ref[:, lanes] * jnp.sqrt(2.0 * steps)
        decay = [spread(decays[m : m + 1]) for m in range(modes)]
        scale = [spread(scales[m : m + 1]) for m in range(modes)]
        q_tap = [spread(q_taps[o : o + 1, lanes]) for o in range(filter_ref.shape[1])]

        def advance(i, held):
            q_back, state = held
            q_now = strided(q_wide, block, i, length)
            qf_ref[i, :, lanes] = filtered(q_tap, q_now, q_back)
            x = signal_ref[i, :, lanes]
            state = tuple(d * s + x for d, s in zip(decay, state))
            y_ref[i, :, lanes] = tree_sum(c * s for c, s in zip(scale, state))
            return (q_now,) + q_back[:-1], state

        zero = jnp.zeros((SEGS, LANES), F32)
        held = (
            tuple(lead_values(q_wide, block, length, rim_ref, 0, lanes)),
            (zero,) * modes,
        )
        lax.fori_loop(0, length, advance, held, unroll=4)


def gate_kernel(
    total, qf_ref, y_ref, carry_ref, incoming_ref, decay_ref, residue_ref, out_ref, gated
):
    length, _, width = qf_ref.shape
    modes = decay_ref.shape[0]
    begin = (lax.broadcasted_iota(jnp.int32, (SEGS, LANES), 0) * length).astype(F32)
    for block in range(width // LANES):
        lanes = slice(block * LANES, (block + 1) * LANES)
        steps = decay_ref[:, lanes] / total
        decays = jnp.exp(-steps)
        weights = residue_ref[:, lanes] * jnp.sqrt(2.0 * steps) * decays
        decay = [spread(decays[m : m + 1]) for m in range(modes)]
        tail = []
        for m in range(modes):
            reach = jnp.exp(-spread(steps[m : m + 1]) * begin)
            held = carry_ref[m, :, lanes] + reach * spread(incoming_ref[m : m + 1, lanes])
            tail.append(spread(weights[m : m + 1]) * held)

        def advance(i, tail):
            mixed = y_ref[i, :, lanes] + tree_sum(tail)
            gated[block, pl.ds(i, SEGS, stride=length), :] = qf_ref[i, :, lanes] * mixed
            return tuple(d * s for d, s in zip(decay, tail))

        lax.fori_loop(0, length, advance, tuple(tail), unroll=4)
    for block in range(width // LANES):
        out_ref[:, block * LANES : (block + 1) * LANES] = gated[block].astype(BF16)


def column_call(body, name, arrays, outs, scratch, width, chan_count):
    def spec(shape):
        if shape[-1] != chan_count:
            return pl.BlockSpec(shape, lambda c: (0,) * len(shape))
        return pl.BlockSpec(shape[:-1] + (width,), lambda c: (0,) * (len(shape) - 1) + (c,))

    return pl.pallas_call(
        body,
        grid=(chan_count // width,),
        in_specs=[spec(a.shape) for a in arrays],
        out_specs=[spec(o.shape) for o in outs],
        out_shape=outs,
        scratch_shapes=scratch,
        compiler_params=pltpu.CompilerParams(vmem_limit_bytes=VMEM_GRANT),
        name=name,
    )(*arrays)


def gated_rows(exchange, q_proj, k_proj, v_proj, short_filter, residue, decay_rate):
    rows, chan_count = q_proj.shape
    modes = decay_rate.shape[0]
    total = float(rows * lax.axis_size("context"))
    width = lane_block(chan_count)
    length = rows // SEGS
    wide = pltpu.VMEM((width // LANES, rows, LANES), F32)
    stepped = jax.ShapeDtypeStruct((length, SEGS, chan_count), F32)
    rims = gather_rims(q_proj, k_proj, v_proj)
    signal, carry, ends = column_call(
        functools.partial(ends_kernel, total), "ends_pass",
        (k_proj, v_proj, rims, short_filter, decay_rate),
        [
            stepped,
            jax.ShapeDtypeStruct((modes, SEGS, chan_count), F32),
            jax.ShapeDtypeStruct((modes, chan_count), F32),
        ],
        [wide, wide], width, chan_count,
    )
    q_feat, y_local = column_call(
        functools.partial(local_kernel, total), "local_pass",
        (q_proj, rims, short_filter, decay_rate, residue, signal),
        [stepped, stepped], [wide], width, chan_count,
    )
    incoming = exchange(ends, decay_rate / total, rows)
    return column_call(
        functools.partial(gate_kernel, total), "gate_pass",
        (q_feat, y_local, carry, incoming, decay_rate, residue),
        [jax.ShapeDtypeStruct((rows, chan_count), BF16)], [wide], width, chan_count,
    )[0]


def product_kernel(weight_count, token_count, same_ref, *refs):
    weights, tokens = refs[:weight_count], refs[weight_count : weight_count + token_count]
    outs, total = refs[weight_count + token_count : -1], refs[-1]
    step = pl.program_id(0)

    @pl.when(step == 0)
    def _():
        total[...] = jnp.zeros_like(total)

    for j, token in enumerate(tokens):
        begin = 0
        for weight in weights:
            end = begin + weight.shape[0]
            total[j, begin:end, :] += lax.dot_general(
                weight[...], token[...], (((1,), (1,)), ((), ())), preferred_element_type=F32
            )
            begin = end

    @pl.when(step == pl.num_programs(0) - 1)
    def _():
        if len(outs) == 1:
            outs[0][...] = total[...].astype(BF16)
        else:
            middle = total.shape[1] // 2
            for same in (1, 0):

                @pl.when(same_ref[0] == same)
                def _():
                    outs[1 - same][...] = total[:, :middle, :].astype(BF16)
                    outs[same][...] = total[:, middle:, :].astype(BF16)


def project(weights, tokens, same, split=False):
    rows, depth = tokens[0].shape
    width = 1024 if depth % 1024 == 0 else LANES
    feat = sum(w.shape[0] for w in weights)
    out_feat = feat // 2 if split else feat
    shape = (len(tokens), out_feat, rows)
    out_count = 2 if split else 1
    return pl.pallas_call(
        functools.partial(product_kernel, len(weights), len(tokens)),
        grid_spec=pltpu.PrefetchScalarGridSpec(
            num_scalar_prefetch=1,
            grid=(depth // width,),
            in_specs=[
                pl.BlockSpec((a.shape[0], width), lambda c, _: (0, c)) for a in weights + tokens
            ],
            out_specs=[pl.BlockSpec(shape, lambda c, _: (0, 0, 0))] * out_count,
            scratch_shapes=[pltpu.VMEM((len(tokens), feat, rows), F32)],
        ),
        out_shape=[jax.ShapeDtypeStruct(shape, BF16)] * out_count,
        compiler_params=pltpu.CompilerParams(vmem_limit_bytes=VMEM_GRANT),
        name="project",
    )(same.reshape(1), *weights, *tokens)


def assemble_kernel(place_ref, *refs):
    feat = refs[0].shape[0] // 2
    same, seat = place_ref[0], place_ref[1]
    out_ref = refs[-1]

    def put(block, member, value):
        at = pl.multiple_of((seat ^ member ^ block) * feat, feat)
        out_ref[pl.ds(at, feat), :] = value

    for at, member in enumerate(FAR):
        for half, block in enumerate((0, ACROSS_Y)):
            put(block, member, refs[at][half * feat : (half + 1) * feat, :])
    for at, member in enumerate(NEAR):
        near, third, fourth = refs[2 + at], refs[4 + at], refs[6 + at]

        @pl.when(same == 1)
        def _():
            put(0, member, near[:feat, :])
            put(ACROSS_Y, member, near[feat:, :])

        @pl.when(same == 0)
        def _():
            put(0, member, third[...])
            put(ACROSS_Y, member, fourth[...])


def assemble(place, far, near, third, fourth):
    rows = far[0].shape[1]
    vmem = pl.BlockSpec(memory_space=pltpu.VMEM)
    return pl.pallas_call(
        assemble_kernel,
        in_specs=[pl.BlockSpec(memory_space=pltpu.SMEM)] + [vmem] * 8,
        out_specs=vmem,
        out_shape=jax.ShapeDtypeStruct((4 * far[0].shape[0], rows), BF16),
        compiler_params=pltpu.CompilerParams(vmem_limit_bytes=VMEM_GRANT),
        name="assemble",
    )(place, *far, *near, *third, *fourth)


def tails_kernel(q_ref, k_ref, v_ref, out_ref):
    lead = LEAD
    for which, ref in enumerate((q_ref, k_ref, v_ref)):
        rows = ref[...].astype(F32)
        out_ref[which * lead : (which + 1) * lead, :] = rows[rows.shape[0] - lead :]
    out_ref[3 * lead :, :] = jnp.zeros((out_ref.shape[0] - 3 * lead, out_ref.shape[1]), F32)


def gather_rims(q_proj, k_proj, v_proj):
    size = lax.axis_size("context")
    rows, chan_count = q_proj.shape
    last = pl.BlockSpec((16, chan_count), lambda i: (rows // 16 - 1, 0))
    tails = pl.pallas_call(
        tails_kernel,
        grid=(1,),
        in_specs=[last] * 3,
        out_specs=pl.BlockSpec((SEGS, chan_count), lambda i: (0, 0)),
        out_shape=jax.ShapeDtypeStruct((SEGS, chan_count), F32),
        compiler_params=pltpu.CompilerParams(vmem_limit_bytes=VMEM_GRANT),
        name="tails",
    )(q_proj, k_proj, v_proj)
    return lax.ppermute(tails, "context", [(i, i + 1) for i in range(size - 1)])


def per_device(q_proj, k_proj, v_proj, short_filter, residue, decay_rate, out_weight):
    place, size = lax.axis_index("context"), lax.axis_size("context")

    def exchange(ends, steps, rows):
        gathered = lax.all_gather(ends, "context")
        gaps = (place - 1 - jnp.arange(size))[:, None, None]
        reach = jnp.exp(-steps[None] * (gaps * rows).astype(F32))
        return jnp.sum(jnp.where(gaps >= 0, reach * gathered, 0.0), axis=0)

    gated = gated_rows(exchange, q_proj, k_proj, v_proj, short_filter, residue, decay_rate)
    partial_terms = lax.dot_general(
        lax.all_gather(out_weight, "context", axis=0, tiled=True),
        gated,
        (((1,), (1,)), ((), ())),
        preferred_element_type=F32,
    )
    return lax.psum_scatter(
        partial_terms.astype(BF16), "tensor", scatter_dimension=0, tiled=True
    )


def swap(block, mask):
    size = lax.axis_size("context")
    return lax.ppermute(block, "context", [(i, i ^ mask) for i in range(size)])


def shift(block, distance):
    size = lax.axis_size("context")
    moves = [(i, i + distance) for i in range(size) if 0 <= i + distance < size]
    return lax.ppermute(block, "context", moves)


def exchange_states(ends, steps, rows, place):
    chan_count = ends.shape[1]
    quarter = chan_count // CREW
    seat = place % CREW

    def part(array, owner):
        return lax.dynamic_slice_in_dim(array, owner * quarter, quarter, 1)

    own_steps = part(steps, seat)

    def reach(count):
        return jnp.exp(-own_steps * (rows * count).astype(F32))

    blocks = [part(ends, seat)] + [swap(part(ends, seat ^ j), j) for j in range(1, CREW)]
    plane = sum(reach(CREW - 1 - (seat ^ j)) * blocks[j] for j in range(CREW))
    before = jnp.zeros_like(plane)
    for hop in range(1, PLANES):
        arrived = shift(plane, hop * CREW)
        before = before + jnp.exp(-own_steps * float(rows * CREW * (hop - 1))) * arrived

    def for_seat(target):
        state = reach(target) * before
        for j in range(CREW):
            gap = target - 1 - (seat ^ j)
            state = state + jnp.where(gap >= 0, reach(jnp.maximum(gap, 0)) * blocks[j], 0.0)
        return state

    mine = [for_seat(seat)] + [swap(for_seat(seat ^ j), j) for j in range(1, CREW)]
    odd, high = seat % 2 == 1, seat >= 2
    ordered = [jnp.where(odd, mine[j ^ 1], mine[j]) for j in range(CREW)]
    ordered = [jnp.where(high, ordered[j ^ 2], ordered[j]) for j in range(CREW)]
    return jnp.concatenate(ordered, axis=1)


def per_device_planes(q_proj, k_proj, v_proj, short_filter, residue, decay_rate, out_weight):
    size = lax.axis_size("context")
    place, side = lax.axis_index("context"), lax.axis_index("tensor")
    top = 2 * FAR[0]
    same = (side == place // top).astype(jnp.int32)

    def exchange(ends, steps, rows):
        return exchange_states(ends, steps, rows, place)

    half = out_weight.shape[0] * 5 // 8
    parts = [out_weight[:half], out_weight[half:]]
    third = [swap(part, top) for part in parts]
    beside = swap(out_weight, ACROSS_Y)
    gated = lax.cond(
        place < size,
        lambda *arrays: gated_rows(exchange, *arrays),
        lambda *arrays: jnp.zeros_like(arrays[0]),
        q_proj, k_proj, v_proj, short_filter, residue, decay_rate,
    )
    def over_tensor(block, to_same):
        moves = []
        for i in range(size):
            keeper = i // top if to_same else 1 - i // top
            moves.append(((1 - keeper) * size + i, keeper * size + i))
        return lax.ppermute(block, ("tensor", "context"), moves)

    def added(kept, arrived):
        return (kept.astype(F32) + arrived.astype(F32)).astype(BF16)

    def finish_near(partials, arrived):
        mine, other = [added(partials[j], arrived[j]) for j in range(2)]
        return [mine, swap(other, NEAR[1])]

    def finish_far(token, member):
        kept, sent = project([out_weight, beside] + third + fourth, [token], same, split=True)
        arrived = lax.ppermute(sent, "tensor", [(0, 1), (1, 0)])
        return swap(added(kept[0], arrived[0]), member)

    gated, third[0], beside = lax.optimization_barrier((gated, third[0], beside))
    near = [gated, swap(gated, NEAR[1])]
    far_first = swap(gated, FAR[0])
    fourth = [swap(third[0], ACROSS_Y)]
    near_part = project([out_weight, beside], near, same)[0]
    near_arrived, third[1] = lax.optimization_barrier((over_tensor(near_part, True), third[1]))
    fourth.append(swap(third[1], ACROSS_Y))
    third_part = project(third, near, same)[0]
    third_arrived = over_tensor(third_part, False)
    far_first, fourth, third_arrived = lax.optimization_barrier(
        (far_first, fourth, third_arrived)
    )
    far = [far_first, swap(far_first, NEAR[1])]
    far_out = [finish_far(token, member) for token, member in zip(far, FAR)]
    fourth_part = project(fourth, near, same)[0]
    near_out = finish_near(near_part, near_arrived)
    third_out = finish_near(third_part, third_arrived)
    fourth_out = finish_near(fourth_part, over_tensor(fourth_part, False))
    where = jnp.stack([same, place % top]).astype(jnp.int32)
    return assemble(where, far_out, near_out, third_out, fourth_out)


def solution(mesh):
    planes = mesh.shape["tensor"] == 2 and mesh.shape["context"] == CREW * PLANES
    return jax.shard_map(
        per_device_planes if planes else per_device,
        mesh=mesh,
        in_specs=(
            P("context", "tensor"),
            P("context", "tensor"),
            P("context", "tensor"),
            P(None, None, "tensor"),
            P(None, "tensor"),
            P(None, "tensor"),
            P("context", "tensor"),
        ),
        out_specs=P("tensor", "context"),
        check_vma=False,
    )
```

```python
import functools

import jax
import jax.numpy as jnp
from jax import lax
from jax.experimental import pallas as pl
from jax.experimental.pallas import tpu as pltpu
from jax.sharding import PartitionSpec as P

LANES = 128
SEGS = 8
CREW = 4
LEAD = 2
PLANES = 4
NEAR = (0, 1)
ACROSS_Y = 2
FAR = (4, 5)
VMEM_GRANT = 56 * 2**20
F32 = jnp.float32
BF16 = jnp.bfloat16


def lane_block(chan_count):
    return 512 if chan_count % 512 == 0 else LANES


def tree_sum(terms):
    terms = list(terms)
    while len(terms) > 1:
        paired = [terms[i] + terms[i + 1] for i in range(0, len(terms) - 1, 2)]
        if len(terms) % 2:
            paired.append(terms[-1])
        terms = paired
    return terms[0]


def spread(row):
    return jnp.broadcast_to(row, (SEGS, LANES))


def local_kernel(
    total, q_ref, k_ref, v_ref, rim_ref, filter_ref, decay_ref, residue_ref,
    qf_ref, y_ref, carry_ref, end_ref, shifted, signal,
):
    rows, width = q_ref.shape
    modes = decay_ref.shape[0]
    length = rows // SEGS
    kinds, tap_count, groups = filter_ref.shape
    group_width = pl.num_programs(0) * width // groups
    chan = pl.program_id(0) * width + lax.broadcasted_iota(jnp.int32, (groups, width), 1)
    first = lax.broadcasted_iota(jnp.int32, (groups, width), 0) * group_width
    member = ((chan >= first) & (chan < first + group_width)).astype(BF16)
    taps = [
        jnp.dot(filter_ref[kind], member, preferred_element_type=F32) for kind in range(kinds)
    ]
    lead = LEAD

    def short_pass(which, ref, lanes):
        pad = shifted.at[which]
        pad[SEGS : SEGS + rows, :] = ref[:, lanes].astype(F32)
        pad[SEGS - lead : SEGS, :] = rim_ref[which * lead : (which + 1) * lead, lanes]
        running = None
        for offset in range(tap_count):
            tap = taps[which][offset : offset + 1, lanes]
            term = tap * pad[SEGS - offset : SEGS - offset + rows, :]
            running = term if running is None else running + term
        return running.astype(BF16)

    for block in range(width // LANES):
        lanes = slice(block * LANES, (block + 1) * LANES)
        qf_ref[:, lanes] = short_pass(0, q_ref, lanes)
        k_feat = short_pass(1, k_ref, lanes).astype(F32)
        v_feat = short_pass(2, v_ref, lanes).astype(F32)
        signal[block] = (k_feat * v_feat).astype(BF16).astype(F32)

    seg = lax.broadcasted_iota(jnp.int32, (SEGS, LANES), 0)
    for block in range(width // LANES):
        lanes = slice(block * LANES, (block + 1) * LANES)
        steps = decay_ref[:, lanes] / total
        decays = jnp.exp(-steps)
        scales = residue_ref[:, lanes] * jnp.sqrt(2.0 * steps)
        decay = [spread(decays[m : m + 1]) for m in range(modes)]
        scale = [spread(scales[m : m + 1]) for m in range(modes)]

        def advance(i, state):
            x = signal[block, pl.ds(i, SEGS, stride=length), :]
            state = tuple(d * s + x for d, s in zip(decay, state))
            y_ref[i, :, lanes] = tree_sum(c * s for c, s in zip(scale, state))
            return state

        zero = jnp.zeros((SEGS, LANES), F32)
        state = lax.fori_loop(0, length, advance, (zero,) * modes, unroll=4)
        for m in range(modes):
            ends = state[m]
            for hop in (1, 2, 4):
                factor = spread(jnp.exp(-steps[m : m + 1] * float(length * hop)))
                ends = ends + factor * jnp.where(seg >= hop, pltpu.roll(ends, hop, 0), 0.0)
            end_ref[m : m + 1, lanes] = ends[SEGS - 1 : SEGS]
            carry_ref[m, :, lanes] = jnp.where(seg >= 1, pltpu.roll(ends, 1, 0), 0.0)


def gate_kernel(
    total, qf_ref, y_ref, carry_ref, incoming_ref, decay_ref, residue_ref, out_ref, mixed
):
    rows, width = qf_ref.shape
    modes = decay_ref.shape[0]
    length = rows // SEGS
    begin = (lax.broadcasted_iota(jnp.int32, (SEGS, LANES), 0) * length).astype(F32)
    for block in range(width // LANES):
        lanes = slice(block * LANES, (block + 1) * LANES)
        steps = decay_ref[:, lanes] / total
        decays = jnp.exp(-steps)
        weights = residue_ref[:, lanes] * jnp.sqrt(2.0 * steps) * decays
        decay = [spread(decays[m : m + 1]) for m in range(modes)]
        tail = []
        for m in range(modes):
            reach = jnp.exp(-spread(steps[m : m + 1]) * begin)
            held = carry_ref[m, :, lanes] + reach * spread(incoming_ref[m : m + 1, lanes])
            tail.append(spread(weights[m : m + 1]) * held)

        def advance(i, tail):
            mixed[block, pl.ds(i, SEGS, stride=length), :] = y_ref[i, :, lanes] + tree_sum(tail)
            return tuple(d * s for d, s in zip(decay, tail))

        lax.fori_loop(0, length, advance, tuple(tail), unroll=4)
    for block in range(width // LANES):
        lanes = slice(block * LANES, (block + 1) * LANES)
        out_ref[:, lanes] = (qf_ref[:, lanes].astype(F32) * mixed[block]).astype(BF16)


def column_call(body, name, arrays, outs, scratch, width, chan_count):
    def spec(shape):
        if shape[-1] != chan_count:
            return pl.BlockSpec(shape, lambda c: (0,) * len(shape))
        return pl.BlockSpec(shape[:-1] + (width,), lambda c: (0,) * (len(shape) - 1) + (c,))

    return pl.pallas_call(
        body,
        grid=(chan_count // width,),
        in_specs=[spec(a.shape) for a in arrays],
        out_specs=[spec(o.shape) for o in outs],
        out_shape=outs,
        scratch_shapes=scratch,
        compiler_params=pltpu.CompilerParams(vmem_limit_bytes=VMEM_GRANT),
        name=name,
    )(*arrays)


def local_rows(q_proj, k_proj, v_proj, rims, short_filter, residue, decay_rate):
    rows, chan_count = q_proj.shape
    modes = decay_rate.shape[0]
    total = float(rows * lax.axis_size("context"))
    width = lane_block(chan_count)
    return column_call(
        functools.partial(local_kernel, total), "local_pass",
        (q_proj, k_proj, v_proj, rims, short_filter, decay_rate, residue),
        [
            jax.ShapeDtypeStruct((rows, chan_count), BF16),
            jax.ShapeDtypeStruct((rows // SEGS, SEGS, chan_count), F32),
            jax.ShapeDtypeStruct((modes, SEGS, chan_count), F32),
            jax.ShapeDtypeStruct((modes, chan_count), F32),
        ],
        [
            pltpu.VMEM((3, rows + SEGS, LANES), F32),
            pltpu.VMEM((width // LANES, rows, LANES), F32),
        ],
        width, chan_count,
    )


def gate_rows(q_feat, y_local, carry, incoming, decay_rate, residue):
    rows, chan_count = q_feat.shape
    total = float(rows * lax.axis_size("context"))
    width = lane_block(chan_count)
    return column_call(
        functools.partial(gate_kernel, total), "gate_pass",
        (q_feat, y_local, carry, incoming, decay_rate, residue),
        [jax.ShapeDtypeStruct((rows, chan_count), BF16)],
        [pltpu.VMEM((width // LANES, rows, LANES), F32)],
        width, chan_count,
    )[0]


def product_kernel(weight_count, token_count, same_ref, *refs):
    weights, tokens = refs[:weight_count], refs[weight_count : weight_count + token_count]
    outs, total, joined = refs[weight_count + token_count : -2], refs[-2], refs[-1]
    step = pl.program_id(0)

    @pl.when(step == 0)
    def _():
        total[...] = jnp.zeros_like(total)

    begin = 0
    for weight in weights:
        end = begin + weight.shape[0]
        joined[begin:end, :] = weight[...]
        begin = end
    for j, token in enumerate(tokens):
        total[j] += lax.dot_general(
            joined[...], token[...], (((1,), (1,)), ((), ())), preferred_element_type=F32
        )

    @pl.when(step == pl.num_programs(0) - 1)
    def _():
        if len(outs) == 1:
            outs[0][...] = total[...].astype(BF16)
        else:
            middle = total.shape[1] // 2
            for same in (1, 0):

                @pl.when(same_ref[0] == same)
                def _():
                    outs[1 - same][...] = total[:, :middle, :].astype(BF16)
                    outs[same][...] = total[:, middle:, :].astype(BF16)


def project(weights, tokens, same, split=False):
    rows, depth = tokens[0].shape
    width = 1024 if depth % 1024 == 0 else LANES
    feat = sum(w.shape[0] for w in weights)
    out_feat = feat // 2 if split else feat
    shape = (len(tokens), out_feat, rows)
    out_count = 2 if split else 1
    return pl.pallas_call(
        functools.partial(product_kernel, len(weights), len(tokens)),
        grid_spec=pltpu.PrefetchScalarGridSpec(
            num_scalar_prefetch=1,
            grid=(depth // width,),
            in_specs=[
                pl.BlockSpec((a.shape[0], width), lambda c, _: (0, c)) for a in weights + tokens
            ],
            out_specs=[pl.BlockSpec(shape, lambda c, _: (0, 0, 0))] * out_count,
            scratch_shapes=[
                pltpu.VMEM((len(tokens), feat, rows), F32),
                pltpu.VMEM((feat, width), BF16),
            ],
        ),
        out_shape=[jax.ShapeDtypeStruct(shape, BF16)] * out_count,
        compiler_params=pltpu.CompilerParams(vmem_limit_bytes=VMEM_GRANT),
        name="project",
    )(same.reshape(1), *weights, *tokens)


def assemble_kernel(place_ref, *refs):
    feat = refs[0].shape[0] // 2
    same, seat = place_ref[0], place_ref[1]
    out_ref = refs[-1]

    def put(block, member, value):
        at = pl.multiple_of((seat ^ member ^ block) * feat, feat)
        out_ref[pl.ds(at, feat), :] = value

    for at, member in enumerate(FAR):
        for half, block in enumerate((0, ACROSS_Y)):
            put(block, member, refs[at][half * feat : (half + 1) * feat, :])
    for at, member in enumerate(NEAR):
        near, third, fourth = refs[2 + at], refs[4 + at], refs[6 + at]

        @pl.when(same == 1)
        def _():
            put(0, member, near[:feat, :])
            put(ACROSS_Y, member, near[feat:, :])

        @pl.when(same == 0)
        def _():
            put(0, member, third[...])
            put(ACROSS_Y, member, fourth[...])


def assemble(place, far, near, third, fourth):
    rows = far[0].shape[1]
    vmem = pl.BlockSpec(memory_space=pltpu.VMEM)
    return pl.pallas_call(
        assemble_kernel,
        in_specs=[pl.BlockSpec(memory_space=pltpu.SMEM)] + [vmem] * 8,
        out_specs=vmem,
        out_shape=jax.ShapeDtypeStruct((4 * far[0].shape[0], rows), BF16),
        compiler_params=pltpu.CompilerParams(vmem_limit_bytes=VMEM_GRANT),
        name="assemble",
    )(place, *far, *near, *third, *fourth)


def tails_kernel(q_ref, k_ref, v_ref, out_ref):
    lead = LEAD
    for which, ref in enumerate((q_ref, k_ref, v_ref)):
        rows = ref[...].astype(F32)
        out_ref[which * lead : (which + 1) * lead, :] = rows[rows.shape[0] - lead :]
    out_ref[3 * lead :, :] = jnp.zeros((out_ref.shape[0] - 3 * lead, out_ref.shape[1]), F32)


def gather_rims(q_proj, k_proj, v_proj):
    size = lax.axis_size("context")
    rows, chan_count = q_proj.shape
    last = pl.BlockSpec((16, chan_count), lambda i: (rows // 16 - 1, 0))
    tails = pl.pallas_call(
        tails_kernel,
        grid=(1,),
        in_specs=[last] * 3,
        out_specs=pl.BlockSpec((SEGS, chan_count), lambda i: (0, 0)),
        out_shape=jax.ShapeDtypeStruct((SEGS, chan_count), F32),
        compiler_params=pltpu.CompilerParams(vmem_limit_bytes=VMEM_GRANT),
        name="tails",
    )(q_proj, k_proj, v_proj)
    return lax.ppermute(tails, "context", [(i, i + 1) for i in range(size - 1)])


def per_device(q_proj, k_proj, v_proj, short_filter, residue, decay_rate, out_weight):
    place, size = lax.axis_index("context"), lax.axis_size("context")

    rows = q_proj.shape[0]
    rims = gather_rims(q_proj, k_proj, v_proj)
    q_feat, y_local, carry, ends = local_rows(
        q_proj, k_proj, v_proj, rims, short_filter, residue, decay_rate
    )
    gathered = lax.all_gather(ends, "context")
    gaps = (place - 1 - jnp.arange(size))[:, None, None]
    reach = jnp.exp(-(decay_rate / float(rows * size))[None] * (gaps * rows).astype(F32))
    incoming = jnp.sum(jnp.where(gaps >= 0, reach * gathered, 0.0), axis=0)
    gated = gate_rows(q_feat, y_local, carry, incoming, decay_rate, residue)
    partial_terms = lax.dot_general(
        lax.all_gather(out_weight, "context", axis=0, tiled=True),
        gated,
        (((1,), (1,)), ((), ())),
        preferred_element_type=F32,
    )
    return lax.psum_scatter(
        partial_terms.astype(BF16), "tensor", scatter_dimension=0, tiled=True
    )


def swap(block, mask):
    size = lax.axis_size("context")
    return lax.ppermute(block, "context", [(i, i ^ mask) for i in range(size)])


def shift(block, distance):
    size = lax.axis_size("context")
    moves = [(i, i + distance) for i in range(size) if 0 <= i + distance < size]
    return lax.ppermute(block, "context", moves)


def exchange_states(ends, steps, rows, place):
    chan_count = ends.shape[1]
    quarter = chan_count // CREW
    seat = place % CREW

    def part(array, owner):
        return lax.dynamic_slice_in_dim(array, owner * quarter, quarter, 1)

    own_steps = part(steps, seat)

    def reach(count):
        return jnp.exp(-own_steps * (rows * count).astype(F32))

    blocks = [part(ends, seat)] + [swap(part(ends, seat ^ j), j) for j in range(1, CREW)]
    plane = sum(reach(CREW - 1 - (seat ^ j)) * blocks[j] for j in range(CREW))
    before = jnp.zeros_like(plane)
    for hop in range(1, PLANES):
        arrived = shift(plane, hop * CREW)
        before = before + jnp.exp(-own_steps * float(rows * CREW * (hop - 1))) * arrived

    def for_seat(target):
        state = reach(target) * before
        for j in range(CREW):
            gap = target - 1 - (seat ^ j)
            state = state + jnp.where(gap >= 0, reach(jnp.maximum(gap, 0)) * blocks[j], 0.0)
        return state

    mine = [for_seat(seat)] + [swap(for_seat(seat ^ j), j) for j in range(1, CREW)]
    odd, high = seat % 2 == 1, seat >= 2
    ordered = [jnp.where(odd, mine[j ^ 1], mine[j]) for j in range(CREW)]
    ordered = [jnp.where(high, ordered[j ^ 2], ordered[j]) for j in range(CREW)]
    return jnp.concatenate(ordered, axis=1)


def per_device_planes(q_proj, k_proj, v_proj, short_filter, residue, decay_rate, out_weight):
    size = lax.axis_size("context")
    place, side = lax.axis_index("context"), lax.axis_index("tensor")
    top = 2 * FAR[0]
    same = (side == place // top).astype(jnp.int32)

    rows, feat = q_proj.shape[0], out_weight.shape[0]
    cuts = [0, feat // 4, feat * 3 // 4, feat]

    rims = gather_rims(q_proj, k_proj, v_proj)
    rims, early = lax.optimization_barrier((rims, out_weight))
    third = [swap(early[: cuts[1]], top)]
    beside = [swap(early[: feat // 2], ACROSS_Y)]
    q_feat, y_local, carry, ends = local_rows(
        q_proj, k_proj, v_proj, rims, short_filter, residue, decay_rate
    )
    ends, third[0], beside[0] = lax.optimization_barrier((ends, third[0], beside[0]))
    incoming = exchange_states(ends, decay_rate / float(rows * size), rows, place)
    incoming, later = lax.optimization_barrier((incoming, out_weight))
    third += [swap(later[low:high], top) for low, high in zip(cuts[1:], cuts[2:])]
    beside.append(swap(later[feat // 2 :], ACROSS_Y))
    gated = lax.cond(
        place < size,
        gate_rows,
        lambda q_feat, *_: jnp.zeros_like(q_feat),
        q_feat, y_local, carry, incoming, decay_rate, residue,
    )

    def over_tensor(block, to_same):
        moves = []
        for i in range(size):
            keeper = i // top if to_same else 1 - i // top
            moves.append(((1 - keeper) * size + i, keeper * size + i))
        return lax.ppermute(block, ("tensor", "context"), moves)

    def added(kept, arrived):
        return (kept.astype(F32) + arrived.astype(F32)).astype(BF16)

    def finish_near(partials, arrived):
        mine, other = [added(partials[j], arrived[j]) for j in range(2)]
        return [mine, swap(other, NEAR[1])]

    def finish_far(token, member):
        kept, sent = project([out_weight] + beside + third + fourth, [token], same, split=True)
        arrived = lax.ppermute(sent, "tensor", [(0, 1), (1, 0)])
        return swap(added(kept[0], arrived[0]), member)

    near = [gated, swap(gated, NEAR[1])]
    far_first = swap(gated, FAR[0])
    near_part = project([out_weight] + beside, near, same)[0]
    near_arrived = over_tensor(near_part, True)
    fourth = [swap(third[0], ACROSS_Y)]
    near_arrived, third[1] = lax.optimization_barrier((near_arrived, third[1]))
    fourth.append(swap(third[1], ACROSS_Y))
    fourth.append(swap(third[2], ACROSS_Y))
    third_part = project(third, near, same)[0]
    third_arrived = over_tensor(third_part, False)
    far_first, fourth, third_arrived = lax.optimization_barrier(
        (far_first, fourth, third_arrived)
    )
    far = [far_first, swap(far_first, NEAR[1])]
    far_out = [finish_far(token, member) for token, member in zip(far, FAR)]
    fourth_part = project(fourth, near, same)[0]
    near_out = finish_near(near_part, near_arrived)
    third_out = finish_near(third_part, third_arrived)
    fourth_out = finish_near(fourth_part, over_tensor(fourth_part, False))
    where = jnp.stack([same, place % top]).astype(jnp.int32)
    return assemble(where, far_out, near_out, third_out, fourth_out)


def solution(mesh):
    planes = mesh.shape["tensor"] == 2 and mesh.shape["context"] == CREW * PLANES
    return jax.shard_map(
        per_device_planes if planes else per_device,
        mesh=mesh,
        in_specs=(
            P("context", "tensor"),
            P("context", "tensor"),
            P("context", "tensor"),
            P(None, None, "tensor"),
            P(None, "tensor"),
            P(None, "tensor"),
            P("context", "tensor"),
        ),
        out_specs=P("tensor", "context"),
        check_vma=False,
    )
```

```python
import functools

import jax
import jax.numpy as jnp
from jax import lax
from jax.experimental import pallas as pl
from jax.experimental.pallas import tpu as pltpu
from jax.sharding import PartitionSpec as P

LANES = 128
SEGS = 8
CREW = 4
LEAD = 2
PLANES = 4
VMEM_GRANT = 56 * 2**20
F32 = jnp.float32
BF16 = jnp.bfloat16


def lane_block(chan_count):
    for width in (1024, 512):
        if chan_count % (CREW * width) == 0:
            return width
    return LANES


def tree_sum(terms):
    terms = list(terms)
    while len(terms) > 1:
        paired = [terms[i] + terms[i + 1] for i in range(0, len(terms) - 1, 2)]
        if len(terms) % 2:
            paired.append(terms[-1])
        terms = paired
    return terms[0]


def spread(row):
    return jnp.broadcast_to(row, (SEGS, LANES))


def local_kernel(
    total, q_ref, k_ref, v_ref, rim_ref, filter_ref, decay_ref, residue_ref,
    qf_ref, y_ref, carry_ref, end_ref, shifted, signal,
):
    rows, width = q_ref.shape
    modes = decay_ref.shape[0]
    length = rows // SEGS
    kinds, tap_count, groups = filter_ref.shape
    group_width = pl.num_programs(0) * width // groups
    chan = pl.program_id(0) * width + lax.broadcasted_iota(jnp.int32, (groups, width), 1)
    first = lax.broadcasted_iota(jnp.int32, (groups, width), 0) * group_width
    member = ((chan >= first) & (chan < first + group_width)).astype(BF16)
    taps = [
        jnp.dot(filter_ref[kind], member, preferred_element_type=F32) for kind in range(kinds)
    ]
    lead = LEAD

    def short_pass(which, ref, lanes):
        pad = shifted.at[which]
        pad[SEGS : SEGS + rows, :] = ref[:, lanes].astype(F32)
        pad[SEGS - lead : SEGS, :] = rim_ref[which * lead : (which + 1) * lead, lanes]
        running = None
        for offset in range(tap_count):
            tap = taps[which][offset : offset + 1, lanes]
            term = tap * pad[SEGS - offset : SEGS - offset + rows, :]
            running = term if running is None else running + term
        return running.astype(BF16)

    for block in range(width // LANES):
        lanes = slice(block * LANES, (block + 1) * LANES)
        qf_ref[:, lanes] = short_pass(0, q_ref, lanes)
        k_feat = short_pass(1, k_ref, lanes).astype(F32)
        v_feat = short_pass(2, v_ref, lanes).astype(F32)
        signal[block] = (k_feat * v_feat).astype(BF16).astype(F32)

    seg = lax.broadcasted_iota(jnp.int32, (SEGS, LANES), 0)
    for block in range(width // LANES):
        lanes = slice(block * LANES, (block + 1) * LANES)
        steps = decay_ref[:, lanes] / total
        decays = jnp.exp(-steps)
        scales = residue_ref[:, lanes] * jnp.sqrt(2.0 * steps)
        decay = [spread(decays[m : m + 1]) for m in range(modes)]
        scale = [spread(scales[m : m + 1]) for m in range(modes)]

        def advance(i, state):
            x = signal[block, pl.ds(i, SEGS, stride=length), :]
            state = tuple(d * s + x for d, s in zip(decay, state))
            y_ref[i, :, lanes] = tree_sum(c * s for c, s in zip(scale, state))
            return state

        zero = jnp.zeros((SEGS, LANES), F32)
        state = lax.fori_loop(0, length, advance, (zero,) * modes, unroll=4)
        for m in range(modes):
            ends = state[m]
            for hop in (1, 2, 4):
                factor = spread(jnp.exp(-steps[m : m + 1] * float(length * hop)))
                ends = ends + factor * jnp.where(seg >= hop, pltpu.roll(ends, hop, 0), 0.0)
            end_ref[m : m + 1, lanes] = ends[SEGS - 1 : SEGS]
            carry_ref[m, :, lanes] = jnp.where(seg >= 1, pltpu.roll(ends, 1, 0), 0.0)


def gate_kernel(
    total, seat_ref, qf_ref, y_ref, carry_ref, incoming_ref, decay_ref, residue_ref,
    head_ref, rest_ref, mixed,
):
    rows, width = qf_ref.shape
    modes = decay_ref.shape[0]
    length = rows // SEGS
    begin = (lax.broadcasted_iota(jnp.int32, (SEGS, LANES), 0) * length).astype(F32)
    for block in range(width // LANES):
        lanes = slice(block * LANES, (block + 1) * LANES)
        steps = decay_ref[:, lanes] / total
        decays = jnp.exp(-steps)
        weights = residue_ref[:, lanes] * jnp.sqrt(2.0 * steps) * decays
        decay = [spread(decays[m : m + 1]) for m in range(modes)]
        tail = []
        for m in range(modes):
            reach = jnp.exp(-spread(steps[m : m + 1]) * begin)
            held = carry_ref[m, :, lanes] + reach * spread(incoming_ref[m : m + 1, lanes])
            tail.append(spread(weights[m : m + 1]) * held)

        def advance(i, tail):
            mixed[block, pl.ds(i, SEGS, stride=length), :] = y_ref[i, :, lanes] + tree_sum(tail)
            return tuple(d * s for d, s in zip(decay, tail))

        lax.fori_loop(0, length, advance, tuple(tail), unroll=4)
    for block in range(width // LANES):
        lanes = slice(block * LANES, (block + 1) * LANES)
        gated = (qf_ref[:, lanes].astype(F32) * mixed[block]).astype(BF16)
        head_ref[:, lanes] = gated[: rows // 2]
        rest_ref[:, lanes] = gated[rows // 2 :]


def column_call(body, name, arrays, outs, scratch, width, chan_count):
    def spec(shape):
        if shape[-1] != chan_count:
            return pl.BlockSpec(shape, lambda c: (0,) * len(shape))
        return pl.BlockSpec(shape[:-1] + (width,), lambda c: (0,) * (len(shape) - 1) + (c,))

    return pl.pallas_call(
        body,
        grid=(chan_count // width,),
        in_specs=[spec(a.shape) for a in arrays],
        out_specs=[spec(o.shape) for o in outs],
        out_shape=outs,
        scratch_shapes=scratch,
        compiler_params=pltpu.CompilerParams(vmem_limit_bytes=VMEM_GRANT),
        name=name,
    )(*arrays)


def local_rows(q_proj, k_proj, v_proj, rims, short_filter, residue, decay_rate):
    rows, chan_count = q_proj.shape
    modes = decay_rate.shape[0]
    total = float(rows * lax.axis_size("context"))
    width = lane_block(chan_count)
    return column_call(
        functools.partial(local_kernel, total), "local_pass",
        (q_proj, k_proj, v_proj, rims, short_filter, decay_rate, residue),
        [
            jax.ShapeDtypeStruct((rows, chan_count), BF16),
            jax.ShapeDtypeStruct((rows // SEGS, SEGS, chan_count), F32),
            jax.ShapeDtypeStruct((modes, SEGS, chan_count), F32),
            jax.ShapeDtypeStruct((modes, chan_count), F32),
        ],
        [
            pltpu.VMEM((3, rows + SEGS, LANES), F32),
            pltpu.VMEM((width // LANES, rows, LANES), F32),
        ],
        width, chan_count,
    )


def gate_rows(q_feat, y_local, carry, incoming, decay_rate, residue, seat):
    rows, chan_count = q_feat.shape
    modes = decay_rate.shape[0]
    total = float(rows * lax.axis_size("context"))
    width = lane_block(chan_count)
    per_part = incoming.shape[2] // width

    def cols(height):
        return pl.BlockSpec((height, width), lambda c, s: (0, c))

    return pl.pallas_call(
        functools.partial(gate_kernel, total),
        grid_spec=pltpu.PrefetchScalarGridSpec(
            num_scalar_prefetch=1,
            grid=(chan_count // width,),
            in_specs=[
                cols(rows),
                pl.BlockSpec((rows // SEGS, SEGS, width), lambda c, s: (0, 0, c)),
                pl.BlockSpec((modes, SEGS, width), lambda c, s: (0, 0, c)),
                pl.BlockSpec(
                    (None, modes, width), lambda c, s: (s[0] ^ (c // per_part), 0, c % per_part)
                ),
                cols(modes),
                cols(modes),
            ],
            out_specs=[cols(rows // 2)] * 2,
            scratch_shapes=[pltpu.VMEM((width // LANES, rows, LANES), F32)],
        ),
        out_shape=[jax.ShapeDtypeStruct((rows // 2, chan_count), BF16)] * 2,
        compiler_params=pltpu.CompilerParams(vmem_limit_bytes=VMEM_GRANT),
        name="gate_pass",
    )(seat.reshape(1), q_feat, y_local, carry, incoming, decay_rate, residue)


def by_seat(seat, blocks):
    ordered = []
    for k in range(CREW):
        value = blocks[0]
        for j in range(1, CREW):
            value = jnp.where((seat ^ k) == j, blocks[j], value)
        ordered.append(value)
    return ordered


def plane_kernel(span, seat_ref, steps_ref, *refs):
    blocks, out_ref = refs[:CREW], refs[CREW]
    reach = jnp.exp(-steps_ref[...] * span)
    ends = by_seat(seat_ref[0], [b[...] for b in blocks])
    state = ends[0]
    for end in ends[1:]:
        state = reach * state + end
    out_ref[...] = state


def incoming_kernel(span, seat_ref, steps_ref, *refs):
    blocks, planes = refs[:CREW], refs[CREW : CREW + PLANES - 1]
    outs = refs[CREW + PLANES - 1 :]
    steps, seat = steps_ref[...], seat_ref[0]
    ends = by_seat(seat, [b[...] for b in blocks])
    reach, reach_plane = jnp.exp(-steps * span), jnp.exp(-steps * (span * CREW))
    state = planes[-1][...]
    for plane in planes[-2::-1]:
        state = reach_plane * state + plane[...]
    states = [state]
    for end in ends[:-1]:
        states.append(reach * states[-1] + end)
    for out_ref, value in zip(outs, by_seat(seat, states)):
        out_ref[...] = value


def state_call(body, name, seat, steps, ends, arrays, out_count):
    modes, quarter = arrays[0].shape

    def owned(_, s):
        return (0, s[0])

    own = pl.BlockSpec((modes, quarter), owned)
    whole = pl.BlockSpec((modes, quarter), lambda _, s: (0, 0))
    shape = jax.ShapeDtypeStruct((modes, quarter), F32)
    return pl.pallas_call(
        body,
        grid_spec=pltpu.PrefetchScalarGridSpec(
            num_scalar_prefetch=1,
            grid=(1,),
            in_specs=[own, own] + [whole] * len(arrays),
            out_specs=[whole] * out_count,
        ),
        out_shape=[shape] * out_count,
        name=name,
    )(seat.reshape(1), steps, ends, *arrays)


def product_kernel(sizes, counts, pieces, pick_ref, *refs):
    refs = list(refs)
    weights = [[refs.pop(0) for _ in range(count)] for count in counts]
    tokens = [[refs.pop(0) for _ in range(count)] for count in pieces]
    outs, (total, joined, pasted) = refs[:-3], refs[-3:]
    step = pl.program_id(0)

    @pl.when(step == 0)
    def _():
        total[...] = jnp.zeros_like(total)

    begin = 0
    for at, (size, choices) in enumerate(zip(sizes, weights)):
        for choice, source in enumerate(choices):

            @pl.when(pick_ref[at] == choice)
            def _():
                joined[begin : begin + size, :] = source[...]

        begin += size
    for j, parts in enumerate(tokens):
        token = parts[0]
        if len(parts) > 1:
            begin = 0
            for part in parts:
                pasted[begin : begin + part.shape[0], :] = part[...]
                begin += part.shape[0]
            token = pasted
        total[j] += lax.dot_general(
            joined[...], token[...], (((1,), (1,)), ((), ())), preferred_element_type=F32
        )

    @pl.when(step == pl.num_programs(0) - 1)
    def _():
        begin = 0
        for out_ref in outs:
            out_ref[...] = total[:, begin : begin + out_ref.shape[1], :].astype(BF16)
            begin += out_ref.shape[1]


def project(slots, picks, tokens, out_sizes):
    rows, depth = sum(part.shape[0] for part in tokens[0]), tokens[0][0].shape[1]
    width = 1024 if depth % 1024 == 0 else LANES

    def columns(size, at):
        return pl.BlockSpec((size, width), lambda c, _: (at, c))

    sizes = [size for size, _ in slots]
    flat = [array for _, choices in slots for array, _ in choices]
    specs = [columns(size, at) for size, choices in slots for _, at in choices]
    flat += [part for token in tokens for part in token]
    specs += [columns(part.shape[0], 0) for token in tokens for part in token]
    feat = sum(sizes)
    shapes = [(len(tokens), size, rows) for size in out_sizes]
    return pl.pallas_call(
        functools.partial(
            product_kernel,
            sizes,
            [len(choices) for _, choices in slots],
            [len(token) for token in tokens],
        ),
        grid_spec=pltpu.PrefetchScalarGridSpec(
            num_scalar_prefetch=1,
            grid=(depth // width,),
            in_specs=specs,
            out_specs=[pl.BlockSpec(shape, lambda c, _: (0, 0, 0)) for shape in shapes],
            scratch_shapes=[
                pltpu.VMEM((len(tokens), feat, rows), F32),
                pltpu.VMEM((feat, width), BF16),
                pltpu.VMEM((rows, width), BF16),
            ],
        ),
        out_shape=[jax.ShapeDtypeStruct(shape, BF16) for shape in shapes],
        compiler_params=pltpu.CompilerParams(vmem_limit_bytes=VMEM_GRANT),
        cost_estimate=pl.CostEstimate(flops=1, bytes_accessed=1, transcendentals=0),
        name="project",
    )(jnp.stack(picks).astype(jnp.int32), *flat)


def relay_kernel(pick_ref, one_ref, other_ref, *outs):
    for first, source in ((1, one_ref), (0, other_ref)):

        @pl.when(pick_ref[0] == first)
        def _():
            begin = 0
            for out_ref in outs:
                out_ref[...] = source[begin : begin + out_ref.shape[0], :]
                begin += out_ref.shape[0]


def relayed(pick, one, other, sizes):
    feat, depth = one.shape
    width = 1024 if depth % 1024 == 0 else LANES
    return pl.pallas_call(
        relay_kernel,
        grid_spec=pltpu.PrefetchScalarGridSpec(
            num_scalar_prefetch=1,
            grid=(depth // width,),
            in_specs=[pl.BlockSpec((feat, width), lambda c, _: (0, c))] * 2,
            out_specs=[pl.BlockSpec((size, width), lambda c, _: (0, c)) for size in sizes],
        ),
        out_shape=[jax.ShapeDtypeStruct((size, depth), BF16) for size in sizes],
        compiler_params=pltpu.CompilerParams(vmem_limit_bytes=VMEM_GRANT),
        cost_estimate=pl.CostEstimate(flops=1, bytes_accessed=1, transcendentals=0),
        name="relay",
    )(pick.astype(jnp.int32).reshape(1), one, other)


def assemble_kernel(place_ref, *refs):
    early, late, last = (refs[i * CREW : (i + 1) * CREW] for i in range(3))
    out_ref = refs[-1]
    feat, part = early[0].shape[0] // 2, late[0].shape[0]
    half = out_ref.shape[0] // 2
    same, low, seat = place_ref[0], place_ref[1], place_ref[2]
    for j in range(CREW):
        within = (seat ^ j) * feat
        first = pl.multiple_of(low * half + within, feat)
        second = pl.multiple_of((1 - low) * half + within, feat)
        split = pl.multiple_of(second + part, feat - part)
        out_ref[pl.ds(first, feat), :] = early[j][:feat, :]

        @pl.when(same == 1)
        def _():
            out_ref[pl.ds(second, feat), :] = early[j][feat:, :]

        @pl.when(same == 0)
        def _():
            out_ref[pl.ds(second, part), :] = late[j][...]
            out_ref[pl.ds(split, feat - part), :] = last[j][...]


def assemble(place, early, late, last):
    rows = early[0].shape[1]
    vmem = pl.BlockSpec(memory_space=pltpu.VMEM)
    return pl.pallas_call(
        assemble_kernel,
        in_specs=[pl.BlockSpec(memory_space=pltpu.SMEM)] + [vmem] * (3 * CREW),
        out_specs=vmem,
        out_shape=jax.ShapeDtypeStruct((CREW * early[0].shape[0], rows), BF16),
        compiler_params=pltpu.CompilerParams(vmem_limit_bytes=VMEM_GRANT),
        name="assemble",
    )(place, *early, *late, *last)


def tails_kernel(q_ref, k_ref, v_ref, out_ref):
    lead = LEAD
    for which, ref in enumerate((q_ref, k_ref, v_ref)):
        rows = ref[...].astype(F32)
        out_ref[which * lead : (which + 1) * lead, :] = rows[rows.shape[0] - lead :]
    out_ref[3 * lead :, :] = jnp.zeros((out_ref.shape[0] - 3 * lead, out_ref.shape[1]), F32)


def gather_rims(q_proj, k_proj, v_proj):
    size = lax.axis_size("context")
    rows, chan_count = q_proj.shape
    last = pl.BlockSpec((16, chan_count), lambda i: (rows // 16 - 1, 0))
    tails = pl.pallas_call(
        tails_kernel,
        grid=(1,),
        in_specs=[last] * 3,
        out_specs=pl.BlockSpec((SEGS, chan_count), lambda i: (0, 0)),
        out_shape=jax.ShapeDtypeStruct((SEGS, chan_count), F32),
        compiler_params=pltpu.CompilerParams(vmem_limit_bytes=VMEM_GRANT),
        name="tails",
    )(q_proj, k_proj, v_proj)
    return lax.ppermute(tails, "context", [(i, i + 1) for i in range(size - 1)])


def per_device(q_proj, k_proj, v_proj, short_filter, residue, decay_rate, out_weight):
    place, size = lax.axis_index("context"), lax.axis_size("context")

    rows = q_proj.shape[0]
    rims = gather_rims(q_proj, k_proj, v_proj)
    q_feat, y_local, carry, ends = local_rows(
        q_proj, k_proj, v_proj, rims, short_filter, residue, decay_rate
    )
    gathered = lax.all_gather(ends, "context")
    gaps = (place - 1 - jnp.arange(size))[:, None, None]
    reach = jnp.exp(-(decay_rate / float(rows * size))[None] * (gaps * rows).astype(F32))
    incoming = jnp.sum(jnp.where(gaps >= 0, reach * gathered, 0.0), axis=0)
    gated = gate_rows(
        q_feat, y_local, carry, incoming[None], decay_rate, residue, jnp.int32(0)
    )
    gated = jnp.concatenate(gated, axis=0)
    partial_terms = lax.dot_general(
        lax.all_gather(out_weight, "context", axis=0, tiled=True),
        gated,
        (((1,), (1,)), ((), ())),
        preferred_element_type=F32,
    )
    return lax.psum_scatter(
        partial_terms.astype(BF16), "tensor", scatter_dimension=0, tiled=True
    )


def swap(block, mask):
    size = lax.axis_size("context")
    return lax.ppermute(block, "context", [(i, i ^ mask) for i in range(size)])


def shift(block, distance):
    size = lax.axis_size("context")
    moves = [(i, i + distance) for i in range(size) if 0 <= i + distance < size]
    return lax.ppermute(block, "context", moves)


def per_device_planes(q_proj, k_proj, v_proj, short_filter, residue, decay_rate, out_weight):
    size = lax.axis_size("context")
    place, side = lax.axis_index("context"), lax.axis_index("tensor")
    plane, seat = place // CREW, place % CREW
    low = plane % 2
    same = (side == plane // 2).astype(jnp.int32)
    rows, feat = q_proj.shape[0], out_weight.shape[0]
    quarter = q_proj.shape[1] // CREW
    span = float(rows)
    steps = decay_rate / (span * size)

    def hops(block, moves):
        return lax.ppermute(
            block, "context",
            [(a * CREW + s, b * CREW + s) for a, b in moves for s in range(CREW)],
        )

    def over_tensor(block, to_same):
        moves = []
        for i in range(size):
            half = i // CREW * 2 // PLANES
            keeper = half if to_same else 1 - half
            moves.append(((1 - keeper) * size + i, keeper * size + i))
        return lax.ppermute(block, ("tensor", "context"), moves)

    def deal(block, mask):
        moves = []
        for i in range(size):
            keeper = 1 - i // CREW * 2 // PLANES
            moves.append((keeper * size + i, keeper * size + (i ^ mask)))
        return lax.ppermute(block, ("tensor", "context"), moves)

    def added(kept, arrived):
        return (kept.astype(F32) + arrived.astype(F32)).astype(BF16)

    rims = gather_rims(q_proj, k_proj, v_proj)
    rims, outgoing = lax.optimization_barrier((rims, out_weight))
    up1, down1 = shift(outgoing, CREW), shift(outgoing, -CREW)
    q_feat, y_local, carry, ends = local_rows(
        q_proj, k_proj, v_proj, rims, short_filter, residue, decay_rate
    )
    blocks = [
        swap(lax.dynamic_slice_in_dim(ends, (seat ^ j) * quarter, quarter, 1), j)
        for j in range(1, CREW)
    ]
    total = state_call(
        functools.partial(plane_kernel, span), "plane_state", seat, steps, ends, blocks, 1
    )[0]
    planes = [shift(total, hop * CREW) for hop in range(1, PLANES)]
    planes[0], up1, down1 = lax.optimization_barrier((planes[0], up1, down1))
    up2 = hops(up1, [(1, 2), (2, 3)])
    down2 = hops(down1, [(2, 1), (1, 0)])

    def finish_gate(ends, steps, blocks, planes, q_feat, y_local, carry, decay_rate, residue):
        mine = state_call(
            functools.partial(incoming_kernel, span), "incoming_state",
            seat, steps, ends, blocks + planes, CREW,
        )
        incoming = jnp.stack([mine[0]] + [swap(mine[j], j) for j in range(1, CREW)])
        return list(gate_rows(q_feat, y_local, carry, incoming, decay_rate, residue, seat))

    gated = lax.cond(
        place < size,
        finish_gate,
        lambda *_: [jnp.zeros((rows // 2, q_proj.shape[1]), BF16)] * 2,
        ends, steps, blocks, planes, q_feat, y_local, carry, decay_rate, residue,
    )
    beyond = [swap(part, 2) for part in gated]
    sizes = [feat * 3 // 4, feat - feat * 3 // 4]
    outer = list(relayed(plane == 2, up2, down2, sizes))
    outer[0], outer[1], up2, down2 = lax.optimization_barrier((*outer, up2, down2))

    slots = [
        (feat, [(out_weight, 0)]),
        (feat, [(down1, 0), (up1, 0)]),
        (feat, [(down2, 0), (up2, 0)]),
    ]
    picks = [jnp.int32(0), low, (plane >= 2).astype(jnp.int32)]

    def combined(near, near_arrived, third, third_arrived, j):
        near_sum, third_sum = added(near[j], near_arrived[j]), added(third[j], third_arrived[j])
        first = jnp.where(same == 1, near_sum[:feat], third_sum)
        return jnp.concatenate([first, near_sum[feat:]], axis=0)

    def finish_early(*tokens):
        near, third = project(slots, picks, tokens, [2 * feat, feat])
        near_arrived, third_arrived = over_tensor(near, True), over_tensor(third, False)
        return [combined(near, near_arrived, third, third_arrived, j) for j in range(2)]

    def no_early(*tokens):
        return [jnp.zeros((2 * feat, rows), BF16)] * 2

    tokens = [tuple(gated), tuple(swap(part, 1) for part in gated)]
    early, beyond[1] = lax.optimization_barrier(
        (lax.cond(place < size, finish_early, no_early, *tokens), beyond[1])
    )
    beyond[0], _ = lax.optimization_barrier((beyond[0], outer[0]))
    tokens += [tuple(beyond), tuple(swap(part, 1) for part in beyond)]
    which = jnp.where(plane == 1, 1, jnp.where(plane == 2, 2, 0))

    def finish_late(part, at):
        size = part.shape[0]
        slot = (size, [(part, 0), (down1, at), (up1, at)])
        partial_terms = project([slot], [which], tokens, [size])[0]
        return partial_terms, over_tensor(partial_terms, False)

    near, third = project(slots, picks, tokens[2:], [2 * feat, feat])
    near_arrived, third_arrived = over_tensor(near, True), over_tensor(third, False)
    outer = [hops(part, [(1, 0), (2, 3)]) for part in outer]
    near, outer[0] = lax.optimization_barrier((near, outer[0]))
    late, late_arrived = finish_late(outer[0], 0)
    late, outer[1] = lax.optimization_barrier((late, outer[1]))
    last, last_arrived = finish_late(outer[1], sizes[0] // sizes[1])
    last, near_arrived, third_arrived = lax.optimization_barrier(
        (last, near_arrived, third_arrived)
    )
    early = list(early) + [
        combined(near, near_arrived, third, third_arrived, j) for j in range(2)
    ]
    early = [early[0]] + [swap(early[j], j) for j in range(1, CREW)]
    late = [added(late[j], late_arrived[j]) for j in range(CREW)]
    late = [late[0]] + [deal(late[j], j) for j in range(1, CREW)]
    last = [added(last[j], last_arrived[j]) for j in range(CREW)]
    last = [last[0]] + [deal(last[j], j) for j in range(1, CREW)]
    where = jnp.stack([same, low, seat]).astype(jnp.int32)
    return assemble(where, early, late, last)


def solution(mesh):
    planes = mesh.shape["tensor"] == 2 and mesh.shape["context"] == CREW * PLANES
    return jax.shard_map(
        per_device_planes if planes else per_device,
        mesh=mesh,
        in_specs=(
            P("context", "tensor"),
            P("context", "tensor"),
            P("context", "tensor"),
            P(None, None, "tensor"),
            P(None, "tensor"),
            P(None, "tensor"),
            P("context", "tensor"),
        ),
        out_specs=P("tensor", "context"),
        check_vma=False,
    )
```

```python
import functools

import jax
import jax.numpy as jnp
from jax import lax
from jax.experimental import pallas as pl
from jax.experimental.pallas import tpu as pltpu
from jax.sharding import PartitionSpec as P

LANES = 128
SEGS = 8
CREW = 4
LEAD = 2
PLANES = 4
VMEM_GRANT = 56 * 2**20
F32 = jnp.float32
BF16 = jnp.bfloat16


def lane_block(chan_count):
    for width in (1024, 512):
        if chan_count % (CREW * width) == 0:
            return width
    return LANES


def tree_sum(terms):
    terms = list(terms)
    while len(terms) > 1:
        paired = [terms[i] + terms[i + 1] for i in range(0, len(terms) - 1, 2)]
        if len(terms) % 2:
            paired.append(terms[-1])
        terms = paired
    return terms[0]


def spread(row):
    return jnp.broadcast_to(row, (SEGS, LANES))


def local_kernel(
    total, q_ref, k_ref, v_ref, rim_ref, filter_ref, decay_ref, residue_ref,
    qf_ref, y_ref, carry_ref, end_ref, shifted, signal,
):
    rows, width = q_ref.shape
    modes = decay_ref.shape[0]
    length = rows // SEGS
    kinds, tap_count, groups = filter_ref.shape
    group_width = pl.num_programs(0) * width // groups
    chan = pl.program_id(0) * width + lax.broadcasted_iota(jnp.int32, (groups, width), 1)
    first = lax.broadcasted_iota(jnp.int32, (groups, width), 0) * group_width
    member = ((chan >= first) & (chan < first + group_width)).astype(BF16)
    taps = [
        jnp.dot(filter_ref[kind], member, preferred_element_type=F32) for kind in range(kinds)
    ]
    lead = LEAD

    def short_pass(which, ref, lanes):
        pad = shifted.at[which]
        pad[SEGS : SEGS + rows, :] = ref[:, lanes].astype(F32)
        pad[SEGS - lead : SEGS, :] = rim_ref[which * lead : (which + 1) * lead, lanes]
        running = None
        for offset in range(tap_count):
            tap = taps[which][offset : offset + 1, lanes]
            term = tap * pad[SEGS - offset : SEGS - offset + rows, :]
            running = term if running is None else running + term
        return running.astype(BF16)

    for block in range(width // LANES):
        lanes = slice(block * LANES, (block + 1) * LANES)
        qf_ref[:, lanes] = short_pass(0, q_ref, lanes)
        k_feat = short_pass(1, k_ref, lanes).astype(F32)
        v_feat = short_pass(2, v_ref, lanes).astype(F32)
        signal[block] = (k_feat * v_feat).astype(BF16).astype(F32)

    seg = lax.broadcasted_iota(jnp.int32, (SEGS, LANES), 0)
    for block in range(width // LANES):
        lanes = slice(block * LANES, (block + 1) * LANES)
        steps = decay_ref[:, lanes] / total
        decays = jnp.exp(-steps)
        scales = residue_ref[:, lanes] * jnp.sqrt(2.0 * steps)
        decay = [spread(decays[m : m + 1]) for m in range(modes)]
        scale = [spread(scales[m : m + 1]) for m in range(modes)]

        def advance(i, state):
            x = signal[block, pl.ds(i, SEGS, stride=length), :]
            state = tuple(d * s + x for d, s in zip(decay, state))
            y_ref[i, :, lanes] = tree_sum(c * s for c, s in zip(scale, state))
            return state

        zero = jnp.zeros((SEGS, LANES), F32)
        state = lax.fori_loop(0, length, advance, (zero,) * modes, unroll=4)
        for m in range(modes):
            ends = state[m]
            for hop in (1, 2, 4):
                factor = spread(jnp.exp(-steps[m : m + 1] * float(length * hop)))
                ends = ends + factor * jnp.where(seg >= hop, pltpu.roll(ends, hop, 0), 0.0)
            end_ref[m : m + 1, lanes] = ends[SEGS - 1 : SEGS]
            carry_ref[m, :, lanes] = jnp.where(seg >= 1, pltpu.roll(ends, 1, 0), 0.0)


def gate_kernel(
    total, seat_ref, qf_ref, y_ref, carry_ref, incoming_ref, decay_ref, residue_ref,
    out_ref, mixed,
):
    rows, width = qf_ref.shape
    modes = decay_ref.shape[0]
    length = rows // SEGS
    begin = (lax.broadcasted_iota(jnp.int32, (SEGS, LANES), 0) * length).astype(F32)
    for block in range(width // LANES):
        lanes = slice(block * LANES, (block + 1) * LANES)
        steps = decay_ref[:, lanes] / total
        decays = jnp.exp(-steps)
        weights = residue_ref[:, lanes] * jnp.sqrt(2.0 * steps) * decays
        decay = [spread(decays[m : m + 1]) for m in range(modes)]
        tail = []
        for m in range(modes):
            reach = jnp.exp(-spread(steps[m : m + 1]) * begin)
            held = carry_ref[m, :, lanes] + reach * spread(incoming_ref[m : m + 1, lanes])
            tail.append(spread(weights[m : m + 1]) * held)

        def advance(i, tail):
            mixed[block, pl.ds(i, SEGS, stride=length), :] = y_ref[i, :, lanes] + tree_sum(tail)
            return tuple(d * s for d, s in zip(decay, tail))

        lax.fori_loop(0, length, advance, tuple(tail), unroll=4)
    for block in range(width // LANES):
        lanes = slice(block * LANES, (block + 1) * LANES)
        out_ref[:, lanes] = (qf_ref[:, lanes].astype(F32) * mixed[block]).astype(BF16)


def column_call(body, name, arrays, outs, scratch, width, chan_count):
    def spec(shape):
        if shape[-1] != chan_count:
            return pl.BlockSpec(shape, lambda c: (0,) * len(shape))
        return pl.BlockSpec(shape[:-1] + (width,), lambda c: (0,) * (len(shape) - 1) + (c,))

    return pl.pallas_call(
        body,
        grid=(chan_count // width,),
        in_specs=[spec(a.shape) for a in arrays],
        out_specs=[spec(o.shape) for o in outs],
        out_shape=outs,
        scratch_shapes=scratch,
        compiler_params=pltpu.CompilerParams(vmem_limit_bytes=VMEM_GRANT),
        name=name,
    )(*arrays)


def local_rows(q_proj, k_proj, v_proj, rims, short_filter, residue, decay_rate):
    rows, chan_count = q_proj.shape
    modes = decay_rate.shape[0]
    total = float(rows * lax.axis_size("context"))
    width = lane_block(chan_count)
    return column_call(
        functools.partial(local_kernel, total), "local_pass",
        (q_proj, k_proj, v_proj, rims, short_filter, decay_rate, residue),
        [
            jax.ShapeDtypeStruct((rows, chan_count), BF16),
            jax.ShapeDtypeStruct((rows // SEGS, SEGS, chan_count), F32),
            jax.ShapeDtypeStruct((modes, SEGS, chan_count), F32),
            jax.ShapeDtypeStruct((modes, chan_count), F32),
        ],
        [
            pltpu.VMEM((3, rows + SEGS, LANES), F32),
            pltpu.VMEM((width // LANES, rows, LANES), F32),
        ],
        width, chan_count,
    )


def gate_rows(q_feat, y_local, carry, incoming, decay_rate, residue, seat):
    rows, chan_count = q_feat.shape
    modes = decay_rate.shape[0]
    total = float(rows * lax.axis_size("context"))
    width = lane_block(chan_count)
    per_part = incoming.shape[2] // width

    def cols(height):
        return pl.BlockSpec((height, width), lambda c, s: (0, c))

    return pl.pallas_call(
        functools.partial(gate_kernel, total),
        grid_spec=pltpu.PrefetchScalarGridSpec(
            num_scalar_prefetch=1,
            grid=(chan_count // width,),
            in_specs=[
                cols(rows),
                pl.BlockSpec((rows // SEGS, SEGS, width), lambda c, s: (0, 0, c)),
                pl.BlockSpec((modes, SEGS, width), lambda c, s: (0, 0, c)),
                pl.BlockSpec(
                    (None, modes, width), lambda c, s: (s[0] ^ (c // per_part), 0, c % per_part)
                ),
                cols(modes),
                cols(modes),
            ],
            out_specs=cols(rows),
            scratch_shapes=[pltpu.VMEM((width // LANES, rows, LANES), F32)],
        ),
        out_shape=jax.ShapeDtypeStruct((rows, chan_count), BF16),
        compiler_params=pltpu.CompilerParams(vmem_limit_bytes=VMEM_GRANT),
        name="gate_pass",
    )(seat.reshape(1), q_feat, y_local, carry, incoming, decay_rate, residue)


def by_seat(seat, blocks):
    ordered = []
    for k in range(CREW):
        value = blocks[0]
        for j in range(1, CREW):
            value = jnp.where((seat ^ k) == j, blocks[j], value)
        ordered.append(value)
    return ordered


def plane_kernel(span, seat_ref, steps_ref, *refs):
    blocks, out_ref = refs[:CREW], refs[CREW]
    reach = jnp.exp(-steps_ref[...] * span)
    ends = by_seat(seat_ref[0], [b[...] for b in blocks])
    state = ends[0]
    for end in ends[1:]:
        state = reach * state + end
    out_ref[...] = state


def incoming_kernel(span, seat_ref, steps_ref, *refs):
    blocks, planes = refs[:CREW], refs[CREW : CREW + PLANES - 1]
    outs = refs[CREW + PLANES - 1 :]
    steps, seat = steps_ref[...], seat_ref[0]
    ends = by_seat(seat, [b[...] for b in blocks])
    reach, reach_plane = jnp.exp(-steps * span), jnp.exp(-steps * (span * CREW))
    state = planes[-1][...]
    for plane in planes[-2::-1]:
        state = reach_plane * state + plane[...]
    states = [state]
    for end in ends[:-1]:
        states.append(reach * states[-1] + end)
    for out_ref, value in zip(outs, by_seat(seat, states)):
        out_ref[...] = value


def state_call(body, name, seat, steps, ends, arrays, out_count):
    modes, quarter = arrays[0].shape

    def owned(_, s):
        return (0, s[0])

    own = pl.BlockSpec((modes, quarter), owned)
    whole = pl.BlockSpec((modes, quarter), lambda _, s: (0, 0))
    shape = jax.ShapeDtypeStruct((modes, quarter), F32)
    return pl.pallas_call(
        body,
        grid_spec=pltpu.PrefetchScalarGridSpec(
            num_scalar_prefetch=1,
            grid=(1,),
            in_specs=[own, own] + [whole] * len(arrays),
            out_specs=[whole] * out_count,
        ),
        out_shape=[shape] * out_count,
        name=name,
    )(seat.reshape(1), steps, ends, *arrays)


def product_kernel(sizes, counts, token_count, flipped, pick_ref, *refs):
    refs = list(refs)
    weights = [[refs.pop(0) for _ in range(count)] for count in counts]
    tokens = [refs.pop(0) for _ in range(token_count)]
    outs, (total, joined) = refs[:-2], refs[-2:]
    step = pl.program_id(0)

    @pl.when(step == 0)
    def _():
        total[...] = jnp.zeros_like(total)

    begin = 0
    for at, (size, choices) in enumerate(zip(sizes, weights)):
        for choice, source in enumerate(choices):

            @pl.when(pick_ref[at] == choice)
            def _():
                joined[begin : begin + size, :] = source[...]

        begin += size
    for j, token in enumerate(tokens):
        left, right = (token, joined) if flipped else (joined, token)
        total[j] += lax.dot_general(
            left[...], right[...], (((1,), (1,)), ((), ())), preferred_element_type=F32
        )

    @pl.when(step == pl.num_programs(0) - 1)
    def _():
        if flipped:
            for j in range(len(tokens)):
                outs[0][j] = jnp.transpose(total[j]).astype(BF16)
            return
        begin = 0
        for out_ref in outs:
            out_ref[...] = total[:, begin : begin + out_ref.shape[1], :].astype(BF16)
            begin += out_ref.shape[1]


def project(slots, picks, tokens, out_sizes, flipped=False):
    rows, depth = tokens[0].shape
    width = 1024 if depth % 1024 == 0 else LANES

    def columns(size):
        return pl.BlockSpec((size, width), lambda c, _: (0, c))

    sizes = [choices[0].shape[0] for choices in slots]
    flat = [array for choices in slots for array in choices]
    flat += tokens
    specs = [columns(array.shape[0]) for array in flat]
    feat = sum(sizes)
    shapes = [(len(tokens), size, rows) for size in out_sizes]
    return pl.pallas_call(
        functools.partial(
            product_kernel,
            sizes,
            [len(choices) for choices in slots],
            len(tokens),
            flipped,
        ),
        grid_spec=pltpu.PrefetchScalarGridSpec(
            num_scalar_prefetch=1,
            grid=(depth // width,),
            in_specs=specs,
            out_specs=[pl.BlockSpec(shape, lambda c, _: (0, 0, 0)) for shape in shapes],
            scratch_shapes=[
                pltpu.VMEM((len(tokens),) + ((rows, feat) if flipped else (feat, rows)), F32),
                pltpu.VMEM((feat, width), BF16),
            ],
        ),
        out_shape=[jax.ShapeDtypeStruct(shape, BF16) for shape in shapes],
        compiler_params=pltpu.CompilerParams(vmem_limit_bytes=VMEM_GRANT),
        cost_estimate=pl.CostEstimate(flops=1, bytes_accessed=1, transcendentals=0),
        name="project",
    )(jnp.stack(picks).astype(jnp.int32), *flat)


def assemble_kernel(place_ref, *refs):
    early, late, last = (refs[i * CREW : (i + 1) * CREW] for i in range(3))
    out_ref = refs[-1]
    feat, part = early[0].shape[0] // 2, last[0].shape[0]
    cut, half = feat - part, out_ref.shape[0] // 2
    same, low, seat = place_ref[0], place_ref[1], place_ref[2]
    for j in range(CREW):
        within = (seat ^ j) * feat
        first = pl.multiple_of(low * half + within, feat)
        second = pl.multiple_of((1 - low) * half + within, feat)

        @pl.when(same == 1)
        def _():
            out_ref[pl.ds(first, feat), :] = early[j][:feat, :]
            out_ref[pl.ds(second, feat), :] = early[j][feat:, :]

        @pl.when(same == 0)
        def _():
            out_ref[pl.ds(first, feat), :] = jnp.concatenate(
                [early[j][:cut, :], late[j][:part, :]], axis=0
            )
            out_ref[pl.ds(second, feat), :] = jnp.concatenate(
                [late[j][part:, :], last[j][...]], axis=0
            )


def assemble(place, early, late, last):
    rows = early[0].shape[1]
    vmem = pl.BlockSpec(memory_space=pltpu.VMEM)
    return pl.pallas_call(
        assemble_kernel,
        in_specs=[pl.BlockSpec(memory_space=pltpu.SMEM)] + [vmem] * (3 * CREW),
        out_specs=vmem,
        out_shape=jax.ShapeDtypeStruct((CREW * early[0].shape[0], rows), BF16),
        compiler_params=pltpu.CompilerParams(vmem_limit_bytes=VMEM_GRANT),
        name="assemble",
    )(place, *early, *late, *last)


def tails_kernel(q_ref, k_ref, v_ref, out_ref):
    lead = LEAD
    for which, ref in enumerate((q_ref, k_ref, v_ref)):
        rows = ref[...].astype(F32)
        out_ref[which * lead : (which + 1) * lead, :] = rows[rows.shape[0] - lead :]
    out_ref[3 * lead :, :] = jnp.zeros((out_ref.shape[0] - 3 * lead, out_ref.shape[1]), F32)


def gather_rims(q_proj, k_proj, v_proj):
    size = lax.axis_size("context")
    rows, chan_count = q_proj.shape
    last = pl.BlockSpec((16, chan_count), lambda i: (rows // 16 - 1, 0))
    tails = pl.pallas_call(
        tails_kernel,
        grid=(1,),
        in_specs=[last] * 3,
        out_specs=pl.BlockSpec((SEGS, chan_count), lambda i: (0, 0)),
        out_shape=jax.ShapeDtypeStruct((SEGS, chan_count), F32),
        compiler_params=pltpu.CompilerParams(vmem_limit_bytes=VMEM_GRANT),
        name="tails",
    )(q_proj, k_proj, v_proj)
    return lax.ppermute(tails, "context", [(i, i + 1) for i in range(size - 1)])


def per_device(q_proj, k_proj, v_proj, short_filter, residue, decay_rate, out_weight):
    place, size = lax.axis_index("context"), lax.axis_size("context")

    rows = q_proj.shape[0]
    rims = gather_rims(q_proj, k_proj, v_proj)
    q_feat, y_local, carry, ends = local_rows(
        q_proj, k_proj, v_proj, rims, short_filter, residue, decay_rate
    )
    gathered = lax.all_gather(ends, "context")
    gaps = (place - 1 - jnp.arange(size))[:, None, None]
    reach = jnp.exp(-(decay_rate / float(rows * size))[None] * (gaps * rows).astype(F32))
    incoming = jnp.sum(jnp.where(gaps >= 0, reach * gathered, 0.0), axis=0)
    gated = gate_rows(
        q_feat, y_local, carry, incoming[None], decay_rate, residue, jnp.int32(0)
    )
    partial_terms = lax.dot_general(
        lax.all_gather(out_weight, "context", axis=0, tiled=True),
        gated,
        (((1,), (1,)), ((), ())),
        preferred_element_type=F32,
    )
    return lax.psum_scatter(
        partial_terms.astype(BF16), "tensor", scatter_dimension=0, tiled=True
    )


def swap(block, mask):
    size = lax.axis_size("context")
    return lax.ppermute(block, "context", [(i, i ^ mask) for i in range(size)])


def shift(block, distance):
    size = lax.axis_size("context")
    moves = [(i, i + distance) for i in range(size) if 0 <= i + distance < size]
    return lax.ppermute(block, "context", moves)


def per_device_planes(q_proj, k_proj, v_proj, short_filter, residue, decay_rate, out_weight):
    size = lax.axis_size("context")
    place, side = lax.axis_index("context"), lax.axis_index("tensor")
    plane, seat = place // CREW, place % CREW
    low = plane % 2
    same = (side == plane // 2).astype(jnp.int32)
    rows, feat = q_proj.shape[0], out_weight.shape[0]
    quarter = q_proj.shape[1] // CREW
    span = float(rows)
    steps = decay_rate / (span * size)

    def hops(block, moves):
        return lax.ppermute(
            block, "context",
            [(a * CREW + s, b * CREW + s) for a, b in moves for s in range(CREW)],
        )

    def over_tensor(block, to_same):
        moves = []
        for i in range(size):
            half = i // CREW * 2 // PLANES
            keeper = half if to_same else 1 - half
            moves.append(((1 - keeper) * size + i, keeper * size + i))
        return lax.ppermute(block, ("tensor", "context"), moves)

    def deal(block, mask):
        moves = []
        for i in range(size):
            keeper = 1 - i // CREW * 2 // PLANES
            moves.append((keeper * size + i, keeper * size + (i ^ mask)))
        return lax.ppermute(block, ("tensor", "context"), moves)

    def added(kept, arrived):
        return (kept.astype(F32) + arrived.astype(F32)).astype(BF16)

    cut = feat * 11 // 16
    own = [out_weight[:cut], out_weight[cut:]]
    rims = gather_rims(q_proj, k_proj, v_proj)
    rims, own[0] = lax.optimization_barrier((rims, own[0]))
    up1, down1 = [shift(own[0], CREW)], [shift(own[0], -CREW)]
    q_feat, y_local, carry, ends = local_rows(
        q_proj, k_proj, v_proj, rims, short_filter, residue, decay_rate
    )
    ends, up1, down1 = lax.optimization_barrier((ends, up1, down1))
    blocks = [
        swap(lax.dynamic_slice_in_dim(ends, (seat ^ j) * quarter, quarter, 1), j)
        for j in range(1, CREW)
    ]
    total = state_call(
        functools.partial(plane_kernel, span), "plane_state", seat, steps, ends, blocks, 1
    )[0]
    planes = [shift(total, hop * CREW) for hop in range(1, PLANES)]
    planes, own[1] = lax.optimization_barrier((planes, own[1]))
    up1.append(shift(own[1], CREW))
    down1.append(shift(own[1], -CREW))

    def finish_gate(ends, steps, blocks, planes, q_feat, y_local, carry, decay_rate, residue):
        mine = state_call(
            functools.partial(incoming_kernel, span), "incoming_state",
            seat, steps, ends, blocks + planes, CREW,
        )
        incoming = jnp.stack([mine[0]] + [swap(mine[j], j) for j in range(1, CREW)])
        return gate_rows(q_feat, y_local, carry, incoming, decay_rate, residue, seat)

    gated = lax.cond(
        place < size,
        finish_gate,
        lambda *_: jnp.zeros_like(q_proj),
        ends, steps, blocks, planes, q_feat, y_local, carry, decay_rate, residue,
    )
    gated, up1, down1 = lax.optimization_barrier((gated, up1, down1))
    up2 = [hops(part, [(1, 2), (2, 3)]) for part in up1]
    down2 = [hops(part, [(2, 1), (1, 0)]) for part in down1]
    beyond = swap(gated, 2)
    zero = jnp.int32(0)
    far = (plane >= 2).astype(jnp.int32)
    near_slots = [[out_weight]] + [list(pair) for pair in zip(down1, up1)]
    near_picks = [zero, low, low]

    def combined(near, near_arrived, third, third_arrived, j):
        near_sum, third_sum = added(near[j], near_arrived[j]), added(third[j], third_arrived[j])
        first = jnp.where(same == 1, near_sum[:cut], third_sum)
        return jnp.concatenate([first, near_sum[cut:]], axis=0)

    def start_early(*tokens):
        near = project(near_slots, near_picks, list(tokens), [2 * feat])[0]
        return near, over_tensor(near, True)

    def no_early(*tokens):
        return (jnp.zeros((2, 2 * feat, rows), BF16),) * 2

    tokens = [gated, swap(gated, 1)]
    early_near, up2[0], down2[0] = lax.optimization_barrier(
        (lax.cond(place < size, start_early, no_early, *tokens), up2[0], down2[0])
    )
    up3, down3 = [hops(up2[0], [(2, 3)])], [hops(down2[0], [(1, 0)])]
    early_near, beyond = lax.optimization_barrier((early_near, beyond))
    third_slots = [[down2[0], up2[0]]]

    def start_beyond(beyond):
        tokens = [beyond, swap(beyond, 1)]
        near, third = project(
            near_slots + third_slots, near_picks + [far], tokens, [2 * feat, cut]
        )
        return near, third, tokens[1]

    def no_beyond(beyond):
        return jnp.zeros((2, 2 * feat, rows), BF16), jnp.zeros((2, cut, rows), BF16), beyond

    near, third, last_token = lax.cond(place < size, start_beyond, no_beyond, beyond)
    tokens += [beyond, last_token]
    near_arrived, third_arrived = over_tensor(near, True), over_tensor(third, False)
    near, up2[1], down2[1] = lax.optimization_barrier((near, up2[1], down2[1]))
    third_slots.append([down2[1], up2[1]])
    up3.append(hops(up2[1], [(2, 3)]))
    down3.append(hops(down2[1], [(1, 0)]))
    near, tokens[0] = lax.optimization_barrier((near, tokens[0]))
    early_third = project(third_slots[:1], [far], tokens[:2], [cut])[0]
    early_arrived = over_tensor(early_third, False)

    def finish_late(slots, picks):
        count = sum(choices[0].shape[0] for choices in slots)
        partial_terms = project(slots, picks, tokens, [count], flipped=True)[0]
        return partial_terms, over_tensor(partial_terms, False)

    fourth_slots = [list(choices) for choices in zip(down3, down1, up1, up3)]
    early_third, fourth_slots[0] = lax.optimization_barrier((early_third, fourth_slots[0]))
    late, late_arrived = finish_late([third_slots[1], fourth_slots[0]], [far, plane])
    late, fourth_slots[1] = lax.optimization_barrier((late, fourth_slots[1]))
    last, last_arrived = finish_late(fourth_slots[1:], [plane])
    last, near_arrived, third_arrived = lax.optimization_barrier(
        (last, near_arrived, third_arrived)
    )
    early = [combined(*early_near, early_third, early_arrived, j) for j in range(2)]
    early += [combined(near, near_arrived, third, third_arrived, j) for j in range(2)]
    early = [early[0]] + [swap(early[j], j) for j in range(1, CREW)]
    late = [added(late[j], late_arrived[j]) for j in range(CREW)]
    late = [late[0]] + [deal(late[j], j) for j in range(1, CREW)]
    last = [added(last[j], last_arrived[j]) for j in range(CREW)]
    last = [last[0]] + [deal(last[j], j) for j in range(1, CREW)]
    where = jnp.stack([same, low, seat]).astype(jnp.int32)
    return assemble(where, early, late, last)


def solution(mesh):
    planes = mesh.shape["tensor"] == 2 and mesh.shape["context"] == CREW * PLANES
    return jax.shard_map(
        per_device_planes if planes else per_device,
        mesh=mesh,
        in_specs=(
            P("context", "tensor"),
            P("context", "tensor"),
            P("context", "tensor"),
            P(None, None, "tensor"),
            P(None, "tensor"),
            P(None, "tensor"),
            P("context", "tensor"),
        ),
        out_specs=P("tensor", "context"),
        check_vma=False,
    )
```

```python
import functools
import math

import jax
import jax.numpy as jnp
from jax import lax
from jax.experimental import pallas as pl
from jax.experimental.pallas import tpu as pltpu
from jax.sharding import PartitionSpec as P

LANES = 128
SEGS = 8
CREW = 4
LEAD = 2
PLANES = 4
VMEM_GRANT = 56 * 2**20
F32 = jnp.float32
BF16 = jnp.bfloat16


def lane_block(chan_count):
    for width in (1024, 512):
        if chan_count % (CREW * width) == 0:
            return width
    return LANES


def tree_sum(terms):
    terms = list(terms)
    while len(terms) > 1:
        paired = [terms[i] + terms[i + 1] for i in range(0, len(terms) - 1, 2)]
        if len(terms) % 2:
            paired.append(terms[-1])
        terms = paired
    return terms[0]


def spread(row):
    return jnp.broadcast_to(row, (SEGS, LANES))


def local_kernel(
    total, q_ref, k_ref, v_ref, rim_ref, filter_ref, decay_ref, residue_ref,
    qf_ref, y_ref, carry_ref, end_ref, shifted, signal,
):
    rows, width = q_ref.shape
    modes = decay_ref.shape[0]
    length = rows // SEGS
    kinds, tap_count, groups = filter_ref.shape
    group_width = pl.num_programs(0) * width // groups
    chan = pl.program_id(0) * width + lax.broadcasted_iota(jnp.int32, (groups, width), 1)
    first = lax.broadcasted_iota(jnp.int32, (groups, width), 0) * group_width
    member = ((chan >= first) & (chan < first + group_width)).astype(BF16)
    taps = [
        jnp.dot(filter_ref[kind], member, preferred_element_type=F32) for kind in range(kinds)
    ]
    lead = LEAD

    def short_pass(which, ref, lanes):
        pad = shifted.at[which]
        pad[SEGS : SEGS + rows, :] = ref[:, lanes].astype(F32)
        pad[SEGS - lead : SEGS, :] = rim_ref[which * lead : (which + 1) * lead, lanes]
        running = None
        for offset in range(tap_count):
            tap = taps[which][offset : offset + 1, lanes]
            term = tap * pad[SEGS - offset : SEGS - offset + rows, :]
            running = term if running is None else running + term
        return running.astype(BF16)

    for block in range(width // LANES):
        lanes = slice(block * LANES, (block + 1) * LANES)
        qf_ref[:, lanes] = short_pass(0, q_ref, lanes)
        k_feat = short_pass(1, k_ref, lanes).astype(F32)
        v_feat = short_pass(2, v_ref, lanes).astype(F32)
        signal[block] = (k_feat * v_feat).astype(BF16).astype(F32)

    seg = lax.broadcasted_iota(jnp.int32, (SEGS, LANES), 0)
    for block in range(width // LANES):
        lanes = slice(block * LANES, (block + 1) * LANES)
        steps = decay_ref[:, lanes] / total
        decays = jnp.exp(-steps)
        scales = residue_ref[:, lanes] * jnp.sqrt(2.0 * steps)
        decay = [spread(decays[m : m + 1]) for m in range(modes)]
        scale = [spread(scales[m : m + 1]) for m in range(modes)]

        def advance(i, state):
            x = signal[block, pl.ds(i, SEGS, stride=length), :]
            state = tuple(d * s + x for d, s in zip(decay, state))
            y_ref[i, :, lanes] = tree_sum(c * s for c, s in zip(scale, state))
            return state

        zero = jnp.zeros((SEGS, LANES), F32)
        state = lax.fori_loop(0, length, advance, (zero,) * modes, unroll=4)
        for m in range(modes):
            ends = state[m]
            for hop in (1, 2, 4):
                factor = spread(jnp.exp(-steps[m : m + 1] * float(length * hop)))
                ends = ends + factor * jnp.where(seg >= hop, pltpu.roll(ends, hop, 0), 0.0)
            end_ref[m : m + 1, lanes] = ends[SEGS - 1 : SEGS]
            carry_ref[m, :, lanes] = jnp.where(seg >= 1, pltpu.roll(ends, 1, 0), 0.0)


def gate_kernel(
    total, seat_ref, qf_ref, y_ref, carry_ref, incoming_ref, decay_ref, residue_ref,
    out_ref, mixed,
):
    rows, width = qf_ref.shape
    modes = decay_ref.shape[0]
    length = rows // SEGS
    begin = (lax.broadcasted_iota(jnp.int32, (SEGS, LANES), 0) * length).astype(F32)
    for block in range(width // LANES):
        lanes = slice(block * LANES, (block + 1) * LANES)
        steps = decay_ref[:, lanes] / total
        decays = jnp.exp(-steps)
        weights = residue_ref[:, lanes] * jnp.sqrt(2.0 * steps) * decays
        decay = [spread(decays[m : m + 1]) for m in range(modes)]
        tail = []
        for m in range(modes):
            reach = jnp.exp(-spread(steps[m : m + 1]) * begin)
            held = carry_ref[m, :, lanes] + reach * spread(incoming_ref[m : m + 1, lanes])
            tail.append(spread(weights[m : m + 1]) * held)

        def advance(i, tail):
            mixed[block, pl.ds(i, SEGS, stride=length), :] = y_ref[i, :, lanes] + tree_sum(tail)
            return tuple(d * s for d, s in zip(decay, tail))

        lax.fori_loop(0, length, advance, tuple(tail), unroll=4)
    for block in range(width // LANES):
        lanes = slice(block * LANES, (block + 1) * LANES)
        out_ref[:, lanes] = (qf_ref[:, lanes].astype(F32) * mixed[block]).astype(BF16)


def column_call(body, name, arrays, outs, scratch, width, chan_count):
    def spec(shape):
        if shape[-1] != chan_count:
            return pl.BlockSpec(shape, lambda c: (0,) * len(shape))
        return pl.BlockSpec(shape[:-1] + (width,), lambda c: (0,) * (len(shape) - 1) + (c,))

    return pl.pallas_call(
        body,
        grid=(chan_count // width,),
        in_specs=[spec(a.shape) for a in arrays],
        out_specs=[spec(o.shape) for o in outs],
        out_shape=outs,
        scratch_shapes=scratch,
        compiler_params=pltpu.CompilerParams(vmem_limit_bytes=VMEM_GRANT),
        name=name,
    )(*arrays)


def local_rows(q_proj, k_proj, v_proj, rims, short_filter, residue, decay_rate):
    rows, chan_count = q_proj.shape
    modes = decay_rate.shape[0]
    total = float(rows * lax.axis_size("context"))
    width = lane_block(chan_count)
    return column_call(
        functools.partial(local_kernel, total), "local_pass",
        (q_proj, k_proj, v_proj, rims, short_filter, decay_rate, residue),
        [
            jax.ShapeDtypeStruct((rows, chan_count), BF16),
            jax.ShapeDtypeStruct((rows // SEGS, SEGS, chan_count), F32),
            jax.ShapeDtypeStruct((modes, SEGS, chan_count), F32),
            jax.ShapeDtypeStruct((modes, chan_count), F32),
        ],
        [
            pltpu.VMEM((3, rows + SEGS, LANES), F32),
            pltpu.VMEM((width // LANES, rows, LANES), F32),
        ],
        width, chan_count,
    )


def gate_rows(q_feat, y_local, carry, incoming, decay_rate, residue, seat):
    rows, chan_count = q_feat.shape
    modes = decay_rate.shape[0]
    total = float(rows * lax.axis_size("context"))
    width = lane_block(chan_count)
    per_part = incoming.shape[2] // width

    def cols(height):
        return pl.BlockSpec((height, width), lambda c, s: (0, c))

    return pl.pallas_call(
        functools.partial(gate_kernel, total),
        grid_spec=pltpu.PrefetchScalarGridSpec(
            num_scalar_prefetch=1,
            grid=(chan_count // width,),
            in_specs=[
                cols(rows),
                pl.BlockSpec((rows // SEGS, SEGS, width), lambda c, s: (0, 0, c)),
                pl.BlockSpec((modes, SEGS, width), lambda c, s: (0, 0, c)),
                pl.BlockSpec(
                    (None, modes, width), lambda c, s: (s[0] ^ (c // per_part), 0, c % per_part)
                ),
                cols(modes),
                cols(modes),
            ],
            out_specs=cols(rows),
            scratch_shapes=[pltpu.VMEM((width // LANES, rows, LANES), F32)],
        ),
        out_shape=jax.ShapeDtypeStruct((rows, chan_count), BF16),
        compiler_params=pltpu.CompilerParams(vmem_limit_bytes=VMEM_GRANT),
        name="gate_pass",
    )(seat.reshape(1), q_feat, y_local, carry, incoming, decay_rate, residue)


def by_seat(seat, blocks):
    ordered = []
    for k in range(CREW):
        value = blocks[0]
        for j in range(1, CREW):
            value = jnp.where((seat ^ k) == j, blocks[j], value)
        ordered.append(value)
    return ordered


def plane_kernel(span, seat_ref, steps_ref, *refs):
    blocks, out_ref = refs[:CREW], refs[CREW]
    reach = jnp.exp(-steps_ref[...] * span)
    ends = by_seat(seat_ref[0], [b[...] for b in blocks])
    state = ends[0]
    for end in ends[1:]:
        state = reach * state + end
    out_ref[...] = state


def incoming_kernel(span, seat_ref, steps_ref, *refs):
    blocks, planes = refs[:CREW], refs[CREW : CREW + PLANES - 1]
    outs = refs[CREW + PLANES - 1 :]
    steps, seat = steps_ref[...], seat_ref[0]
    ends = by_seat(seat, [b[...] for b in blocks])
    reach, reach_plane = jnp.exp(-steps * span), jnp.exp(-steps * (span * CREW))
    state = planes[-1][...]
    for plane in planes[-2::-1]:
        state = reach_plane * state + plane[...]
    states = [state]
    for end in ends[:-1]:
        states.append(reach * states[-1] + end)
    for out_ref, value in zip(outs, by_seat(seat, states)):
        out_ref[...] = value


def state_call(body, name, seat, steps, ends, arrays, out_count):
    modes, quarter = arrays[0].shape

    def owned(_, s):
        return (0, s[0])

    own = pl.BlockSpec((modes, quarter), owned)
    whole = pl.BlockSpec((modes, quarter), lambda _, s: (0, 0))
    shape = jax.ShapeDtypeStruct((modes, quarter), F32)
    return pl.pallas_call(
        body,
        grid_spec=pltpu.PrefetchScalarGridSpec(
            num_scalar_prefetch=1,
            grid=(1,),
            in_specs=[own, own] + [whole] * len(arrays),
            out_specs=[whole] * out_count,
        ),
        out_shape=[shape] * out_count,
        name=name,
    )(seat.reshape(1), steps, ends, *arrays)


def product_kernel(token_count, side_ref, weight_ref, *refs):
    tokens, (kept_ref, sent_ref, total) = refs[:token_count], refs[token_count:]
    planes, feat, width = weight_ref.shape
    step = pl.program_id(0)

    @pl.when(step == 0)
    def _():
        total[...] = jnp.zeros_like(total)

    weights = weight_ref[...].reshape(planes * feat, width)
    for j, token in enumerate(tokens):
        total[j] += lax.dot_general(
            weights, token[...], (((1,), (1,)), ((), ())), preferred_element_type=F32
        )

    @pl.when(step == pl.num_programs(0) - 1)
    def _():
        middle = total.shape[1] // 2
        for side, outs in ((0, (kept_ref, sent_ref)), (1, (sent_ref, kept_ref))):

            @pl.when(side_ref[0] == side)
            def _():
                outs[0][...] = total[:, :middle, :].astype(BF16)
                outs[1][...] = total[:, middle:, :].astype(BF16)


def project(weights, tokens, side):
    rows, depth = tokens[0].shape
    planes, feat, _ = weights.shape
    width = 1024 if depth % 1024 == 0 else LANES
    shape = (len(tokens), planes * feat // 2, rows)
    return pl.pallas_call(
        functools.partial(product_kernel, len(tokens)),
        grid_spec=pltpu.PrefetchScalarGridSpec(
            num_scalar_prefetch=1,
            grid=(depth // width,),
            in_specs=[pl.BlockSpec((planes, feat, width), lambda c, _: (0, 0, c))]
            + [pl.BlockSpec((rows, width), lambda c, _: (0, c)) for _ in tokens],
            out_specs=[pl.BlockSpec(shape, lambda c, _: (0, 0, 0))] * 2,
            scratch_shapes=[pltpu.VMEM((len(tokens), planes * feat, rows), F32)],
        ),
        out_shape=[jax.ShapeDtypeStruct(shape, BF16)] * 2,
        compiler_params=pltpu.CompilerParams(vmem_limit_bytes=VMEM_GRANT),
        cost_estimate=pl.CostEstimate(flops=1, bytes_accessed=1, transcendentals=0),
        name="project",
    )(side.reshape(1), weights, *tokens)


def assemble_kernel(seat_ref, *refs):
    pieces, out_ref = refs[:-1], refs[-1]
    halves = PLANES // 2
    block = out_ref.shape[0] // halves
    feat = block // CREW
    for j in range(CREW):
        begin = 0
        for piece in pieces[j::CREW]:
            size = piece.shape[0] // halves
            for half in range(halves):
                at = half * block + (seat_ref[0] ^ j) * feat + begin
                at = pl.multiple_of(at, math.gcd(size, begin) if begin else size)
                out_ref[pl.ds(at, size), :] = piece[half * size : (half + 1) * size, :]
            begin += size


def assemble(seat, pieces):
    rows = pieces[0].shape[1]
    vmem = pl.BlockSpec(memory_space=pltpu.VMEM)
    return pl.pallas_call(
        assemble_kernel,
        in_specs=[pl.BlockSpec(memory_space=pltpu.SMEM)] + [vmem] * len(pieces),
        out_specs=vmem,
        out_shape=jax.ShapeDtypeStruct((sum(p.shape[0] for p in pieces), rows), BF16),
        compiler_params=pltpu.CompilerParams(vmem_limit_bytes=VMEM_GRANT),
        name="assemble",
    )(seat.reshape(1), *pieces)


def tails_kernel(q_ref, k_ref, v_ref, out_ref):
    lead = LEAD
    for which, ref in enumerate((q_ref, k_ref, v_ref)):
        rows = ref[...].astype(F32)
        out_ref[which * lead : (which + 1) * lead, :] = rows[rows.shape[0] - lead :]
    out_ref[3 * lead :, :] = jnp.zeros((out_ref.shape[0] - 3 * lead, out_ref.shape[1]), F32)


def gather_rims(q_proj, k_proj, v_proj):
    size = lax.axis_size("context")
    rows, chan_count = q_proj.shape
    last = pl.BlockSpec((16, chan_count), lambda i: (rows // 16 - 1, 0))
    tails = pl.pallas_call(
        tails_kernel,
        grid=(1,),
        in_specs=[last] * 3,
        out_specs=pl.BlockSpec((SEGS, chan_count), lambda i: (0, 0)),
        out_shape=jax.ShapeDtypeStruct((SEGS, chan_count), F32),
        compiler_params=pltpu.CompilerParams(vmem_limit_bytes=VMEM_GRANT),
        name="tails",
    )(q_proj, k_proj, v_proj)
    return lax.ppermute(tails, "context", [(i, i + 1) for i in range(size - 1)])


def per_device(q_proj, k_proj, v_proj, short_filter, residue, decay_rate, out_weight):
    place, size = lax.axis_index("context"), lax.axis_size("context")

    rows = q_proj.shape[0]
    rims = gather_rims(q_proj, k_proj, v_proj)
    q_feat, y_local, carry, ends = local_rows(
        q_proj, k_proj, v_proj, rims, short_filter, residue, decay_rate
    )
    gathered = lax.all_gather(ends, "context")
    gaps = (place - 1 - jnp.arange(size))[:, None, None]
    reach = jnp.exp(-(decay_rate / float(rows * size))[None] * (gaps * rows).astype(F32))
    incoming = jnp.sum(jnp.where(gaps >= 0, reach * gathered, 0.0), axis=0)
    gated = gate_rows(
        q_feat, y_local, carry, incoming[None], decay_rate, residue, jnp.int32(0)
    )
    partial_terms = lax.dot_general(
        lax.all_gather(out_weight, "context", axis=0, tiled=True),
        gated,
        (((1,), (1,)), ((), ())),
        preferred_element_type=F32,
    )
    return lax.psum_scatter(
        partial_terms.astype(BF16), "tensor", scatter_dimension=0, tiled=True
    )


def swap(block, mask):
    size = lax.axis_size("context")
    return lax.ppermute(block, "context", [(i, i ^ mask) for i in range(size)])


def shift(block, distance):
    size = lax.axis_size("context")
    moves = [(i, i + distance) for i in range(size) if 0 <= i + distance < size]
    return lax.ppermute(block, "context", moves)


def per_device_planes(q_proj, k_proj, v_proj, short_filter, residue, decay_rate, out_weight):
    size = lax.axis_size("context")
    seat = lax.axis_index("context") % CREW
    side = lax.axis_index("tensor")
    rows, feat = q_proj.shape[0], out_weight.shape[0]
    quarter = q_proj.shape[1] // CREW
    span = float(rows)
    steps = decay_rate / (span * size)
    columns = [[p * CREW + s for p in range(PLANES)] for s in range(CREW)]
    cut = feat * 3 // 4
    weights = [
        lax.all_gather(part, "context", axis_index_groups=columns)
        for part in (out_weight[:cut], out_weight[cut:])
    ]

    rims = gather_rims(q_proj, k_proj, v_proj)
    q_feat, y_local, carry, ends = local_rows(
        q_proj, k_proj, v_proj, rims, short_filter, residue, decay_rate
    )
    blocks = [
        swap(lax.dynamic_slice_in_dim(ends, (seat ^ j) * quarter, quarter, 1), j)
        for j in range(1, CREW)
    ]
    total = state_call(
        functools.partial(plane_kernel, span), "plane_state", seat, steps, ends, blocks, 1
    )[0]
    planes = [shift(total, hop * CREW) for hop in range(1, PLANES)]
    mine = state_call(
        functools.partial(incoming_kernel, span), "incoming_state",
        seat, steps, ends, blocks + planes, CREW,
    )
    incoming = jnp.stack([mine[0]] + [swap(mine[j], j) for j in range(1, CREW)])
    gated = gate_rows(q_feat, y_local, carry, incoming, decay_rate, residue, seat)
    tokens = [gated, swap(gated, 1), swap(gated, 2)]
    tokens.append(swap(tokens[2], 1))

    def finish(weights, members):
        kept, sent = project(weights, [tokens[j] for j in members], side)
        arrived = lax.ppermute(sent, "tensor", [(0, 1), (1, 0)])
        sums = [
            (kept[at].astype(F32) + arrived[at].astype(F32)).astype(BF16)
            for at in range(len(members))
        ]
        return [swap(part, j) if j else part for part, j in zip(sums, members)]

    pieces = finish(weights[0], (0, 1)) + finish(weights[0], (2, 3))
    pieces += finish(weights[1], (0, 1, 2, 3))
    return assemble(seat, pieces)


def solution(mesh):
    planes = mesh.shape["tensor"] == 2 and mesh.shape["context"] == CREW * PLANES
    return jax.shard_map(
        per_device_planes if planes else per_device,
        mesh=mesh,
        in_specs=(
            P("context", "tensor"),
            P("context", "tensor"),
            P("context", "tensor"),
            P(None, None, "tensor"),
            P(None, "tensor"),
            P(None, "tensor"),
            P("context", "tensor"),
        ),
        out_specs=P("tensor", "context"),
        check_vma=False,
    )
```

```python
import functools

import jax
import jax.numpy as jnp
from jax import lax
from jax.experimental import pallas as pl
from jax.experimental.pallas import tpu as pltpu
from jax.sharding import PartitionSpec as P

LANES = 128
SEGS = 8
CREW = 4
LEAD = 2
PLANES = 4
NEAR = (0, 1)
FAR = (4, 5)
VMEM_GRANT = 56 * 2**20
F32 = jnp.float32
BF16 = jnp.bfloat16


def lane_block(chan_count):
    for width in (1024, 512):
        if chan_count % (CREW * width) == 0:
            return width
    return LANES


def tree_sum(terms):
    terms = list(terms)
    while len(terms) > 1:
        paired = [terms[i] + terms[i + 1] for i in range(0, len(terms) - 1, 2)]
        if len(terms) % 2:
            paired.append(terms[-1])
        terms = paired
    return terms[0]


def spread(row):
    return jnp.broadcast_to(row, (SEGS, LANES))


def local_kernel(
    total, q_ref, k_ref, v_ref, rim_ref, filter_ref, decay_ref, residue_ref,
    qf_ref, y_ref, carry_ref, end_ref, shifted, signal,
):
    rows, width = q_ref.shape
    modes = decay_ref.shape[0]
    length = rows // SEGS
    kinds, tap_count, groups = filter_ref.shape
    group_width = pl.num_programs(0) * width // groups
    chan = pl.program_id(0) * width + lax.broadcasted_iota(jnp.int32, (groups, width), 1)
    first = lax.broadcasted_iota(jnp.int32, (groups, width), 0) * group_width
    member = ((chan >= first) & (chan < first + group_width)).astype(BF16)
    taps = [
        jnp.dot(filter_ref[kind], member, preferred_element_type=F32) for kind in range(kinds)
    ]
    lead = LEAD

    def short_pass(which, ref, lanes):
        pad = shifted.at[which]
        pad[SEGS : SEGS + rows, :] = ref[:, lanes].astype(F32)
        pad[SEGS - lead : SEGS, :] = rim_ref[which * lead : (which + 1) * lead, lanes]
        running = None
        for offset in range(tap_count):
            tap = taps[which][offset : offset + 1, lanes]
            term = tap * pad[SEGS - offset : SEGS - offset + rows, :]
            running = term if running is None else running + term
        return running.astype(BF16)

    for block in range(width // LANES):
        lanes = slice(block * LANES, (block + 1) * LANES)
        qf_ref[:, lanes] = short_pass(0, q_ref, lanes)
        k_feat = short_pass(1, k_ref, lanes).astype(F32)
        v_feat = short_pass(2, v_ref, lanes).astype(F32)
        signal[block] = (k_feat * v_feat).astype(BF16).astype(F32)

    seg = lax.broadcasted_iota(jnp.int32, (SEGS, LANES), 0)
    for block in range(width // LANES):
        lanes = slice(block * LANES, (block + 1) * LANES)
        steps = decay_ref[:, lanes] / total
        decays = jnp.exp(-steps)
        scales = residue_ref[:, lanes] * jnp.sqrt(2.0 * steps)
        decay = [spread(decays[m : m + 1]) for m in range(modes)]
        scale = [spread(scales[m : m + 1]) for m in range(modes)]

        def advance(i, state):
            x = signal[block, pl.ds(i, SEGS, stride=length), :]
            state = tuple(d * s + x for d, s in zip(decay, state))
            y_ref[i, :, lanes] = tree_sum(c * s for c, s in zip(scale, state))
            return state

        zero = jnp.zeros((SEGS, LANES), F32)
        state = lax.fori_loop(0, length, advance, (zero,) * modes, unroll=4)
        for m in range(modes):
            ends = state[m]
            for hop in (1, 2, 4):
                factor = spread(jnp.exp(-steps[m : m + 1] * float(length * hop)))
                ends = ends + factor * jnp.where(seg >= hop, pltpu.roll(ends, hop, 0), 0.0)
            end_ref[m : m + 1, lanes] = ends[SEGS - 1 : SEGS]
            carry_ref[m, :, lanes] = jnp.where(seg >= 1, pltpu.roll(ends, 1, 0), 0.0)


def gate_kernel(
    total, seat_ref, qf_ref, y_ref, carry_ref, incoming_ref, decay_ref, residue_ref,
    out_ref, mixed,
):
    rows, width = qf_ref.shape
    modes = decay_ref.shape[0]
    length = rows // SEGS
    begin = (lax.broadcasted_iota(jnp.int32, (SEGS, LANES), 0) * length).astype(F32)
    for block in range(width // LANES):
        lanes = slice(block * LANES, (block + 1) * LANES)
        steps = decay_ref[:, lanes] / total
        decays = jnp.exp(-steps)
        weights = residue_ref[:, lanes] * jnp.sqrt(2.0 * steps) * decays
        decay = [spread(decays[m : m + 1]) for m in range(modes)]
        tail = []
        for m in range(modes):
            reach = jnp.exp(-spread(steps[m : m + 1]) * begin)
            held = carry_ref[m, :, lanes] + reach * spread(incoming_ref[m : m + 1, lanes])
            tail.append(spread(weights[m : m + 1]) * held)

        def advance(i, tail):
            mixed[block, pl.ds(i, SEGS, stride=length), :] = y_ref[i, :, lanes] + tree_sum(tail)
            return tuple(d * s for d, s in zip(decay, tail))

        lax.fori_loop(0, length, advance, tuple(tail), unroll=4)
    for block in range(width // LANES):
        lanes = slice(block * LANES, (block + 1) * LANES)
        out_ref[:, lanes] = (qf_ref[:, lanes].astype(F32) * mixed[block]).astype(BF16)


def column_call(body, name, arrays, outs, scratch, width, chan_count):
    def spec(shape):
        if shape[-1] != chan_count:
            return pl.BlockSpec(shape, lambda c: (0,) * len(shape))
        return pl.BlockSpec(shape[:-1] + (width,), lambda c: (0,) * (len(shape) - 1) + (c,))

    return pl.pallas_call(
        body,
        grid=(chan_count // width,),
        in_specs=[spec(a.shape) for a in arrays],
        out_specs=[spec(o.shape) for o in outs],
        out_shape=outs,
        scratch_shapes=scratch,
        compiler_params=pltpu.CompilerParams(vmem_limit_bytes=VMEM_GRANT),
        name=name,
    )(*arrays)


def local_rows(q_proj, k_proj, v_proj, rims, short_filter, residue, decay_rate):
    rows, chan_count = q_proj.shape
    modes = decay_rate.shape[0]
    total = float(rows * lax.axis_size("context"))
    width = lane_block(chan_count)
    return column_call(
        functools.partial(local_kernel, total), "local_pass",
        (q_proj, k_proj, v_proj, rims, short_filter, decay_rate, residue),
        [
            jax.ShapeDtypeStruct((rows, chan_count), BF16),
            jax.ShapeDtypeStruct((rows // SEGS, SEGS, chan_count), F32),
            jax.ShapeDtypeStruct((modes, SEGS, chan_count), F32),
            jax.ShapeDtypeStruct((modes, chan_count), F32),
        ],
        [
            pltpu.VMEM((3, rows + SEGS, LANES), F32),
            pltpu.VMEM((width // LANES, rows, LANES), F32),
        ],
        width, chan_count,
    )


def gate_rows(q_feat, y_local, carry, incoming, decay_rate, residue, seat):
    rows, chan_count = q_feat.shape
    modes = decay_rate.shape[0]
    total = float(rows * lax.axis_size("context"))
    width = lane_block(chan_count)
    per_part = incoming.shape[2] // width

    def cols(height):
        return pl.BlockSpec((height, width), lambda c, s: (0, c))

    return pl.pallas_call(
        functools.partial(gate_kernel, total),
        grid_spec=pltpu.PrefetchScalarGridSpec(
            num_scalar_prefetch=1,
            grid=(chan_count // width,),
            in_specs=[
                cols(rows),
                pl.BlockSpec((rows // SEGS, SEGS, width), lambda c, s: (0, 0, c)),
                pl.BlockSpec((modes, SEGS, width), lambda c, s: (0, 0, c)),
                pl.BlockSpec(
                    (None, modes, width), lambda c, s: (s[0] ^ (c // per_part), 0, c % per_part)
                ),
                cols(modes),
                cols(modes),
            ],
            out_specs=cols(rows),
            scratch_shapes=[pltpu.VMEM((width // LANES, rows, LANES), F32)],
        ),
        out_shape=jax.ShapeDtypeStruct((rows, chan_count), BF16),
        compiler_params=pltpu.CompilerParams(vmem_limit_bytes=VMEM_GRANT),
        name="gate_pass",
    )(seat.reshape(1), q_feat, y_local, carry, incoming, decay_rate, residue)


def by_seat(seat, blocks):
    ordered = []
    for k in range(CREW):
        value = blocks[0]
        for j in range(1, CREW):
            value = jnp.where((seat ^ k) == j, blocks[j], value)
        ordered.append(value)
    return ordered


def plane_kernel(span, seat_ref, steps_ref, *refs):
    blocks, out_ref = refs[:CREW], refs[CREW]
    reach = jnp.exp(-steps_ref[...] * span)
    ends = by_seat(seat_ref[0], [b[...] for b in blocks])
    state = ends[0]
    for end in ends[1:]:
        state = reach * state + end
    out_ref[...] = state


def incoming_kernel(span, seat_ref, steps_ref, *refs):
    blocks, planes = refs[:CREW], refs[CREW : CREW + PLANES - 1]
    outs = refs[CREW + PLANES - 1 :]
    steps, seat = steps_ref[...], seat_ref[0]
    ends = by_seat(seat, [b[...] for b in blocks])
    reach, reach_plane = jnp.exp(-steps * span), jnp.exp(-steps * (span * CREW))
    state = planes[-1][...]
    for plane in planes[-2::-1]:
        state = reach_plane * state + plane[...]
    states = [state]
    for end in ends[:-1]:
        states.append(reach * states[-1] + end)
    for out_ref, value in zip(outs, by_seat(seat, states)):
        out_ref[...] = value


def state_call(body, name, seat, steps, ends, arrays, out_count):
    modes, quarter = arrays[0].shape

    def owned(_, s):
        return (0, s[0])

    own = pl.BlockSpec((modes, quarter), owned)
    whole = pl.BlockSpec((modes, quarter), lambda _, s: (0, 0))
    shape = jax.ShapeDtypeStruct((modes, quarter), F32)
    return pl.pallas_call(
        body,
        grid_spec=pltpu.PrefetchScalarGridSpec(
            num_scalar_prefetch=1,
            grid=(1,),
            in_specs=[own, own] + [whole] * len(arrays),
            out_specs=[whole] * out_count,
        ),
        out_shape=[shape] * out_count,
        name=name,
    )(seat.reshape(1), steps, ends, *arrays)


def product_kernel(token_count, side_ref, weight_ref, *refs):
    tokens, (kept_ref, sent_ref, total) = refs[:token_count], refs[token_count:]
    planes, feat, width = weight_ref.shape
    step = pl.program_id(0)

    @pl.when(step == 0)
    def _():
        total[...] = jnp.zeros_like(total)

    weights = weight_ref[...].reshape(planes * feat, width)
    for j, token in enumerate(tokens):
        total[j] += lax.dot_general(
            weights, token[...], (((1,), (1,)), ((), ())), preferred_element_type=F32
        )

    @pl.when(step == pl.num_programs(0) - 1)
    def _():
        middle = total.shape[1] // 2
        for side, outs in ((0, (kept_ref, sent_ref)), (1, (sent_ref, kept_ref))):

            @pl.when(side_ref[0] == side)
            def _():
                outs[0][...] = total[:, :middle, :].astype(BF16)
                outs[1][...] = total[:, middle:, :].astype(BF16)


def project(weights, tokens, side):
    rows, depth = tokens[0].shape
    planes, feat, _ = weights.shape
    width = 1024 if depth % 1024 == 0 else LANES
    shape = (len(tokens), planes * feat // 2, rows)
    return pl.pallas_call(
        functools.partial(product_kernel, len(tokens)),
        grid_spec=pltpu.PrefetchScalarGridSpec(
            num_scalar_prefetch=1,
            grid=(depth // width,),
            in_specs=[pl.BlockSpec((planes, feat, width), lambda c, _: (0, 0, c))]
            + [pl.BlockSpec((rows, width), lambda c, _: (0, c)) for _ in tokens],
            out_specs=[pl.BlockSpec(shape, lambda c, _: (0, 0, 0))] * 2,
            scratch_shapes=[pltpu.VMEM((len(tokens), planes * feat, rows), F32)],
        ),
        out_shape=[jax.ShapeDtypeStruct(shape, BF16)] * 2,
        compiler_params=pltpu.CompilerParams(vmem_limit_bytes=VMEM_GRANT),
        cost_estimate=pl.CostEstimate(flops=1, bytes_accessed=1, transcendentals=0),
        name="project",
    )(side.reshape(1), weights, *tokens)


def assemble_kernel(place_ref, *refs):
    pieces, out_ref = refs[:-1], refs[-1]
    feat = out_ref.shape[0] // (2 * CREW)
    upper, odd = place_ref[0], place_ref[1]
    for member, piece in zip(NEAR + FAR, pieces):
        first = ((upper ^ (member // CREW)) * CREW + (odd ^ (member % 2))) * feat
        for row in range(2):
            at = pl.multiple_of(first + row * 2 * feat, feat)
            out_ref[pl.ds(at, feat), :] = piece[row * feat : (row + 1) * feat, :]


def assemble(place, pieces):
    rows = pieces[0].shape[1]
    vmem = pl.BlockSpec(memory_space=pltpu.VMEM)
    return pl.pallas_call(
        assemble_kernel,
        in_specs=[pl.BlockSpec(memory_space=pltpu.SMEM)] + [vmem] * len(pieces),
        out_specs=vmem,
        out_shape=jax.ShapeDtypeStruct((sum(p.shape[0] for p in pieces), rows), BF16),
        compiler_params=pltpu.CompilerParams(vmem_limit_bytes=VMEM_GRANT),
        name="assemble",
    )(place, *pieces)


def tails_kernel(q_ref, k_ref, v_ref, out_ref):
    lead = LEAD
    for which, ref in enumerate((q_ref, k_ref, v_ref)):
        rows = ref[...].astype(F32)
        out_ref[which * lead : (which + 1) * lead, :] = rows[rows.shape[0] - lead :]
    out_ref[3 * lead :, :] = jnp.zeros((out_ref.shape[0] - 3 * lead, out_ref.shape[1]), F32)


def gather_rims(q_proj, k_proj, v_proj):
    size = lax.axis_size("context")
    rows, chan_count = q_proj.shape
    last = pl.BlockSpec((16, chan_count), lambda i: (rows // 16 - 1, 0))
    tails = pl.pallas_call(
        tails_kernel,
        grid=(1,),
        in_specs=[last] * 3,
        out_specs=pl.BlockSpec((SEGS, chan_count), lambda i: (0, 0)),
        out_shape=jax.ShapeDtypeStruct((SEGS, chan_count), F32),
        compiler_params=pltpu.CompilerParams(vmem_limit_bytes=VMEM_GRANT),
        name="tails",
    )(q_proj, k_proj, v_proj)
    return lax.ppermute(tails, "context", [(i, i + 1) for i in range(size - 1)])


def per_device(q_proj, k_proj, v_proj, short_filter, residue, decay_rate, out_weight):
    place, size = lax.axis_index("context"), lax.axis_size("context")

    rows = q_proj.shape[0]
    rims = gather_rims(q_proj, k_proj, v_proj)
    q_feat, y_local, carry, ends = local_rows(
        q_proj, k_proj, v_proj, rims, short_filter, residue, decay_rate
    )
    gathered = lax.all_gather(ends, "context")
    gaps = (place - 1 - jnp.arange(size))[:, None, None]
    reach = jnp.exp(-(decay_rate / float(rows * size))[None] * (gaps * rows).astype(F32))
    incoming = jnp.sum(jnp.where(gaps >= 0, reach * gathered, 0.0), axis=0)
    gated = gate_rows(
        q_feat, y_local, carry, incoming[None], decay_rate, residue, jnp.int32(0)
    )
    partial_terms = lax.dot_general(
        lax.all_gather(out_weight, "context", axis=0, tiled=True),
        gated,
        (((1,), (1,)), ((), ())),
        preferred_element_type=F32,
    )
    return lax.psum_scatter(
        partial_terms.astype(BF16), "tensor", scatter_dimension=0, tiled=True
    )


def swap(block, mask):
    size = lax.axis_size("context")
    return lax.ppermute(block, "context", [(i, i ^ mask) for i in range(size)])


def shift(block, distance):
    size = lax.axis_size("context")
    moves = [(i, i + distance) for i in range(size) if 0 <= i + distance < size]
    return lax.ppermute(block, "context", moves)


def per_device_planes(q_proj, k_proj, v_proj, short_filter, residue, decay_rate, out_weight):
    size = lax.axis_size("context")
    seat = lax.axis_index("context") % CREW
    seat_of_plane = lax.axis_index("context") // CREW % 2
    side = lax.axis_index("tensor")
    rows, feat = q_proj.shape[0], out_weight.shape[0]
    quarter = q_proj.shape[1] // CREW
    span = float(rows)
    steps = decay_rate / (span * size)
    half = 2 * CREW
    owners = [
        [h * half + z * CREW + y * 2 + c for h in range(2) for y in range(2)]
        for z in range(2)
        for c in range(2)
    ]
    weights = lax.all_gather(out_weight, "context", axis_index_groups=owners)

    rims = gather_rims(q_proj, k_proj, v_proj)
    q_feat, y_local, carry, ends = local_rows(
        q_proj, k_proj, v_proj, rims, short_filter, residue, decay_rate
    )
    blocks = [
        swap(lax.dynamic_slice_in_dim(ends, (seat ^ j) * quarter, quarter, 1), j)
        for j in range(1, CREW)
    ]
    total = state_call(
        functools.partial(plane_kernel, span), "plane_state", seat, steps, ends, blocks, 1
    )[0]
    planes = [shift(total, hop * CREW) for hop in range(1, PLANES)]
    mine = state_call(
        functools.partial(incoming_kernel, span), "incoming_state",
        seat, steps, ends, blocks + planes, CREW,
    )
    incoming = jnp.stack([mine[0]] + [swap(mine[j], j) for j in range(1, CREW)])
    gated = gate_rows(q_feat, y_local, carry, incoming, decay_rate, residue, seat)
    far = swap(gated, FAR[0])
    near = [gated, swap(gated, NEAR[1])]

    def finish(kept, sent, members):
        arrived = lax.ppermute(sent, "tensor", [(0, 1), (1, 0)])
        sums = [
            (kept[at].astype(F32) + arrived[at].astype(F32)).astype(BF16)
            for at in range(len(members))
        ]
        return [swap(part, j) if j else part for part, j in zip(sums, members)]

    near_kept, near_sent = project(weights, near, side)
    near_kept, far = lax.optimization_barrier((near_kept, far))
    pieces = finish(near_kept, near_sent, NEAR)
    pieces += finish(*project(weights, [far], side), FAR[:1])
    pieces += finish(*project(weights, [swap(far, NEAR[1])], side), FAR[1:])
    place = jnp.stack([seat_of_plane, seat % 2]).astype(jnp.int32)
    return assemble(place, pieces)


def solution(mesh):
    planes = mesh.shape["tensor"] == 2 and mesh.shape["context"] == CREW * PLANES
    return jax.shard_map(
        per_device_planes if planes else per_device,
        mesh=mesh,
        in_specs=(
            P("context", "tensor"),
            P("context", "tensor"),
            P("context", "tensor"),
            P(None, None, "tensor"),
            P(None, "tensor"),
            P(None, "tensor"),
            P("context", "tensor"),
        ),
        out_specs=P("tensor", "context"),
        check_vma=False,
    )
```

```python
import functools

import jax
import jax.numpy as jnp
from jax import lax
from jax.experimental import pallas as pl
from jax.experimental.pallas import tpu as pltpu
from jax.sharding import PartitionSpec as P

LANES = 128
SEGS = 8
CREW = 4
LEAD = 2
PLANES = 4
VMEM_GRANT = 56 * 2**20
F32 = jnp.float32
BF16 = jnp.bfloat16


def lane_block(chan_count):
    for width in (1024, 512):
        if chan_count % (CREW * width) == 0:
            return width
    return LANES


def tree_sum(terms):
    terms = list(terms)
    while len(terms) > 1:
        paired = [terms[i] + terms[i + 1] for i in range(0, len(terms) - 1, 2)]
        if len(terms) % 2:
            paired.append(terms[-1])
        terms = paired
    return terms[0]


def spread(row):
    return jnp.broadcast_to(row, (SEGS, LANES))


def local_kernel(
    total, q_ref, k_ref, v_ref, rim_ref, filter_ref, decay_ref, residue_ref,
    qf_ref, y_ref, carry_ref, end_ref, shifted, signal,
):
    rows, width = q_ref.shape
    modes = decay_ref.shape[0]
    length = rows // SEGS
    kinds, tap_count, groups = filter_ref.shape
    group_width = pl.num_programs(0) * width // groups
    chan = pl.program_id(0) * width + lax.broadcasted_iota(jnp.int32, (groups, width), 1)
    first = lax.broadcasted_iota(jnp.int32, (groups, width), 0) * group_width
    member = ((chan >= first) & (chan < first + group_width)).astype(BF16)
    taps = [
        jnp.dot(filter_ref[kind], member, preferred_element_type=F32) for kind in range(kinds)
    ]
    lead = LEAD

    def short_pass(which, ref, lanes):
        pad = shifted.at[which]
        pad[SEGS : SEGS + rows, :] = ref[:, lanes].astype(F32)
        pad[SEGS - lead : SEGS, :] = rim_ref[which * lead : (which + 1) * lead, lanes]
        running = None
        for offset in range(tap_count):
            tap = taps[which][offset : offset + 1, lanes]
            term = tap * pad[SEGS - offset : SEGS - offset + rows, :]
            running = term if running is None else running + term
        return running.astype(BF16)

    for block in range(width // LANES):
        lanes = slice(block * LANES, (block + 1) * LANES)
        qf_ref[:, lanes] = short_pass(0, q_ref, lanes)
        k_feat = short_pass(1, k_ref, lanes).astype(F32)
        v_feat = short_pass(2, v_ref, lanes).astype(F32)
        signal[block] = (k_feat * v_feat).astype(BF16).astype(F32)

    seg = lax.broadcasted_iota(jnp.int32, (SEGS, LANES), 0)
    for block in range(width // LANES):
        lanes = slice(block * LANES, (block + 1) * LANES)
        steps = decay_ref[:, lanes] / total
        decays = jnp.exp(-steps)
        scales = residue_ref[:, lanes] * jnp.sqrt(2.0 * steps)
        decay = [spread(decays[m : m + 1]) for m in range(modes)]
        scale = [spread(scales[m : m + 1]) for m in range(modes)]

        def advance(i, state):
            x = signal[block, pl.ds(i, SEGS, stride=length), :]
            state = tuple(d * s + x for d, s in zip(decay, state))
            y_ref[i, :, lanes] = tree_sum(c * s for c, s in zip(scale, state))
            return state

        zero = jnp.zeros((SEGS, LANES), F32)
        state = lax.fori_loop(0, length, advance, (zero,) * modes, unroll=4)
        for m in range(modes):
            ends = state[m]
            for hop in (1, 2, 4):
                factor = spread(jnp.exp(-steps[m : m + 1] * float(length * hop)))
                ends = ends + factor * jnp.where(seg >= hop, pltpu.roll(ends, hop, 0), 0.0)
            end_ref[m : m + 1, lanes] = ends[SEGS - 1 : SEGS]
            carry_ref[m, :, lanes] = jnp.where(seg >= 1, pltpu.roll(ends, 1, 0), 0.0)


def gate_kernel(
    total, seat_ref, qf_ref, y_ref, carry_ref, incoming_ref, decay_ref, residue_ref,
    out_ref, mixed,
):
    rows, width = qf_ref.shape
    modes = decay_ref.shape[0]
    length = rows // SEGS
    begin = (lax.broadcasted_iota(jnp.int32, (SEGS, LANES), 0) * length).astype(F32)
    for block in range(width // LANES):
        lanes = slice(block * LANES, (block + 1) * LANES)
        steps = decay_ref[:, lanes] / total
        decays = jnp.exp(-steps)
        weights = residue_ref[:, lanes] * jnp.sqrt(2.0 * steps) * decays
        decay = [spread(decays[m : m + 1]) for m in range(modes)]
        tail = []
        for m in range(modes):
            reach = jnp.exp(-spread(steps[m : m + 1]) * begin)
            held = carry_ref[m, :, lanes] + reach * spread(incoming_ref[m : m + 1, lanes])
            tail.append(spread(weights[m : m + 1]) * held)

        def advance(i, tail):
            mixed[block, pl.ds(i, SEGS, stride=length), :] = y_ref[i, :, lanes] + tree_sum(tail)
            return tuple(d * s for d, s in zip(decay, tail))

        lax.fori_loop(0, length, advance, tuple(tail), unroll=4)
    for block in range(width // LANES):
        lanes = slice(block * LANES, (block + 1) * LANES)
        out_ref[:, lanes] = (qf_ref[:, lanes].astype(F32) * mixed[block]).astype(BF16)


def column_call(body, name, arrays, outs, scratch, width, chan_count):
    def spec(shape):
        if shape[-1] != chan_count:
            return pl.BlockSpec(shape, lambda c: (0,) * len(shape))
        return pl.BlockSpec(shape[:-1] + (width,), lambda c: (0,) * (len(shape) - 1) + (c,))

    return pl.pallas_call(
        body,
        grid=(chan_count // width,),
        in_specs=[spec(a.shape) for a in arrays],
        out_specs=[spec(o.shape) for o in outs],
        out_shape=outs,
        scratch_shapes=scratch,
        compiler_params=pltpu.CompilerParams(vmem_limit_bytes=VMEM_GRANT),
        name=name,
    )(*arrays)


def local_rows(q_proj, k_proj, v_proj, rims, short_filter, residue, decay_rate):
    rows, chan_count = q_proj.shape
    modes = decay_rate.shape[0]
    total = float(rows * lax.axis_size("context"))
    width = lane_block(chan_count)
    return column_call(
        functools.partial(local_kernel, total), "local_pass",
        (q_proj, k_proj, v_proj, rims, short_filter, decay_rate, residue),
        [
            jax.ShapeDtypeStruct((rows, chan_count), BF16),
            jax.ShapeDtypeStruct((rows // SEGS, SEGS, chan_count), F32),
            jax.ShapeDtypeStruct((modes, SEGS, chan_count), F32),
            jax.ShapeDtypeStruct((modes, chan_count), F32),
        ],
        [
            pltpu.VMEM((3, rows + SEGS, LANES), F32),
            pltpu.VMEM((width // LANES, rows, LANES), F32),
        ],
        width, chan_count,
    )


def gate_rows(q_feat, y_local, carry, incoming, decay_rate, residue, seat):
    rows, chan_count = q_feat.shape
    modes = decay_rate.shape[0]
    total = float(rows * lax.axis_size("context"))
    width = lane_block(chan_count)
    per_part = incoming.shape[2] // width

    def cols(height):
        return pl.BlockSpec((height, width), lambda c, s: (0, c))

    return pl.pallas_call(
        functools.partial(gate_kernel, total),
        grid_spec=pltpu.PrefetchScalarGridSpec(
            num_scalar_prefetch=1,
            grid=(chan_count // width,),
            in_specs=[
                cols(rows),
                pl.BlockSpec((rows // SEGS, SEGS, width), lambda c, s: (0, 0, c)),
                pl.BlockSpec((modes, SEGS, width), lambda c, s: (0, 0, c)),
                pl.BlockSpec(
                    (None, modes, width), lambda c, s: (s[0] ^ (c // per_part), 0, c % per_part)
                ),
                cols(modes),
                cols(modes),
            ],
            out_specs=cols(rows),
            scratch_shapes=[pltpu.VMEM((width // LANES, rows, LANES), F32)],
        ),
        out_shape=jax.ShapeDtypeStruct((rows, chan_count), BF16),
        compiler_params=pltpu.CompilerParams(vmem_limit_bytes=VMEM_GRANT),
        name="gate_pass",
    )(seat.reshape(1), q_feat, y_local, carry, incoming, decay_rate, residue)


def by_seat(seat, blocks):
    ordered = []
    for k in range(CREW):
        value = blocks[0]
        for j in range(1, CREW):
            value = jnp.where((seat ^ k) == j, blocks[j], value)
        ordered.append(value)
    return ordered


def plane_kernel(span, seat_ref, steps_ref, *refs):
    blocks, out_ref = refs[:CREW], refs[CREW]
    reach = jnp.exp(-steps_ref[...] * span)
    ends = by_seat(seat_ref[0], [b[...] for b in blocks])
    state = ends[0]
    for end in ends[1:]:
        state = reach * state + end
    out_ref[...] = state


def incoming_kernel(span, seat_ref, steps_ref, *refs):
    blocks, planes = refs[:CREW], refs[CREW : CREW + PLANES - 1]
    outs = refs[CREW + PLANES - 1 :]
    steps, seat = steps_ref[...], seat_ref[0]
    ends = by_seat(seat, [b[...] for b in blocks])
    reach, reach_plane = jnp.exp(-steps * span), jnp.exp(-steps * (span * CREW))
    state = planes[-1][...]
    for plane in planes[-2::-1]:
        state = reach_plane * state + plane[...]
    states = [state]
    for end in ends[:-1]:
        states.append(reach * states[-1] + end)
    for out_ref, value in zip(outs, by_seat(seat, states)):
        out_ref[...] = value


def state_call(body, name, seat, steps, ends, arrays, out_count):
    modes, quarter = arrays[0].shape

    def owned(_, s):
        return (0, s[0])

    own = pl.BlockSpec((modes, quarter), owned)
    whole = pl.BlockSpec((modes, quarter), lambda _, s: (0, 0))
    shape = jax.ShapeDtypeStruct((modes, quarter), F32)
    return pl.pallas_call(
        body,
        grid_spec=pltpu.PrefetchScalarGridSpec(
            num_scalar_prefetch=1,
            grid=(1,),
            in_specs=[own, own] + [whole] * len(arrays),
            out_specs=[whole] * out_count,
        ),
        out_shape=[shape] * out_count,
        name=name,
    )(seat.reshape(1), steps, ends, *arrays)


def product_kernel(token_count, pick_ref, gathered_ref, *refs):
    refs = list(refs)
    relayed = [refs.pop(0) for _ in range(2 * PLANES - 1)]
    tokens = [refs.pop(0) for _ in range(token_count)]
    kept_ref, sent_ref, total, joined = refs
    planes, cut, _ = gathered_ref.shape
    feat = cut + relayed[0].shape[0]
    step = pl.program_id(0)

    @pl.when(step == 0)
    def _():
        total[...] = jnp.zeros_like(total)

    for plane in range(planes):
        joined[plane * feat : plane * feat + cut, :] = gathered_ref[plane]
        for here in range(planes):

            @pl.when(pick_ref[1] == here)
            def _():
                source = relayed[planes - 1 + here - plane]
                joined[plane * feat + cut : (plane + 1) * feat, :] = source[...]

    for j, token in enumerate(tokens):
        total[j] += lax.dot_general(
            joined[...], token[...], (((1,), (1,)), ((), ())), preferred_element_type=F32
        )

    @pl.when(step == pl.num_programs(0) - 1)
    def _():
        middle = total.shape[1] // 2
        for side, outs in ((0, (kept_ref, sent_ref)), (1, (sent_ref, kept_ref))):

            @pl.when(pick_ref[0] == side)
            def _():
                outs[0][...] = total[:, :middle, :].astype(BF16)
                outs[1][...] = total[:, middle:, :].astype(BF16)


def project(picks, gathered, relayed, tokens):
    rows, depth = tokens[0].shape
    planes, cut, _ = gathered.shape
    feat = cut + relayed[0].shape[0]
    width = 1024 if depth % 1024 == 0 else LANES
    shape = (len(tokens), planes * feat // 2, rows)
    return pl.pallas_call(
        functools.partial(product_kernel, len(tokens)),
        grid_spec=pltpu.PrefetchScalarGridSpec(
            num_scalar_prefetch=1,
            grid=(depth // width,),
            in_specs=[pl.BlockSpec((planes, cut, width), lambda c, _: (0, 0, c))]
            + [pl.BlockSpec((a.shape[0], width), lambda c, _: (0, c)) for a in relayed + tokens],
            out_specs=[pl.BlockSpec(shape, lambda c, _: (0, 0, 0))] * 2,
            scratch_shapes=[
                pltpu.VMEM((len(tokens), planes * feat, rows), F32),
                pltpu.VMEM((planes * feat, width), BF16),
            ],
        ),
        out_shape=[jax.ShapeDtypeStruct(shape, BF16)] * 2,
        compiler_params=pltpu.CompilerParams(vmem_limit_bytes=VMEM_GRANT),
        cost_estimate=pl.CostEstimate(
            flops=2 * len(tokens) * planes * feat * rows * depth,
            bytes_accessed=2 * depth * (planes * feat + len(tokens) * rows),
            transcendentals=0,
        ),
        name="project",
    )(picks, gathered, *relayed, *tokens)


def assemble_kernel(seat_ref, *refs):
    pieces, out_ref = refs[:-1], refs[-1]
    halves = PLANES // 2
    block = out_ref.shape[0] // halves
    feat = block // CREW
    for j in range(CREW):
        for half in range(halves):
            at = pl.multiple_of(half * block + (seat_ref[0] ^ j) * feat, feat)
            out_ref[pl.ds(at, feat), :] = pieces[j][half * feat : (half + 1) * feat, :]


def assemble(seat, pieces):
    rows = pieces[0].shape[1]
    vmem = pl.BlockSpec(memory_space=pltpu.VMEM)
    return pl.pallas_call(
        assemble_kernel,
        in_specs=[pl.BlockSpec(memory_space=pltpu.SMEM)] + [vmem] * len(pieces),
        out_specs=vmem,
        out_shape=jax.ShapeDtypeStruct((sum(p.shape[0] for p in pieces), rows), BF16),
        compiler_params=pltpu.CompilerParams(vmem_limit_bytes=VMEM_GRANT),
        name="assemble",
    )(seat.reshape(1), *pieces)


def tails_kernel(q_ref, k_ref, v_ref, out_ref):
    lead = LEAD
    for which, ref in enumerate((q_ref, k_ref, v_ref)):
        rows = ref[...].astype(F32)
        out_ref[which * lead : (which + 1) * lead, :] = rows[rows.shape[0] - lead :]
    out_ref[3 * lead :, :] = jnp.zeros((out_ref.shape[0] - 3 * lead, out_ref.shape[1]), F32)


def gather_rims(q_proj, k_proj, v_proj):
    size = lax.axis_size("context")
    rows, chan_count = q_proj.shape
    last = pl.BlockSpec((16, chan_count), lambda i: (rows // 16 - 1, 0))
    tails = pl.pallas_call(
        tails_kernel,
        grid=(1,),
        in_specs=[last] * 3,
        out_specs=pl.BlockSpec((SEGS, chan_count), lambda i: (0, 0)),
        out_shape=jax.ShapeDtypeStruct((SEGS, chan_count), F32),
        compiler_params=pltpu.CompilerParams(vmem_limit_bytes=VMEM_GRANT),
        name="tails",
    )(q_proj, k_proj, v_proj)
    return lax.ppermute(tails, "context", [(i, i + 1) for i in range(size - 1)])


def per_device(q_proj, k_proj, v_proj, short_filter, residue, decay_rate, out_weight):
    place, size = lax.axis_index("context"), lax.axis_size("context")

    rows = q_proj.shape[0]
    rims = gather_rims(q_proj, k_proj, v_proj)
    q_feat, y_local, carry, ends = local_rows(
        q_proj, k_proj, v_proj, rims, short_filter, residue, decay_rate
    )
    gathered = lax.all_gather(ends, "context")
    gaps = (place - 1 - jnp.arange(size))[:, None, None]
    reach = jnp.exp(-(decay_rate / float(rows * size))[None] * (gaps * rows).astype(F32))
    incoming = jnp.sum(jnp.where(gaps >= 0, reach * gathered, 0.0), axis=0)
    gated = gate_rows(
        q_feat, y_local, carry, incoming[None], decay_rate, residue, jnp.int32(0)
    )
    partial_terms = lax.dot_general(
        lax.all_gather(out_weight, "context", axis=0, tiled=True),
        gated,
        (((1,), (1,)), ((), ())),
        preferred_element_type=F32,
    )
    return lax.psum_scatter(
        partial_terms.astype(BF16), "tensor", scatter_dimension=0, tiled=True
    )


def swap(block, mask):
    size = lax.axis_size("context")
    return lax.ppermute(block, "context", [(i, i ^ mask) for i in range(size)])


def shift(block, distance):
    size = lax.axis_size("context")
    moves = [(i, i + distance) for i in range(size) if 0 <= i + distance < size]
    return lax.ppermute(block, "context", moves)


def per_device_planes(q_proj, k_proj, v_proj, short_filter, residue, decay_rate, out_weight):
    size = lax.axis_size("context")
    seat = lax.axis_index("context") % CREW
    side = lax.axis_index("tensor")
    rows, feat = q_proj.shape[0], out_weight.shape[0]
    quarter = q_proj.shape[1] // CREW
    span = float(rows)
    steps = decay_rate / (span * size)
    columns = [[p * CREW + s for p in range(PLANES)] for s in range(CREW)]
    cut = feat * 3 // 4
    most, k_proj = lax.optimization_barrier((out_weight[:cut], k_proj))
    gathered = lax.all_gather(most, "context", axis_index_groups=columns)
    picks = jnp.stack([side, lax.axis_index("context") // CREW]).astype(jnp.int32)

    def hops(block, moves):
        return lax.ppermute(
            block, "context",
            [(a * CREW + s, b * CREW + s) for a, b in moves for s in range(CREW)],
        )

    rims = gather_rims(q_proj, k_proj, v_proj)
    rims, own = lax.optimization_barrier((rims, out_weight[cut:]))
    up1, down1 = shift(own, CREW), shift(own, -CREW)
    q_feat, y_local, carry, ends = local_rows(
        q_proj, k_proj, v_proj, rims, short_filter, residue, decay_rate
    )
    ends, up1, down1 = lax.optimization_barrier((ends, up1, down1))
    up2, down2 = hops(up1, [(1, 2), (2, 3)]), hops(down1, [(2, 1), (1, 0)])
    blocks = [
        swap(lax.dynamic_slice_in_dim(ends, (seat ^ j) * quarter, quarter, 1), j)
        for j in range(1, CREW)
    ]
    total = state_call(
        functools.partial(plane_kernel, span), "plane_state", seat, steps, ends, blocks, 1
    )[0]
    total, up2, down2 = lax.optimization_barrier((total, up2, down2))
    planes = [shift(total, hop * CREW) for hop in range(1, PLANES)]
    planes, last_up, last_down = lax.optimization_barrier((planes, up2, down2))
    up3, down3 = hops(last_up, [(2, 3)]), hops(last_down, [(1, 0)])
    mine = state_call(
        functools.partial(incoming_kernel, span), "incoming_state",
        seat, steps, ends, blocks + planes, CREW,
    )
    incoming = jnp.stack([mine[0]] + [swap(mine[j], j) for j in range(1, CREW)])
    gated = gate_rows(q_feat, y_local, carry, incoming, decay_rate, residue, seat)
    gated, up3, down3 = lax.optimization_barrier((gated, up3, down3))
    relayed = [down3, down2, down1, own, up1, up2, up3]
    far = swap(gated, 2)
    near = [gated, swap(gated, 1)]

    def finish(kept, sent, members):
        arrived = lax.ppermute(sent, "tensor", [(0, 1), (1, 0)])
        sums = [
            (kept[at].astype(F32) + arrived[at].astype(F32)).astype(BF16)
            for at in range(len(members))
        ]
        return [swap(part, j) if j else part for part, j in zip(sums, members)]

    kept, sent = project(picks, gathered, relayed, [far, swap(far, 1)])
    kept, near[0] = lax.optimization_barrier((kept, near[0]))
    beyond = finish(kept, sent, (2, 3))
    pieces = finish(*project(picks, gathered, relayed, near), (0, 1)) + beyond
    return assemble(seat, pieces)


def solution(mesh):
    planes = mesh.shape["tensor"] == 2 and mesh.shape["context"] == CREW * PLANES
    return jax.shard_map(
        per_device_planes if planes else per_device,
        mesh=mesh,
        in_specs=(
            P("context", "tensor"),
            P("context", "tensor"),
            P("context", "tensor"),
            P(None, None, "tensor"),
            P(None, "tensor"),
            P(None, "tensor"),
            P("context", "tensor"),
        ),
        out_specs=P("tensor", "context"),
        check_vma=False,
    )
```

```python
import functools
import math

import jax
import jax.numpy as jnp
from jax import lax
from jax.experimental import pallas as pl
from jax.experimental.pallas import tpu as pltpu
from jax.sharding import PartitionSpec as P

LANES = 128
SEGS = 8
CREW = 4
LEAD = 2
PLANES = 4
VMEM_GRANT = 56 * 2**20
F32 = jnp.float32
BF16 = jnp.bfloat16


def lane_block(chan_count):
    for width in (1024, 512):
        if chan_count % (CREW * width) == 0:
            return width
    return LANES


def tree_sum(terms):
    terms = list(terms)
    while len(terms) > 1:
        paired = [terms[i] + terms[i + 1] for i in range(0, len(terms) - 1, 2)]
        if len(terms) % 2:
            paired.append(terms[-1])
        terms = paired
    return terms[0]


def spread(row):
    return jnp.broadcast_to(row, (SEGS, LANES))


def local_kernel(
    total, q_ref, k_ref, v_ref, rim_ref, filter_ref, decay_ref, residue_ref,
    qf_ref, y_ref, carry_ref, end_ref, shifted, signal,
):
    rows, width = q_ref.shape
    modes = decay_ref.shape[0]
    length = rows // SEGS
    kinds, tap_count, groups = filter_ref.shape
    group_width = pl.num_programs(0) * width // groups
    chan = pl.program_id(0) * width + lax.broadcasted_iota(jnp.int32, (groups, width), 1)
    first = lax.broadcasted_iota(jnp.int32, (groups, width), 0) * group_width
    member = ((chan >= first) & (chan < first + group_width)).astype(BF16)
    taps = [
        jnp.dot(filter_ref[kind], member, preferred_element_type=F32) for kind in range(kinds)
    ]
    lead = LEAD

    def short_pass(which, ref, lanes):
        pad = shifted.at[which]
        pad[SEGS : SEGS + rows, :] = ref[:, lanes].astype(F32)
        pad[SEGS - lead : SEGS, :] = rim_ref[which * lead : (which + 1) * lead, lanes]
        running = None
        for offset in range(tap_count):
            tap = taps[which][offset : offset + 1, lanes]
            term = tap * pad[SEGS - offset : SEGS - offset + rows, :]
            running = term if running is None else running + term
        return running.astype(BF16)

    for block in range(width // LANES):
        lanes = slice(block * LANES, (block + 1) * LANES)
        qf_ref[:, lanes] = short_pass(0, q_ref, lanes)
        k_feat = short_pass(1, k_ref, lanes).astype(F32)
        v_feat = short_pass(2, v_ref, lanes).astype(F32)
        signal[block] = (k_feat * v_feat).astype(BF16).astype(F32)

    seg = lax.broadcasted_iota(jnp.int32, (SEGS, LANES), 0)
    for block in range(width // LANES):
        lanes = slice(block * LANES, (block + 1) * LANES)
        steps = decay_ref[:, lanes] / total
        decays = jnp.exp(-steps)
        scales = residue_ref[:, lanes] * jnp.sqrt(2.0 * steps)
        decay = [spread(decays[m : m + 1]) for m in range(modes)]
        scale = [spread(scales[m : m + 1]) for m in range(modes)]

        def advance(i, state):
            x = signal[block, pl.ds(i, SEGS, stride=length), :]
            state = tuple(d * s + x for d, s in zip(decay, state))
            y_ref[i, :, lanes] = tree_sum(c * s for c, s in zip(scale, state))
            return state

        zero = jnp.zeros((SEGS, LANES), F32)
        state = lax.fori_loop(0, length, advance, (zero,) * modes, unroll=4)
        for m in range(modes):
            ends = state[m]
            for hop in (1, 2, 4):
                factor = spread(jnp.exp(-steps[m : m + 1] * float(length * hop)))
                ends = ends + factor * jnp.where(seg >= hop, pltpu.roll(ends, hop, 0), 0.0)
            end_ref[m : m + 1, lanes] = ends[SEGS - 1 : SEGS]
            carry_ref[m, :, lanes] = jnp.where(seg >= 1, pltpu.roll(ends, 1, 0), 0.0)


def gate_kernel(
    total, seat_ref, qf_ref, y_ref, carry_ref, incoming_ref, decay_ref, residue_ref,
    out_ref, mixed,
):
    rows, width = qf_ref.shape
    modes = decay_ref.shape[0]
    length = rows // SEGS
    begin = (lax.broadcasted_iota(jnp.int32, (SEGS, LANES), 0) * length).astype(F32)
    for block in range(width // LANES):
        lanes = slice(block * LANES, (block + 1) * LANES)
        steps = decay_ref[:, lanes] / total
        decays = jnp.exp(-steps)
        weights = residue_ref[:, lanes] * jnp.sqrt(2.0 * steps) * decays
        decay = [spread(decays[m : m + 1]) for m in range(modes)]
        tail = []
        for m in range(modes):
            reach = jnp.exp(-spread(steps[m : m + 1]) * begin)
            held = carry_ref[m, :, lanes] + reach * spread(incoming_ref[m : m + 1, lanes])
            tail.append(spread(weights[m : m + 1]) * held)

        def advance(i, tail):
            mixed[block, pl.ds(i, SEGS, stride=length), :] = y_ref[i, :, lanes] + tree_sum(tail)
            return tuple(d * s for d, s in zip(decay, tail))

        lax.fori_loop(0, length, advance, tuple(tail), unroll=4)
    for block in range(width // LANES):
        lanes = slice(block * LANES, (block + 1) * LANES)
        out_ref[:, lanes] = (qf_ref[:, lanes].astype(F32) * mixed[block]).astype(BF16)


def column_call(body, name, arrays, outs, scratch, width, chan_count):
    def spec(shape):
        if shape[-1] != chan_count:
            return pl.BlockSpec(shape, lambda c: (0,) * len(shape))
        return pl.BlockSpec(shape[:-1] + (width,), lambda c: (0,) * (len(shape) - 1) + (c,))

    return pl.pallas_call(
        body,
        grid=(chan_count // width,),
        in_specs=[spec(a.shape) for a in arrays],
        out_specs=[spec(o.shape) for o in outs],
        out_shape=outs,
        scratch_shapes=scratch,
        compiler_params=pltpu.CompilerParams(vmem_limit_bytes=VMEM_GRANT),
        name=name,
    )(*arrays)


def local_rows(q_proj, k_proj, v_proj, rims, short_filter, residue, decay_rate):
    rows, chan_count = q_proj.shape
    modes = decay_rate.shape[0]
    total = float(rows * lax.axis_size("context"))
    width = lane_block(chan_count)
    return column_call(
        functools.partial(local_kernel, total), "local_pass",
        (q_proj, k_proj, v_proj, rims, short_filter, decay_rate, residue),
        [
            jax.ShapeDtypeStruct((rows, chan_count), BF16),
            jax.ShapeDtypeStruct((rows // SEGS, SEGS, chan_count), F32),
            jax.ShapeDtypeStruct((modes, SEGS, chan_count), F32),
            jax.ShapeDtypeStruct((modes, chan_count), F32),
        ],
        [
            pltpu.VMEM((3, rows + SEGS, LANES), F32),
            pltpu.VMEM((width // LANES, rows, LANES), F32),
        ],
        width, chan_count,
    )


def gate_rows(q_feat, y_local, carry, incoming, decay_rate, residue, seat):
    rows, chan_count = q_feat.shape
    modes = decay_rate.shape[0]
    total = float(rows * lax.axis_size("context"))
    width = lane_block(chan_count)
    per_part = incoming.shape[2] // width

    def cols(height):
        return pl.BlockSpec((height, width), lambda c, s: (0, c))

    return pl.pallas_call(
        functools.partial(gate_kernel, total),
        grid_spec=pltpu.PrefetchScalarGridSpec(
            num_scalar_prefetch=1,
            grid=(chan_count // width,),
            in_specs=[
                cols(rows),
                pl.BlockSpec((rows // SEGS, SEGS, width), lambda c, s: (0, 0, c)),
                pl.BlockSpec((modes, SEGS, width), lambda c, s: (0, 0, c)),
                pl.BlockSpec(
                    (None, modes, width), lambda c, s: (s[0] ^ (c // per_part), 0, c % per_part)
                ),
                cols(modes),
                cols(modes),
            ],
            out_specs=cols(rows),
            scratch_shapes=[pltpu.VMEM((width // LANES, rows, LANES), F32)],
        ),
        out_shape=jax.ShapeDtypeStruct((rows, chan_count), BF16),
        compiler_params=pltpu.CompilerParams(vmem_limit_bytes=VMEM_GRANT),
        name="gate_pass",
    )(seat.reshape(1), q_feat, y_local, carry, incoming, decay_rate, residue)


def by_seat(seat, blocks):
    ordered = []
    for k in range(CREW):
        value = blocks[0]
        for j in range(1, CREW):
            value = jnp.where((seat ^ k) == j, blocks[j], value)
        ordered.append(value)
    return ordered


def plane_kernel(span, seat_ref, steps_ref, *refs):
    blocks, out_ref = refs[:CREW], refs[CREW]
    reach = jnp.exp(-steps_ref[...] * span)
    ends = by_seat(seat_ref[0], [b[...] for b in blocks])
    state = ends[0]
    for end in ends[1:]:
        state = reach * state + end
    out_ref[...] = state


def incoming_kernel(span, seat_ref, steps_ref, *refs):
    blocks, planes = refs[:CREW], refs[CREW : CREW + PLANES - 1]
    outs = refs[CREW + PLANES - 1 :]
    steps, seat = steps_ref[...], seat_ref[0]
    ends = by_seat(seat, [b[...] for b in blocks])
    reach, reach_plane = jnp.exp(-steps * span), jnp.exp(-steps * (span * CREW))
    state = planes[-1][...]
    for plane in planes[-2::-1]:
        state = reach_plane * state + plane[...]
    states = [state]
    for end in ends[:-1]:
        states.append(reach * states[-1] + end)
    for out_ref, value in zip(outs, by_seat(seat, states)):
        out_ref[...] = value


def state_call(body, name, seat, steps, ends, arrays, out_count):
    modes, quarter = arrays[0].shape

    def owned(_, s):
        return (0, s[0])

    own = pl.BlockSpec((modes, quarter), owned)
    whole = pl.BlockSpec((modes, quarter), lambda _, s: (0, 0))
    shape = jax.ShapeDtypeStruct((modes, quarter), F32)
    return pl.pallas_call(
        body,
        grid_spec=pltpu.PrefetchScalarGridSpec(
            num_scalar_prefetch=1,
            grid=(1,),
            in_specs=[own, own] + [whole] * len(arrays),
            out_specs=[whole] * out_count,
        ),
        out_shape=[shape] * out_count,
        name=name,
    )(seat.reshape(1), steps, ends, *arrays)


def product_kernel(relayed_count, token_count, pick_ref, *refs):
    refs = list(refs)
    relayed = [refs.pop(0) for _ in range(relayed_count)]
    gathered_ref = None if relayed else refs.pop(0)
    tokens = [refs.pop(0) for _ in range(token_count)]
    kept_ref, sent_ref, total = refs[:3]
    step = pl.program_id(0)

    @pl.when(step == 0)
    def _():
        total[...] = jnp.zeros_like(total)

    if relayed:
        joined = refs[3]
        feat = relayed[0].shape[0]
        for plane in range(PLANES):
            for here in range(PLANES):

                @pl.when(pick_ref[1] == here)
                def _():
                    source = relayed[PLANES - 1 + here - plane]
                    joined[plane * feat : (plane + 1) * feat, :] = source[...]

        weights = joined[...]
    else:
        planes, feat, width = gathered_ref.shape
        weights = gathered_ref[...].reshape(planes * feat, width)
    for j, token in enumerate(tokens):
        total[j] += lax.dot_general(
            weights, token[...], (((1,), (1,)), ((), ())), preferred_element_type=F32
        )

    @pl.when(step == pl.num_programs(0) - 1)
    def _():
        middle = total.shape[1] // 2
        for side, outs in ((0, (kept_ref, sent_ref)), (1, (sent_ref, kept_ref))):

            @pl.when(pick_ref[0] == side)
            def _():
                outs[0][...] = total[:, :middle, :].astype(BF16)
                outs[1][...] = total[:, middle:, :].astype(BF16)


def project(picks, weights, tokens):
    rows, depth = tokens[0].shape
    width = 1024 if depth % 1024 == 0 else LANES
    relayed = weights if isinstance(weights, list) else []
    scratch = []
    if relayed:
        feat = relayed[0].shape[0]
        specs = [pl.BlockSpec((feat, width), lambda c, _: (0, c)) for _ in relayed]
        scratch = [pltpu.VMEM((PLANES * feat, width), BF16)]
    else:
        feat = weights.shape[1]
        specs = [pl.BlockSpec((PLANES, feat, width), lambda c, _: (0, 0, c))]
        weights = [weights]
    shape = (len(tokens), PLANES * feat // 2, rows)
    return pl.pallas_call(
        functools.partial(product_kernel, len(relayed), len(tokens)),
        grid_spec=pltpu.PrefetchScalarGridSpec(
            num_scalar_prefetch=1,
            grid=(depth // width,),
            in_specs=specs + [pl.BlockSpec((rows, width), lambda c, _: (0, c)) for _ in tokens],
            out_specs=[pl.BlockSpec(shape, lambda c, _: (0, 0, 0))] * 2,
            scratch_shapes=[pltpu.VMEM((len(tokens), PLANES * feat, rows), F32)] + scratch,
        ),
        out_shape=[jax.ShapeDtypeStruct(shape, BF16)] * 2,
        compiler_params=pltpu.CompilerParams(vmem_limit_bytes=VMEM_GRANT),
        cost_estimate=pl.CostEstimate(flops=1, bytes_accessed=1, transcendentals=0),
        name="project",
    )(picks, *weights, *tokens)


def assemble_kernel(seat_ref, *refs):
    pieces, out_ref = refs[:-1], refs[-1]
    halves = PLANES // 2
    block = out_ref.shape[0] // halves
    feat = block // CREW
    for j in range(CREW):
        begin = 0
        for piece in pieces[j::CREW]:
            size = piece.shape[0] // halves
            for half in range(halves):
                at = half * block + (seat_ref[0] ^ j) * feat + begin
                at = pl.multiple_of(at, math.gcd(size, begin) if begin else size)
                out_ref[pl.ds(at, size), :] = piece[half * size : (half + 1) * size, :]
            begin += size


def assemble(seat, pieces):
    rows = pieces[0].shape[1]
    vmem = pl.BlockSpec(memory_space=pltpu.VMEM)
    return pl.pallas_call(
        assemble_kernel,
        in_specs=[pl.BlockSpec(memory_space=pltpu.SMEM)] + [vmem] * len(pieces),
        out_specs=vmem,
        out_shape=jax.ShapeDtypeStruct((sum(p.shape[0] for p in pieces), rows), BF16),
        compiler_params=pltpu.CompilerParams(vmem_limit_bytes=VMEM_GRANT),
        name="assemble",
    )(seat.reshape(1), *pieces)


def tails_kernel(q_ref, k_ref, v_ref, out_ref):
    lead = LEAD
    for which, ref in enumerate((q_ref, k_ref, v_ref)):
        rows = ref[...].astype(F32)
        out_ref[which * lead : (which + 1) * lead, :] = rows[rows.shape[0] - lead :]
    out_ref[3 * lead :, :] = jnp.zeros((out_ref.shape[0] - 3 * lead, out_ref.shape[1]), F32)


def gather_rims(q_proj, k_proj, v_proj):
    size = lax.axis_size("context")
    rows, chan_count = q_proj.shape
    last = pl.BlockSpec((16, chan_count), lambda i: (rows // 16 - 1, 0))
    tails = pl.pallas_call(
        tails_kernel,
        grid=(1,),
        in_specs=[last] * 3,
        out_specs=pl.BlockSpec((SEGS, chan_count), lambda i: (0, 0)),
        out_shape=jax.ShapeDtypeStruct((SEGS, chan_count), F32),
        compiler_params=pltpu.CompilerParams(vmem_limit_bytes=VMEM_GRANT),
        name="tails",
    )(q_proj, k_proj, v_proj)
    return lax.ppermute(tails, "context", [(i, i + 1) for i in range(size - 1)])


def per_device(q_proj, k_proj, v_proj, short_filter, residue, decay_rate, out_weight):
    place, size = lax.axis_index("context"), lax.axis_size("context")

    rows = q_proj.shape[0]
    rims = gather_rims(q_proj, k_proj, v_proj)
    q_feat, y_local, carry, ends = local_rows(
        q_proj, k_proj, v_proj, rims, short_filter, residue, decay_rate
    )
    gathered = lax.all_gather(ends, "context")
    gaps = (place - 1 - jnp.arange(size))[:, None, None]
    reach = jnp.exp(-(decay_rate / float(rows * size))[None] * (gaps * rows).astype(F32))
    incoming = jnp.sum(jnp.where(gaps >= 0, reach * gathered, 0.0), axis=0)
    gated = gate_rows(
        q_feat, y_local, carry, incoming[None], decay_rate, residue, jnp.int32(0)
    )
    partial_terms = lax.dot_general(
        lax.all_gather(out_weight, "context", axis=0, tiled=True),
        gated,
        (((1,), (1,)), ((), ())),
        preferred_element_type=F32,
    )
    return lax.psum_scatter(
        partial_terms.astype(BF16), "tensor", scatter_dimension=0, tiled=True
    )


def swap(block, mask):
    size = lax.axis_size("context")
    return lax.ppermute(block, "context", [(i, i ^ mask) for i in range(size)])


def shift(block, distance):
    size = lax.axis_size("context")
    moves = [(i, i + distance) for i in range(size) if 0 <= i + distance < size]
    return lax.ppermute(block, "context", moves)


def per_device_planes(q_proj, k_proj, v_proj, short_filter, residue, decay_rate, out_weight):
    size = lax.axis_size("context")
    seat = lax.axis_index("context") % CREW
    side = lax.axis_index("tensor")
    rows, feat = q_proj.shape[0], out_weight.shape[0]
    quarter = q_proj.shape[1] // CREW
    span = float(rows)
    steps = decay_rate / (span * size)
    columns = [[p * CREW + s for p in range(PLANES)] for s in range(CREW)]
    cut = feat * 3 // 4
    most, k_proj = lax.optimization_barrier((out_weight[:cut], k_proj))
    gathered = lax.all_gather(most, "context", axis_index_groups=columns)
    picks = jnp.stack([side, lax.axis_index("context") // CREW]).astype(jnp.int32)

    def hops(block, moves):
        return lax.ppermute(
            block, "context",
            [(a * CREW + s, b * CREW + s) for a, b in moves for s in range(CREW)],
        )

    rims = gather_rims(q_proj, k_proj, v_proj)
    q_feat, y_local, carry, ends = local_rows(
        q_proj, k_proj, v_proj, rims, short_filter, residue, decay_rate
    )
    blocks = [
        swap(lax.dynamic_slice_in_dim(ends, (seat ^ j) * quarter, quarter, 1), j)
        for j in range(1, CREW)
    ]
    total = state_call(
        functools.partial(plane_kernel, span), "plane_state", seat, steps, ends, blocks, 1
    )[0]
    planes = [shift(total, hop * CREW) for hop in range(1, PLANES)]
    planes, own = lax.optimization_barrier((planes, out_weight[cut:]))
    up1, down1 = shift(own, CREW), shift(own, -CREW)
    mine = state_call(
        functools.partial(incoming_kernel, span), "incoming_state",
        seat, steps, ends, blocks + planes, CREW,
    )
    incoming = jnp.stack([mine[0]] + [swap(mine[j], j) for j in range(1, CREW)])
    gated = gate_rows(q_feat, y_local, carry, incoming, decay_rate, residue, seat)
    far = swap(gated, 2)
    beside, up1, down1 = lax.optimization_barrier((swap(gated, 1), up1, down1))
    up2, down2 = hops(up1, [(1, 2), (2, 3)]), hops(down1, [(2, 1), (1, 0)])

    def finish(kept, sent, members):
        arrived = lax.ppermute(sent, "tensor", [(0, 1), (1, 0)])
        sums = [
            (kept[at].astype(F32) + arrived[at].astype(F32)).astype(BF16)
            for at in range(len(members))
        ]
        return [swap(part, j) if j else part for part, j in zip(sums, members)]

    near = [gated, beside]
    kept, sent = project(picks, gathered, near)
    kept, far, last_up, last_down = lax.optimization_barrier((kept, far, up2, down2))
    up3, down3 = hops(last_up, [(2, 3)]), hops(last_down, [(1, 0)])
    pieces = finish(kept, sent, (0, 1))
    beyond = [far, swap(far, 1)]
    kept, sent = project(picks, gathered, beyond)
    kept, up3, down3 = lax.optimization_barrier((kept, up3, down3))
    pieces += finish(kept, sent, (2, 3))
    relayed = [down3, down2, down1, own, up1, up2, up3]
    pieces += finish(*project(picks, relayed, near + beyond), (0, 1, 2, 3))
    return assemble(seat, pieces)


def solution(mesh):
    planes = mesh.shape["tensor"] == 2 and mesh.shape["context"] == CREW * PLANES
    return jax.shard_map(
        per_device_planes if planes else per_device,
        mesh=mesh,
        in_specs=(
            P("context", "tensor"),
            P("context", "tensor"),
            P("context", "tensor"),
            P(None, None, "tensor"),
            P(None, "tensor"),
            P(None, "tensor"),
            P("context", "tensor"),
        ),
        out_specs=P("tensor", "context"),
        check_vma=False,
    )
```

```python
import functools
import math

import jax
import jax.numpy as jnp
from jax import lax
from jax.experimental import pallas as pl
from jax.experimental.pallas import tpu as pltpu
from jax.sharding import PartitionSpec as P

LANES = 128
SEGS = 8
CREW = 4
LEAD = 2
PLANES = 4
VMEM_GRANT = 56 * 2**20
F32 = jnp.float32
BF16 = jnp.bfloat16


def lane_block(chan_count):
    for width in (1024, 512):
        if chan_count % (CREW * width) == 0:
            return width
    return LANES


def tree_sum(terms):
    terms = list(terms)
    while len(terms) > 1:
        paired = [terms[i] + terms[i + 1] for i in range(0, len(terms) - 1, 2)]
        if len(terms) % 2:
            paired.append(terms[-1])
        terms = paired
    return terms[0]


def spread(row):
    return jnp.broadcast_to(row, (SEGS, LANES))


def local_kernel(
    total, q_ref, k_ref, v_ref, rim_ref, filter_ref, decay_ref, residue_ref,
    qf_ref, y_ref, carry_ref, end_ref, shifted, signal,
):
    rows, width = q_ref.shape
    modes = decay_ref.shape[0]
    length = rows // SEGS
    kinds, tap_count, groups = filter_ref.shape
    group_width = pl.num_programs(0) * width // groups
    begin, count = 0, groups
    if groups % LANES == 0 and LANES * group_width % width == 0:
        begin, count = pl.program_id(0) * width // (LANES * group_width) * LANES, LANES
        begin = pl.multiple_of(begin, LANES)
    chan = pl.program_id(0) * width + lax.broadcasted_iota(jnp.int32, (count, width), 1)
    first = (begin + lax.broadcasted_iota(jnp.int32, (count, width), 0)) * group_width
    member = ((chan >= first) & (chan < first + group_width)).astype(BF16)
    filters = [filter_ref[kind, :, pl.ds(begin, count)].astype(F32) for kind in range(kinds)]
    taps = jnp.dot(
        jnp.concatenate(filters, axis=0).astype(BF16), member, preferred_element_type=F32
    )
    lead = LEAD

    def short_pass(which, ref, lanes):
        pad = shifted.at[which]
        pad[SEGS : SEGS + rows, :] = ref[:, lanes].astype(F32)
        pad[SEGS - lead : SEGS, :] = rim_ref[which * lead : (which + 1) * lead, lanes]
        running = None
        for offset in range(tap_count):
            row = which * tap_count + offset
            tap = taps[row : row + 1, lanes]
            term = tap * pad[SEGS - offset : SEGS - offset + rows, :]
            running = term if running is None else running + term
        return running.astype(BF16)

    for block in range(width // LANES):
        lanes = slice(block * LANES, (block + 1) * LANES)
        qf_ref[:, lanes] = short_pass(0, q_ref, lanes)
        k_feat = short_pass(1, k_ref, lanes).astype(F32)
        v_feat = short_pass(2, v_ref, lanes).astype(F32)
        signal[block] = (k_feat * v_feat).astype(BF16).astype(F32)

    seg = lax.broadcasted_iota(jnp.int32, (SEGS, LANES), 0)
    for block in range(width // LANES):
        lanes = slice(block * LANES, (block + 1) * LANES)
        steps = decay_ref[:, lanes] / total
        decays = jnp.exp(-steps)
        scales = residue_ref[:, lanes] * jnp.sqrt(2.0 * steps)
        decay = [spread(decays[m : m + 1]) for m in range(modes)]
        scale = [spread(scales[m : m + 1]) for m in range(modes)]

        def advance(i, state):
            x = signal[block, pl.ds(i, SEGS, stride=length), :]
            state = tuple(d * s + x for d, s in zip(decay, state))
            y_ref[i, :, lanes] = tree_sum(c * s for c, s in zip(scale, state))
            return state

        zero = jnp.zeros((SEGS, LANES), F32)
        state = lax.fori_loop(0, length, advance, (zero,) * modes, unroll=4)
        for m in range(modes):
            ends = state[m]
            for hop in (1, 2, 4):
                factor = spread(jnp.exp(-steps[m : m + 1] * float(length * hop)))
                ends = ends + factor * jnp.where(seg >= hop, pltpu.roll(ends, hop, 0), 0.0)
            end_ref[m : m + 1, lanes] = ends[SEGS - 1 : SEGS]
            carry_ref[m, :, lanes] = jnp.where(seg >= 1, pltpu.roll(ends, 1, 0), 0.0)


def gate_kernel(
    total, seat_ref, qf_ref, y_ref, carry_ref, incoming_ref, decay_ref, residue_ref,
    out_ref, mixed,
):
    rows, width = qf_ref.shape
    modes = decay_ref.shape[0]
    length = rows // SEGS
    begin = (lax.broadcasted_iota(jnp.int32, (SEGS, LANES), 0) * length).astype(F32)
    for block in range(width // LANES):
        lanes = slice(block * LANES, (block + 1) * LANES)
        steps = decay_ref[:, lanes] / total
        decays = jnp.exp(-steps)
        weights = residue_ref[:, lanes] * jnp.sqrt(2.0 * steps) * decays
        decay = [spread(decays[m : m + 1]) for m in range(modes)]
        tail = []
        for m in range(modes):
            reach = jnp.exp(-spread(steps[m : m + 1]) * begin)
            held = carry_ref[m, :, lanes] + reach * spread(incoming_ref[m : m + 1, lanes])
            tail.append(spread(weights[m : m + 1]) * held)

        def advance(i, tail):
            mixed[block, pl.ds(i, SEGS, stride=length), :] = y_ref[i, :, lanes] + tree_sum(tail)
            return tuple(d * s for d, s in zip(decay, tail))

        lax.fori_loop(0, length, advance, tuple(tail), unroll=4)
    for block in range(width // LANES):
        lanes = slice(block * LANES, (block + 1) * LANES)
        out_ref[:, lanes] = (qf_ref[:, lanes].astype(F32) * mixed[block]).astype(BF16)


def column_call(body, name, arrays, outs, scratch, width, chan_count):
    def spec(shape):
        if shape[-1] != chan_count:
            return pl.BlockSpec(shape, lambda c: (0,) * len(shape))
        return pl.BlockSpec(shape[:-1] + (width,), lambda c: (0,) * (len(shape) - 1) + (c,))

    return pl.pallas_call(
        body,
        grid=(chan_count // width,),
        in_specs=[spec(a.shape) for a in arrays],
        out_specs=[spec(o.shape) for o in outs],
        out_shape=outs,
        scratch_shapes=scratch,
        compiler_params=pltpu.CompilerParams(vmem_limit_bytes=VMEM_GRANT),
        name=name,
    )(*arrays)


def local_rows(q_proj, k_proj, v_proj, rims, short_filter, residue, decay_rate):
    rows, chan_count = q_proj.shape
    modes = decay_rate.shape[0]
    total = float(rows * lax.axis_size("context"))
    width = lane_block(chan_count)
    return column_call(
        functools.partial(local_kernel, total), "local_pass",
        (q_proj, k_proj, v_proj, rims, short_filter, decay_rate, residue),
        [
            jax.ShapeDtypeStruct((rows, chan_count), BF16),
            jax.ShapeDtypeStruct((rows // SEGS, SEGS, chan_count), F32),
            jax.ShapeDtypeStruct((modes, SEGS, chan_count), F32),
            jax.ShapeDtypeStruct((modes, chan_count), F32),
        ],
        [
            pltpu.VMEM((3, rows + SEGS, LANES), F32),
            pltpu.VMEM((width // LANES, rows, LANES), F32),
        ],
        width, chan_count,
    )


def gate_rows(q_feat, y_local, carry, incoming, decay_rate, residue, seat):
    rows, chan_count = q_feat.shape
    modes = decay_rate.shape[0]
    total = float(rows * lax.axis_size("context"))
    width = lane_block(chan_count)
    per_part = incoming.shape[2] // width

    def cols(height):
        return pl.BlockSpec((height, width), lambda c, s: (0, c))

    return pl.pallas_call(
        functools.partial(gate_kernel, total),
        grid_spec=pltpu.PrefetchScalarGridSpec(
            num_scalar_prefetch=1,
            grid=(chan_count // width,),
            in_specs=[
                cols(rows),
                pl.BlockSpec((rows // SEGS, SEGS, width), lambda c, s: (0, 0, c)),
                pl.BlockSpec((modes, SEGS, width), lambda c, s: (0, 0, c)),
                pl.BlockSpec(
                    (None, modes, width), lambda c, s: (s[0] ^ (c // per_part), 0, c % per_part)
                ),
                cols(modes),
                cols(modes),
            ],
            out_specs=cols(rows),
            scratch_shapes=[pltpu.VMEM((width // LANES, rows, LANES), F32)],
        ),
        out_shape=jax.ShapeDtypeStruct((rows, chan_count), BF16),
        compiler_params=pltpu.CompilerParams(vmem_limit_bytes=VMEM_GRANT),
        name="gate_pass",
    )(seat.reshape(1), q_feat, y_local, carry, incoming, decay_rate, residue)


def by_seat(seat, blocks):
    ordered = []
    for k in range(CREW):
        value = blocks[0]
        for j in range(1, CREW):
            value = jnp.where((seat ^ k) == j, blocks[j], value)
        ordered.append(value)
    return ordered


def plane_kernel(span, seat_ref, steps_ref, *refs):
    blocks, out_ref = refs[:CREW], refs[CREW]
    reach = jnp.exp(-steps_ref[...] * span)
    ends = by_seat(seat_ref[0], [b[...] for b in blocks])
    state = ends[0]
    for end in ends[1:]:
        state = reach * state + end
    out_ref[...] = state


def incoming_kernel(span, seat_ref, steps_ref, *refs):
    blocks, planes = refs[:CREW], refs[CREW : CREW + PLANES - 1]
    outs = refs[CREW + PLANES - 1 :]
    steps, seat = steps_ref[...], seat_ref[0]
    ends = by_seat(seat, [b[...] for b in blocks])
    reach, reach_plane = jnp.exp(-steps * span), jnp.exp(-steps * (span * CREW))
    state = planes[-1][...]
    for plane in planes[-2::-1]:
        state = reach_plane * state + plane[...]
    states = [state]
    for end in ends[:-1]:
        states.append(reach * states[-1] + end)
    for out_ref, value in zip(outs, by_seat(seat, states)):
        out_ref[...] = value


def state_call(body, name, seat, steps, ends, arrays, out_count):
    modes, quarter = arrays[0].shape

    def owned(_, s):
        return (0, s[0])

    own = pl.BlockSpec((modes, quarter), owned)
    whole = pl.BlockSpec((modes, quarter), lambda _, s: (0, 0))
    shape = jax.ShapeDtypeStruct((modes, quarter), F32)
    return pl.pallas_call(
        body,
        grid_spec=pltpu.PrefetchScalarGridSpec(
            num_scalar_prefetch=1,
            grid=(1,),
            in_specs=[own, own] + [whole] * len(arrays),
            out_specs=[whole] * out_count,
        ),
        out_shape=[shape] * out_count,
        name=name,
    )(seat.reshape(1), steps, ends, *arrays)


def product_kernel(relayed_count, token_count, pick_ref, *refs):
    refs = list(refs)
    relayed = [refs.pop(0) for _ in range(relayed_count)]
    gathered_ref = None if relayed else refs.pop(0)
    tokens = [refs.pop(0) for _ in range(token_count)]
    kept_ref, sent_ref, total = refs[:3]
    step = pl.program_id(0)

    @pl.when(step == 0)
    def _():
        total[...] = jnp.zeros_like(total)

    if relayed:
        joined = refs[3]
        feat = relayed[0].shape[0]
        for plane in range(PLANES):
            for here in range(PLANES):

                @pl.when(pick_ref[1] == here)
                def _():
                    source = relayed[PLANES - 1 + here - plane]
                    joined[plane * feat : (plane + 1) * feat, :] = source[...]

        weights = joined[...]
    else:
        planes, feat, width = gathered_ref.shape
        weights = gathered_ref[...].reshape(planes * feat, width)
    for j, token in enumerate(tokens):
        total[j] += lax.dot_general(
            weights, token[...], (((1,), (1,)), ((), ())), preferred_element_type=F32
        )

    @pl.when(step == pl.num_programs(0) - 1)
    def _():
        middle = total.shape[1] // 2
        for side, outs in ((0, (kept_ref, sent_ref)), (1, (sent_ref, kept_ref))):

            @pl.when(pick_ref[0] == side)
            def _():
                outs[0][...] = total[:, :middle, :].astype(BF16)
                outs[1][...] = total[:, middle:, :].astype(BF16)


def project(picks, weights, tokens):
    rows, depth = tokens[0].shape
    width = 1024 if depth % 1024 == 0 else LANES
    relayed = weights if isinstance(weights, list) else []
    scratch = []
    if relayed:
        feat = relayed[0].shape[0]
        specs = [pl.BlockSpec((feat, width), lambda c, _: (0, c)) for _ in relayed]
        scratch = [pltpu.VMEM((PLANES * feat, width), BF16)]
    else:
        feat = weights.shape[1]
        specs = [pl.BlockSpec((PLANES, feat, width), lambda c, _: (0, 0, c))]
        weights = [weights]
    shape = (len(tokens), PLANES * feat // 2, rows)
    return pl.pallas_call(
        functools.partial(product_kernel, len(relayed), len(tokens)),
        grid_spec=pltpu.PrefetchScalarGridSpec(
            num_scalar_prefetch=1,
            grid=(depth // width,),
            in_specs=specs + [pl.BlockSpec((rows, width), lambda c, _: (0, c)) for _ in tokens],
            out_specs=[pl.BlockSpec(shape, lambda c, _: (0, 0, 0))] * 2,
            scratch_shapes=[pltpu.VMEM((len(tokens), PLANES * feat, rows), F32)] + scratch,
        ),
        out_shape=[jax.ShapeDtypeStruct(shape, BF16)] * 2,
        compiler_params=pltpu.CompilerParams(vmem_limit_bytes=VMEM_GRANT),
        cost_estimate=pl.CostEstimate(
            flops=1, bytes_accessed=4 * len(tokens) * rows * depth * 2 if relayed else 1,
            transcendentals=0,
        ),
        name="project",
    )(picks, *weights, *tokens)


def assemble_kernel(seat_ref, *refs):
    pieces, out_ref = refs[:-1], refs[-1]
    halves = PLANES // 2
    block = out_ref.shape[0] // halves
    feat = block // CREW
    for j in range(CREW):
        begin = 0
        for piece in pieces[j::CREW]:
            size = piece.shape[0] // halves
            for half in range(halves):
                at = half * block + (seat_ref[0] ^ j) * feat + begin
                at = pl.multiple_of(at, math.gcd(size, begin) if begin else size)
                out_ref[pl.ds(at, size), :] = piece[half * size : (half + 1) * size, :]
            begin += size


def assemble(seat, pieces):
    rows = pieces[0].shape[1]
    vmem = pl.BlockSpec(memory_space=pltpu.VMEM)
    return pl.pallas_call(
        assemble_kernel,
        in_specs=[pl.BlockSpec(memory_space=pltpu.SMEM)] + [vmem] * len(pieces),
        out_specs=vmem,
        out_shape=jax.ShapeDtypeStruct((sum(p.shape[0] for p in pieces), rows), BF16),
        compiler_params=pltpu.CompilerParams(vmem_limit_bytes=VMEM_GRANT),
        name="assemble",
    )(seat.reshape(1), *pieces)


def tails_kernel(q_ref, k_ref, v_ref, out_ref):
    lead = LEAD
    for which, ref in enumerate((q_ref, k_ref, v_ref)):
        rows = ref[...].astype(F32)
        out_ref[which * lead : (which + 1) * lead, :] = rows[rows.shape[0] - lead :]
    out_ref[3 * lead :, :] = jnp.zeros((out_ref.shape[0] - 3 * lead, out_ref.shape[1]), F32)


def gather_rims(q_proj, k_proj, v_proj):
    size = lax.axis_size("context")
    rows, chan_count = q_proj.shape
    last = pl.BlockSpec((16, chan_count), lambda i: (rows // 16 - 1, 0))
    tails = pl.pallas_call(
        tails_kernel,
        grid=(1,),
        in_specs=[last] * 3,
        out_specs=pl.BlockSpec((SEGS, chan_count), lambda i: (0, 0)),
        out_shape=jax.ShapeDtypeStruct((SEGS, chan_count), F32),
        compiler_params=pltpu.CompilerParams(vmem_limit_bytes=VMEM_GRANT),
        name="tails",
    )(q_proj, k_proj, v_proj)
    return lax.ppermute(tails, "context", [(i, i + 1) for i in range(size - 1)])


def per_device(q_proj, k_proj, v_proj, short_filter, residue, decay_rate, out_weight):
    place, size = lax.axis_index("context"), lax.axis_size("context")

    rows = q_proj.shape[0]
    rims = gather_rims(q_proj, k_proj, v_proj)
    q_feat, y_local, carry, ends = local_rows(
        q_proj, k_proj, v_proj, rims, short_filter, residue, decay_rate
    )
    gathered = lax.all_gather(ends, "context")
    gaps = (place - 1 - jnp.arange(size))[:, None, None]
    reach = jnp.exp(-(decay_rate / float(rows * size))[None] * (gaps * rows).astype(F32))
    incoming = jnp.sum(jnp.where(gaps >= 0, reach * gathered, 0.0), axis=0)
    gated = gate_rows(
        q_feat, y_local, carry, incoming[None], decay_rate, residue, jnp.int32(0)
    )
    partial_terms = lax.dot_general(
        lax.all_gather(out_weight, "context", axis=0, tiled=True),
        gated,
        (((1,), (1,)), ((), ())),
        preferred_element_type=F32,
    )
    return lax.psum_scatter(
        partial_terms.astype(BF16), "tensor", scatter_dimension=0, tiled=True
    )


def swap(block, mask):
    size = lax.axis_size("context")
    return lax.ppermute(block, "context", [(i, i ^ mask) for i in range(size)])


def shift(block, distance):
    size = lax.axis_size("context")
    moves = [(i, i + distance) for i in range(size) if 0 <= i + distance < size]
    return lax.ppermute(block, "context", moves)


def per_device_planes(q_proj, k_proj, v_proj, short_filter, residue, decay_rate, out_weight):
    size = lax.axis_size("context")
    seat = lax.axis_index("context") % CREW
    side = lax.axis_index("tensor")
    rows, feat = q_proj.shape[0], out_weight.shape[0]
    quarter = q_proj.shape[1] // CREW
    span = float(rows)
    steps = decay_rate / (span * size)
    columns = [[p * CREW + s for p in range(PLANES)] for s in range(CREW)]
    cut = feat * 7 // 8
    most, k_proj = lax.optimization_barrier((out_weight[:cut], k_proj))
    gathered = lax.all_gather(most, "context", axis_index_groups=columns)
    picks = jnp.stack([side, lax.axis_index("context") // CREW]).astype(jnp.int32)

    def hops(block, moves):
        return lax.ppermute(
            block, "context",
            [(a * CREW + s, b * CREW + s) for a, b in moves for s in range(CREW)],
        )

    rims = gather_rims(q_proj, k_proj, v_proj)
    q_feat, y_local, carry, ends = local_rows(
        q_proj, k_proj, v_proj, rims, short_filter, residue, decay_rate
    )
    blocks = [
        swap(lax.dynamic_slice_in_dim(ends, (seat ^ j) * quarter, quarter, 1), j)
        for j in range(1, CREW)
    ]
    total = state_call(
        functools.partial(plane_kernel, span), "plane_state", seat, steps, ends, blocks, 1
    )[0]
    planes = [shift(total, hop * CREW) for hop in range(1, PLANES)]
    planes, own = lax.optimization_barrier((planes, out_weight[cut:]))
    up1, down1 = shift(own, CREW), shift(own, -CREW)
    mine = state_call(
        functools.partial(incoming_kernel, span), "incoming_state",
        seat, steps, ends, blocks + planes, CREW,
    )
    incoming = jnp.stack([mine[0]] + [swap(mine[j], j) for j in range(1, CREW)])
    gated = gate_rows(q_feat, y_local, carry, incoming, decay_rate, residue, seat)
    beside = swap(gated, 1)
    far, up1, down1 = lax.optimization_barrier((swap(gated, 2), up1, down1))
    up2, down2 = hops(up1, [(1, 2), (2, 3)]), hops(down1, [(2, 1), (1, 0)])

    def added(kept, arrived):
        return [
            (kept[at].astype(F32) + arrived[at].astype(F32)).astype(BF16)
            for at in range(kept.shape[0])
        ]

    def deal(parts, members):
        return [swap(part, j) if j else part for part, j in zip(parts, members)]

    def finish(kept, arrived, members):
        return deal(added(kept, arrived), members)

    near, beyond = [gated, beside], [far, swap(far, 1)]
    kept, sent = project(picks, gathered, beyond)
    kept, near[0], up2, down2 = lax.optimization_barrier((kept, near[0], up2, down2))
    up3, down3 = hops(up2, [(2, 3)]), hops(down2, [(1, 0)])
    far_pieces = added(kept, lax.ppermute(sent, "tensor", [(0, 1), (1, 0)]))
    kept, sent = project(picks, gathered, near)
    near_arrived = lax.ppermute(sent, "tensor", [(0, 1), (1, 0)])
    kept, up3, down3, far_pieces = lax.optimization_barrier((kept, up3, down3, far_pieces))
    relayed = [down3, down2, down1, own, up1, up2, up3]
    last_kept, last_sent = project(picks, relayed, near + beyond)
    pieces = finish(kept, near_arrived, (0, 1)) + deal(far_pieces, (2, 3))
    last_arrived = lax.ppermute(last_sent, "tensor", [(0, 1), (1, 0)])
    pieces += finish(last_kept, last_arrived, (0, 1, 2, 3))
    return assemble(seat, pieces)


def solution(mesh):
    planes = mesh.shape["tensor"] == 2 and mesh.shape["context"] == CREW * PLANES
    return jax.shard_map(
        per_device_planes if planes else per_device,
        mesh=mesh,
        in_specs=(
            P("context", "tensor"),
            P("context", "tensor"),
            P("context", "tensor"),
            P(None, None, "tensor"),
            P(None, "tensor"),
            P(None, "tensor"),
            P("context", "tensor"),
        ),
        out_specs=P("tensor", "context"),
        check_vma=False,
    )
```

```python
import functools
import math

import jax
import jax.numpy as jnp
from jax import lax
from jax.experimental import pallas as pl
from jax.experimental.pallas import tpu as pltpu
from jax.sharding import PartitionSpec as P

LANES = 128
SEGS = 8
CREW = 4
LEAD = 2
PLANES = 4
VMEM_GRANT = 56 * 2**20
F32 = jnp.float32
BF16 = jnp.bfloat16


def lane_block(chan_count):
    for width in (1024, 512):
        if chan_count % (CREW * width) == 0:
            return width
    return LANES


def tree_sum(terms):
    terms = list(terms)
    while len(terms) > 1:
        paired = [terms[i] + terms[i + 1] for i in range(0, len(terms) - 1, 2)]
        if len(terms) % 2:
            paired.append(terms[-1])
        terms = paired
    return terms[0]


def spread(row):
    return jnp.broadcast_to(row, (SEGS, LANES))


def local_kernel(
    total, q_ref, k_ref, v_ref, rim_ref, filter_ref, decay_ref, residue_ref,
    qf_ref, y_ref, carry_ref, end_ref, shifted, signal,
):
    rows, width = q_ref.shape
    modes = decay_ref.shape[0]
    length = rows // SEGS
    kinds, tap_count, groups = filter_ref.shape
    group_width = pl.num_programs(0) * width // groups
    begin, count = 0, groups
    if groups % LANES == 0 and LANES * group_width % width == 0:
        begin, count = pl.program_id(0) * width // (LANES * group_width) * LANES, LANES
        begin = pl.multiple_of(begin, LANES)
    chan = pl.program_id(0) * width + lax.broadcasted_iota(jnp.int32, (count, width), 1)
    first = (begin + lax.broadcasted_iota(jnp.int32, (count, width), 0)) * group_width
    member = ((chan >= first) & (chan < first + group_width)).astype(BF16)
    filters = [filter_ref[kind, :, pl.ds(begin, count)].astype(F32) for kind in range(kinds)]
    taps = jnp.dot(
        jnp.concatenate(filters, axis=0).astype(BF16), member, preferred_element_type=F32
    )
    lead = LEAD

    def short_pass(which, ref, lanes):
        pad = shifted.at[which]
        pad[SEGS : SEGS + rows, :] = ref[:, lanes].astype(F32)
        pad[SEGS - lead : SEGS, :] = rim_ref[which * lead : (which + 1) * lead, lanes]
        running = None
        for offset in range(tap_count):
            row = which * tap_count + offset
            tap = taps[row : row + 1, lanes]
            term = tap * pad[SEGS - offset : SEGS - offset + rows, :]
            running = term if running is None else running + term
        return running.astype(BF16)

    for block in range(width // LANES):
        lanes = slice(block * LANES, (block + 1) * LANES)
        qf_ref[:, lanes] = short_pass(0, q_ref, lanes)
        k_feat = short_pass(1, k_ref, lanes).astype(F32)
        v_feat = short_pass(2, v_ref, lanes).astype(F32)
        signal[block] = (k_feat * v_feat).astype(BF16).astype(F32)

    seg = lax.broadcasted_iota(jnp.int32, (SEGS, LANES), 0)
    for block in range(width // LANES):
        lanes = slice(block * LANES, (block + 1) * LANES)
        steps = decay_ref[:, lanes] / total
        decays = jnp.exp(-steps)
        scales = residue_ref[:, lanes] * jnp.sqrt(2.0 * steps)
        decay = [spread(decays[m : m + 1]) for m in range(modes)]
        scale = [spread(scales[m : m + 1]) for m in range(modes)]

        def advance(i, state):
            x = signal[block, pl.ds(i, SEGS, stride=length), :]
            state = tuple(d * s + x for d, s in zip(decay, state))
            y_ref[i, :, lanes] = tree_sum(c * s for c, s in zip(scale, state))
            return state

        zero = jnp.zeros((SEGS, LANES), F32)
        state = lax.fori_loop(0, length, advance, (zero,) * modes, unroll=4)
        for m in range(modes):
            ends = state[m]
            for hop in (1, 2, 4):
                factor = spread(jnp.exp(-steps[m : m + 1] * float(length * hop)))
                ends = ends + factor * jnp.where(seg >= hop, pltpu.roll(ends, hop, 0), 0.0)
            end_ref[m : m + 1, lanes] = ends[SEGS - 1 : SEGS]
            carry_ref[m, :, lanes] = jnp.where(seg >= 1, pltpu.roll(ends, 1, 0), 0.0)


def gate_kernel(
    total, seat_ref, qf_ref, y_ref, carry_ref, incoming_ref, decay_ref, residue_ref,
    out_ref, mixed,
):
    rows, width = qf_ref.shape
    modes = decay_ref.shape[0]
    length = rows // SEGS
    begin = (lax.broadcasted_iota(jnp.int32, (SEGS, LANES), 0) * length).astype(F32)
    for block in range(width // LANES):
        lanes = slice(block * LANES, (block + 1) * LANES)
        steps = decay_ref[:, lanes] / total
        decays = jnp.exp(-steps)
        weights = residue_ref[:, lanes] * jnp.sqrt(2.0 * steps) * decays
        decay = [spread(decays[m : m + 1]) for m in range(modes)]
        tail = []
        for m in range(modes):
            reach = jnp.exp(-spread(steps[m : m + 1]) * begin)
            held = carry_ref[m, :, lanes] + reach * spread(incoming_ref[m : m + 1, lanes])
            tail.append(spread(weights[m : m + 1]) * held)

        def advance(i, tail):
            mixed[block, pl.ds(i, SEGS, stride=length), :] = y_ref[i, :, lanes] + tree_sum(tail)
            return tuple(d * s for d, s in zip(decay, tail))

        lax.fori_loop(0, length, advance, tuple(tail), unroll=4)
    for block in range(width // LANES):
        lanes = slice(block * LANES, (block + 1) * LANES)
        out_ref[:, lanes] = (qf_ref[:, lanes].astype(F32) * mixed[block]).astype(BF16)


def column_call(body, name, arrays, outs, scratch, width, chan_count):
    def spec(shape):
        if shape[-1] != chan_count:
            return pl.BlockSpec(shape, lambda c: (0,) * len(shape))
        return pl.BlockSpec(shape[:-1] + (width,), lambda c: (0,) * (len(shape) - 1) + (c,))

    return pl.pallas_call(
        body,
        grid=(chan_count // width,),
        in_specs=[spec(a.shape) for a in arrays],
        out_specs=[spec(o.shape) for o in outs],
        out_shape=outs,
        scratch_shapes=scratch,
        compiler_params=pltpu.CompilerParams(vmem_limit_bytes=VMEM_GRANT),
        name=name,
    )(*arrays)


def local_rows(q_proj, k_proj, v_proj, rims, short_filter, residue, decay_rate):
    rows, chan_count = q_proj.shape
    modes = decay_rate.shape[0]
    total = float(rows * lax.axis_size("context"))
    width = lane_block(chan_count)
    return column_call(
        functools.partial(local_kernel, total), "local_pass",
        (q_proj, k_proj, v_proj, rims, short_filter, decay_rate, residue),
        [
            jax.ShapeDtypeStruct((rows, chan_count), BF16),
            jax.ShapeDtypeStruct((rows // SEGS, SEGS, chan_count), F32),
            jax.ShapeDtypeStruct((modes, SEGS, chan_count), F32),
            jax.ShapeDtypeStruct((modes, chan_count), F32),
        ],
        [
            pltpu.VMEM((3, rows + SEGS, LANES), F32),
            pltpu.VMEM((width // LANES, rows, LANES), F32),
        ],
        width, chan_count,
    )


def gate_rows(q_feat, y_local, carry, incoming, decay_rate, residue, seat):
    rows, chan_count = q_feat.shape
    modes = decay_rate.shape[0]
    total = float(rows * lax.axis_size("context"))
    width = lane_block(chan_count)
    per_part = incoming.shape[2] // width

    def cols(height):
        return pl.BlockSpec((height, width), lambda c, s: (0, c))

    return pl.pallas_call(
        functools.partial(gate_kernel, total),
        grid_spec=pltpu.PrefetchScalarGridSpec(
            num_scalar_prefetch=1,
            grid=(chan_count // width,),
            in_specs=[
                cols(rows),
                pl.BlockSpec((rows // SEGS, SEGS, width), lambda c, s: (0, 0, c)),
                pl.BlockSpec((modes, SEGS, width), lambda c, s: (0, 0, c)),
                pl.BlockSpec(
                    (None, modes, width), lambda c, s: (s[0] ^ (c // per_part), 0, c % per_part)
                ),
                cols(modes),
                cols(modes),
            ],
            out_specs=cols(rows),
            scratch_shapes=[pltpu.VMEM((width // LANES, rows, LANES), F32)],
        ),
        out_shape=jax.ShapeDtypeStruct((rows, chan_count), BF16),
        compiler_params=pltpu.CompilerParams(vmem_limit_bytes=VMEM_GRANT),
        name="gate_pass",
    )(seat.reshape(1), q_feat, y_local, carry, incoming, decay_rate, residue)


def by_seat(seat, blocks):
    ordered = []
    for k in range(CREW):
        value = blocks[0]
        for j in range(1, CREW):
            value = jnp.where((seat ^ k) == j, blocks[j], value)
        ordered.append(value)
    return ordered


def plane_kernel(span, seat_ref, steps_ref, *refs):
    blocks, out_ref = refs[:CREW], refs[CREW]
    reach = jnp.exp(-steps_ref[...] * span)
    ends = by_seat(seat_ref[0], [b[...] for b in blocks])
    state = ends[0]
    for end in ends[1:]:
        state = reach * state + end
    out_ref[...] = state


def incoming_kernel(span, seat_ref, steps_ref, *refs):
    blocks, planes = refs[:CREW], refs[CREW : CREW + PLANES - 1]
    outs = refs[CREW + PLANES - 1 :]
    steps, seat = steps_ref[...], seat_ref[0]
    ends = by_seat(seat, [b[...] for b in blocks])
    reach, reach_plane = jnp.exp(-steps * span), jnp.exp(-steps * (span * CREW))
    state = planes[-1][...]
    for plane in planes[-2::-1]:
        state = reach_plane * state + plane[...]
    states = [state]
    for end in ends[:-1]:
        states.append(reach * states[-1] + end)
    for out_ref, value in zip(outs, by_seat(seat, states)):
        out_ref[...] = value


def state_call(body, name, seat, steps, ends, arrays, out_count):
    modes, quarter = arrays[0].shape

    def owned(_, s):
        return (0, s[0])

    own = pl.BlockSpec((modes, quarter), owned)
    whole = pl.BlockSpec((modes, quarter), lambda _, s: (0, 0))
    shape = jax.ShapeDtypeStruct((modes, quarter), F32)
    return pl.pallas_call(
        body,
        grid_spec=pltpu.PrefetchScalarGridSpec(
            num_scalar_prefetch=1,
            grid=(1,),
            in_specs=[own, own] + [whole] * len(arrays),
            out_specs=[whole] * out_count,
        ),
        out_shape=[shape] * out_count,
        name=name,
    )(seat.reshape(1), steps, ends, *arrays)


def product_kernel(relayed_count, token_count, pick_ref, *refs):
    refs = list(refs)
    relayed = [refs.pop(0) for _ in range(relayed_count)]
    gathered_ref = None if relayed else refs.pop(0)
    tokens = [refs.pop(0) for _ in range(token_count)]
    kept_ref, sent_ref, total = refs[:3]
    step = pl.program_id(0)

    @pl.when(step == 0)
    def _():
        total[...] = jnp.zeros_like(total)

    if relayed:
        joined = refs[3]
        feat = relayed[0].shape[0]
        for plane in range(PLANES):
            for here in range(PLANES):

                @pl.when(pick_ref[1] == here)
                def _():
                    source = relayed[PLANES - 1 + here - plane]
                    joined[plane * feat : (plane + 1) * feat, :] = source[...]

        weights = joined[...]
    else:
        planes, feat, width = gathered_ref.shape
        weights = gathered_ref[...].reshape(planes * feat, width)
    for j, token in enumerate(tokens):
        total[j] += lax.dot_general(
            weights, token[...], (((1,), (1,)), ((), ())), preferred_element_type=F32
        )

    @pl.when(step == pl.num_programs(0) - 1)
    def _():
        middle = total.shape[1] // 2
        for side, outs in ((0, (kept_ref, sent_ref)), (1, (sent_ref, kept_ref))):

            @pl.when(pick_ref[0] == side)
            def _():
                outs[0][...] = total[:, :middle, :].astype(BF16)
                outs[1][...] = total[:, middle:, :].astype(BF16)


def project(picks, weights, tokens):
    rows, depth = tokens[0].shape
    width = 1024 if depth % 1024 == 0 else LANES
    relayed = weights if isinstance(weights, list) else []
    scratch = []
    if relayed:
        feat = relayed[0].shape[0]
        specs = [pl.BlockSpec((feat, width), lambda c, _: (0, c)) for _ in relayed]
        scratch = [pltpu.VMEM((PLANES * feat, width), BF16)]
    else:
        feat = weights.shape[1]
        specs = [pl.BlockSpec((PLANES, feat, width), lambda c, _: (0, 0, c))]
        weights = [weights]
    shape = (len(tokens), PLANES * feat // 2, rows)
    return pl.pallas_call(
        functools.partial(product_kernel, len(relayed), len(tokens)),
        grid_spec=pltpu.PrefetchScalarGridSpec(
            num_scalar_prefetch=1,
            grid=(depth // width,),
            in_specs=specs + [pl.BlockSpec((rows, width), lambda c, _: (0, c)) for _ in tokens],
            out_specs=[pl.BlockSpec(shape, lambda c, _: (0, 0, 0))] * 2,
            scratch_shapes=[pltpu.VMEM((len(tokens), PLANES * feat, rows), F32)] + scratch,
        ),
        out_shape=[jax.ShapeDtypeStruct(shape, BF16)] * 2,
        compiler_params=pltpu.CompilerParams(vmem_limit_bytes=VMEM_GRANT),
        cost_estimate=pl.CostEstimate(flops=1, bytes_accessed=1, transcendentals=0),
        name="project",
    )(picks, *weights, *tokens)


def assemble_kernel(seat_ref, *refs):
    pieces, out_ref = refs[:-1], refs[-1]
    halves = PLANES // 2
    block = out_ref.shape[0] // halves
    feat = block // CREW
    for j in range(CREW):
        begin = 0
        for piece in pieces[j::CREW]:
            size = piece.shape[0] // halves
            for half in range(halves):
                at = half * block + (seat_ref[0] ^ j) * feat + begin
                at = pl.multiple_of(at, math.gcd(size, begin) if begin else size)
                out_ref[pl.ds(at, size), :] = piece[half * size : (half + 1) * size, :]
            begin += size


def assemble(seat, pieces):
    rows = pieces[0].shape[1]
    vmem = pl.BlockSpec(memory_space=pltpu.VMEM)
    return pl.pallas_call(
        assemble_kernel,
        in_specs=[pl.BlockSpec(memory_space=pltpu.SMEM)] + [vmem] * len(pieces),
        out_specs=vmem,
        out_shape=jax.ShapeDtypeStruct((sum(p.shape[0] for p in pieces), rows), BF16),
        compiler_params=pltpu.CompilerParams(vmem_limit_bytes=VMEM_GRANT),
        name="assemble",
    )(seat.reshape(1), *pieces)


def tails_kernel(q_ref, k_ref, v_ref, out_ref):
    lead = LEAD
    for which, ref in enumerate((q_ref, k_ref, v_ref)):
        rows = ref[...].astype(F32)
        out_ref[which * lead : (which + 1) * lead, :] = rows[rows.shape[0] - lead :]
    out_ref[3 * lead :, :] = jnp.zeros((out_ref.shape[0] - 3 * lead, out_ref.shape[1]), F32)


def gather_rims(q_proj, k_proj, v_proj):
    size = lax.axis_size("context")
    rows, chan_count = q_proj.shape
    last = pl.BlockSpec((16, chan_count), lambda i: (rows // 16 - 1, 0))
    tails = pl.pallas_call(
        tails_kernel,
        grid=(1,),
        in_specs=[last] * 3,
        out_specs=pl.BlockSpec((SEGS, chan_count), lambda i: (0, 0)),
        out_shape=jax.ShapeDtypeStruct((SEGS, chan_count), F32),
        compiler_params=pltpu.CompilerParams(vmem_limit_bytes=VMEM_GRANT),
        name="tails",
    )(q_proj, k_proj, v_proj)
    return lax.ppermute(tails, "context", [(i, i + 1) for i in range(size - 1)])


def per_device(q_proj, k_proj, v_proj, short_filter, residue, decay_rate, out_weight):
    place, size = lax.axis_index("context"), lax.axis_size("context")

    rows = q_proj.shape[0]
    rims = gather_rims(q_proj, k_proj, v_proj)
    q_feat, y_local, carry, ends = local_rows(
        q_proj, k_proj, v_proj, rims, short_filter, residue, decay_rate
    )
    gathered = lax.all_gather(ends, "context")
    gaps = (place - 1 - jnp.arange(size))[:, None, None]
    reach = jnp.exp(-(decay_rate / float(rows * size))[None] * (gaps * rows).astype(F32))
    incoming = jnp.sum(jnp.where(gaps >= 0, reach * gathered, 0.0), axis=0)
    gated = gate_rows(
        q_feat, y_local, carry, incoming[None], decay_rate, residue, jnp.int32(0)
    )
    partial_terms = lax.dot_general(
        lax.all_gather(out_weight, "context", axis=0, tiled=True),
        gated,
        (((1,), (1,)), ((), ())),
        preferred_element_type=F32,
    )
    return lax.psum_scatter(
        partial_terms.astype(BF16), "tensor", scatter_dimension=0, tiled=True
    )


def swap(block, mask):
    size = lax.axis_size("context")
    return lax.ppermute(block, "context", [(i, i ^ mask) for i in range(size)])


def shift(block, distance):
    size = lax.axis_size("context")
    moves = [(i, i + distance) for i in range(size) if 0 <= i + distance < size]
    return lax.ppermute(block, "context", moves)


def per_device_planes(q_proj, k_proj, v_proj, short_filter, residue, decay_rate, out_weight):
    size = lax.axis_size("context")
    seat = lax.axis_index("context") % CREW
    side = lax.axis_index("tensor")
    rows, feat = q_proj.shape[0], out_weight.shape[0]
    quarter = q_proj.shape[1] // CREW
    span = float(rows)
    steps = decay_rate / (span * size)
    columns = [[p * CREW + s for p in range(PLANES)] for s in range(CREW)]
    cut = feat * 13 // 16
    most, k_proj = lax.optimization_barrier((out_weight[:cut], k_proj))
    gathered = lax.all_gather(most, "context", axis_index_groups=columns)
    picks = jnp.stack([side, lax.axis_index("context") // CREW]).astype(jnp.int32)

    def hops(block, moves):
        return lax.ppermute(
            block, "context",
            [(a * CREW + s, b * CREW + s) for a, b in moves for s in range(CREW)],
        )

    rims = gather_rims(q_proj, k_proj, v_proj)
    q_feat, y_local, carry, ends = local_rows(
        q_proj, k_proj, v_proj, rims, short_filter, residue, decay_rate
    )
    blocks = [
        swap(lax.dynamic_slice_in_dim(ends, (seat ^ j) * quarter, quarter, 1), j)
        for j in range(1, CREW)
    ]
    total = state_call(
        functools.partial(plane_kernel, span), "plane_state", seat, steps, ends, blocks, 1
    )[0]
    planes = [shift(total, hop * CREW) for hop in range(1, PLANES)]
    planes, own = lax.optimization_barrier((planes, out_weight[cut:]))
    up1, down1 = shift(own, CREW), shift(own, -CREW)
    mine = state_call(
        functools.partial(incoming_kernel, span), "incoming_state",
        seat, steps, ends, blocks + planes, CREW,
    )
    incoming = jnp.stack([mine[0]] + [swap(mine[j], j) for j in range(1, CREW)])
    gated = gate_rows(q_feat, y_local, carry, incoming, decay_rate, residue, seat)
    far = swap(gated, 2)
    beside, up1, down1 = lax.optimization_barrier((swap(gated, 1), up1, down1))
    up2, down2 = hops(up1, [(1, 2), (2, 3)]), hops(down1, [(2, 1), (1, 0)])

    def crossed(sent):
        return lax.ppermute(sent, "tensor", [(0, 1), (1, 0)])

    def finish(kept, arrived, members):
        sums = [
            (kept[at].astype(F32) + arrived[at].astype(F32)).astype(BF16)
            for at in range(len(members))
        ]
        return [swap(part, j) if j else part for part, j in zip(sums, members)]

    near = [gated, beside]
    gathered, up2, down2 = lax.optimization_barrier((gathered, up2, down2))
    kept, sent = project(picks, gathered, near)
    kept, far = lax.optimization_barrier((kept, far))
    kept, last_up, last_down = lax.optimization_barrier((kept, up2, down2))
    up3, down3 = hops(last_up, [(2, 3)]), hops(last_down, [(1, 0)])
    near_kept, near_arrived = kept, crossed(sent)
    beyond = [far, swap(far, 1)]
    kept, sent = project(picks, gathered, beyond)
    arrived = crossed(sent)
    kept, up3, down3 = lax.optimization_barrier((kept, up3, down3))
    relayed = [down3, down2, down1, own, up1, up2, up3]
    last_kept, last_sent = project(picks, relayed, near + beyond)
    last_kept, near_arrived = lax.optimization_barrier((last_kept, near_arrived))
    last_arrived = crossed(last_sent)
    pieces = finish(near_kept, near_arrived, (0, 1)) + finish(kept, arrived, (2, 3))
    pieces += finish(last_kept, last_arrived, (0, 1, 2, 3))
    return assemble(seat, pieces)


def solution(mesh):
    planes = mesh.shape["tensor"] == 2 and mesh.shape["context"] == CREW * PLANES
    return jax.shard_map(
        per_device_planes if planes else per_device,
        mesh=mesh,
        in_specs=(
            P("context", "tensor"),
            P("context", "tensor"),
            P("context", "tensor"),
            P(None, None, "tensor"),
            P(None, "tensor"),
            P(None, "tensor"),
            P("context", "tensor"),
        ),
        out_specs=P("tensor", "context"),
        check_vma=False,
    )
```

```python
import functools
import math

import jax
import jax.numpy as jnp
from jax import lax
from jax.experimental import pallas as pl
from jax.experimental.pallas import tpu as pltpu
from jax.sharding import PartitionSpec as P

LANES = 128
SEGS = 8
CREW = 4
LEAD = 2
PLANES = 4
VMEM_GRANT = 56 * 2**20
F32 = jnp.float32
BF16 = jnp.bfloat16


def lane_block(chan_count):
    for width in (1024, 512):
        if chan_count % (CREW * width) == 0:
            return width
    return LANES


def tree_sum(terms):
    terms = list(terms)
    while len(terms) > 1:
        paired = [terms[i] + terms[i + 1] for i in range(0, len(terms) - 1, 2)]
        if len(terms) % 2:
            paired.append(terms[-1])
        terms = paired
    return terms[0]


def spread(row):
    return jnp.broadcast_to(row, (SEGS, LANES))


def local_kernel(
    total, q_ref, k_ref, v_ref, rim_ref, filter_ref, decay_ref, residue_ref,
    qf_ref, y_ref, carry_ref, end_ref, shifted, signal,
):
    rows, width = q_ref.shape
    modes = decay_ref.shape[0]
    length = rows // SEGS
    kinds, tap_count, groups = filter_ref.shape
    group_width = pl.num_programs(0) * width // groups
    begin, count = 0, groups
    if groups % LANES == 0 and LANES * group_width % width == 0:
        begin, count = pl.program_id(0) * width // (LANES * group_width) * LANES, LANES
        begin = pl.multiple_of(begin, LANES)
    chan = pl.program_id(0) * width + lax.broadcasted_iota(jnp.int32, (count, width), 1)
    first = (begin + lax.broadcasted_iota(jnp.int32, (count, width), 0)) * group_width
    member = ((chan >= first) & (chan < first + group_width)).astype(BF16)
    filters = [filter_ref[kind, :, pl.ds(begin, count)].astype(F32) for kind in range(kinds)]
    taps = jnp.dot(
        jnp.concatenate(filters, axis=0).astype(BF16), member, preferred_element_type=F32
    )
    lead = LEAD

    def short_pass(which, ref, lanes):
        pad = shifted.at[which]
        pad[SEGS : SEGS + rows, :] = ref[:, lanes].astype(F32)
        pad[SEGS - lead : SEGS, :] = rim_ref[which * lead : (which + 1) * lead, lanes]
        running = None
        for offset in range(tap_count):
            row = which * tap_count + offset
            tap = taps[row : row + 1, lanes]
            term = tap * pad[SEGS - offset : SEGS - offset + rows, :]
            running = term if running is None else running + term
        return running.astype(BF16)

    for block in range(width // LANES):
        lanes = slice(block * LANES, (block + 1) * LANES)
        qf_ref[:, lanes] = short_pass(0, q_ref, lanes)
        k_feat = short_pass(1, k_ref, lanes).astype(F32)
        v_feat = short_pass(2, v_ref, lanes).astype(F32)
        signal[block] = (k_feat * v_feat).astype(BF16).astype(F32)

    seg = lax.broadcasted_iota(jnp.int32, (SEGS, LANES), 0)
    for block in range(width // LANES):
        lanes = slice(block * LANES, (block + 1) * LANES)
        steps = decay_ref[:, lanes] / total
        decays = jnp.exp(-steps)
        scales = residue_ref[:, lanes] * jnp.sqrt(2.0 * steps)
        decay = [spread(decays[m : m + 1]) for m in range(modes)]
        scale = [spread(scales[m : m + 1]) for m in range(modes)]

        def advance(i, state):
            x = signal[block, pl.ds(i, SEGS, stride=length), :]
            state = tuple(d * s + x for d, s in zip(decay, state))
            y_ref[i, :, lanes] = tree_sum(c * s for c, s in zip(scale, state))
            return state

        zero = jnp.zeros((SEGS, LANES), F32)
        state = lax.fori_loop(0, length, advance, (zero,) * modes, unroll=4)
        for m in range(modes):
            ends = state[m]
            for hop in (1, 2, 4):
                factor = spread(jnp.exp(-steps[m : m + 1] * float(length * hop)))
                ends = ends + factor * jnp.where(seg >= hop, pltpu.roll(ends, hop, 0), 0.0)
            end_ref[m : m + 1, lanes] = ends[SEGS - 1 : SEGS]
            carry_ref[m, :, lanes] = jnp.where(seg >= 1, pltpu.roll(ends, 1, 0), 0.0)


def gate_kernel(
    total, seat_ref, qf_ref, y_ref, carry_ref, incoming_ref, decay_ref, residue_ref,
    out_ref, mixed,
):
    rows, width = qf_ref.shape
    modes = decay_ref.shape[0]
    length = rows // SEGS
    begin = (lax.broadcasted_iota(jnp.int32, (SEGS, LANES), 0) * length).astype(F32)
    for block in range(width // LANES):
        lanes = slice(block * LANES, (block + 1) * LANES)
        steps = decay_ref[:, lanes] / total
        decays = jnp.exp(-steps)
        weights = residue_ref[:, lanes] * jnp.sqrt(2.0 * steps) * decays
        decay = [spread(decays[m : m + 1]) for m in range(modes)]
        tail = []
        for m in range(modes):
            reach = jnp.exp(-spread(steps[m : m + 1]) * begin)
            held = carry_ref[m, :, lanes] + reach * spread(incoming_ref[m : m + 1, lanes])
            tail.append(spread(weights[m : m + 1]) * held)

        def advance(i, tail):
            mixed[block, pl.ds(i, SEGS, stride=length), :] = y_ref[i, :, lanes] + tree_sum(tail)
            return tuple(d * s for d, s in zip(decay, tail))

        lax.fori_loop(0, length, advance, tuple(tail), unroll=4)
    for block in range(width // LANES):
        lanes = slice(block * LANES, (block + 1) * LANES)
        out_ref[:, lanes] = (qf_ref[:, lanes].astype(F32) * mixed[block]).astype(BF16)


def column_call(body, name, arrays, outs, scratch, width, chan_count):
    def spec(shape):
        if shape[-1] != chan_count:
            return pl.BlockSpec(shape, lambda c: (0,) * len(shape))
        return pl.BlockSpec(shape[:-1] + (width,), lambda c: (0,) * (len(shape) - 1) + (c,))

    return pl.pallas_call(
        body,
        grid=(chan_count // width,),
        in_specs=[spec(a.shape) for a in arrays],
        out_specs=[spec(o.shape) for o in outs],
        out_shape=outs,
        scratch_shapes=scratch,
        compiler_params=pltpu.CompilerParams(vmem_limit_bytes=VMEM_GRANT),
        name=name,
    )(*arrays)


def local_rows(q_proj, k_proj, v_proj, rims, short_filter, residue, decay_rate):
    rows, chan_count = q_proj.shape
    modes = decay_rate.shape[0]
    total = float(rows * lax.axis_size("context"))
    width = lane_block(chan_count)
    return column_call(
        functools.partial(local_kernel, total), "local_pass",
        (q_proj, k_proj, v_proj, rims, short_filter, decay_rate, residue),
        [
            jax.ShapeDtypeStruct((rows, chan_count), BF16),
            jax.ShapeDtypeStruct((rows // SEGS, SEGS, chan_count), F32),
            jax.ShapeDtypeStruct((modes, SEGS, chan_count), F32),
            jax.ShapeDtypeStruct((modes, chan_count), F32),
        ],
        [
            pltpu.VMEM((3, rows + SEGS, LANES), F32),
            pltpu.VMEM((width // LANES, rows, LANES), F32),
        ],
        width, chan_count,
    )


def gate_rows(q_feat, y_local, carry, incoming, decay_rate, residue, seat):
    rows, chan_count = q_feat.shape
    modes = decay_rate.shape[0]
    total = float(rows * lax.axis_size("context"))
    width = lane_block(chan_count)
    per_part = incoming.shape[2] // width

    def cols(height):
        return pl.BlockSpec((height, width), lambda c, s: (0, c))

    return pl.pallas_call(
        functools.partial(gate_kernel, total),
        grid_spec=pltpu.PrefetchScalarGridSpec(
            num_scalar_prefetch=1,
            grid=(chan_count // width,),
            in_specs=[
                cols(rows),
                pl.BlockSpec((rows // SEGS, SEGS, width), lambda c, s: (0, 0, c)),
                pl.BlockSpec((modes, SEGS, width), lambda c, s: (0, 0, c)),
                pl.BlockSpec(
                    (None, modes, width), lambda c, s: (s[0] ^ (c // per_part), 0, c % per_part)
                ),
                cols(modes),
                cols(modes),
            ],
            out_specs=cols(rows),
            scratch_shapes=[pltpu.VMEM((width // LANES, rows, LANES), F32)],
        ),
        out_shape=jax.ShapeDtypeStruct((rows, chan_count), BF16),
        compiler_params=pltpu.CompilerParams(vmem_limit_bytes=VMEM_GRANT),
        name="gate_pass",
    )(seat.reshape(1), q_feat, y_local, carry, incoming, decay_rate, residue)


def by_seat(seat, blocks):
    ordered = []
    for k in range(CREW):
        value = blocks[0]
        for j in range(1, CREW):
            value = jnp.where((seat ^ k) == j, blocks[j], value)
        ordered.append(value)
    return ordered


def plane_kernel(span, seat_ref, steps_ref, *refs):
    blocks, out_ref = refs[:CREW], refs[CREW]
    reach = jnp.exp(-steps_ref[...] * span)
    ends = by_seat(seat_ref[0], [b[...] for b in blocks])
    state = ends[0]
    for end in ends[1:]:
        state = reach * state + end
    out_ref[...] = state


def incoming_kernel(span, seat_ref, steps_ref, *refs):
    blocks, planes = refs[:CREW], refs[CREW : CREW + PLANES - 1]
    outs = refs[CREW + PLANES - 1 :]
    steps, seat = steps_ref[...], seat_ref[0]
    ends = by_seat(seat, [b[...] for b in blocks])
    reach, reach_plane = jnp.exp(-steps * span), jnp.exp(-steps * (span * CREW))
    state = planes[-1][...]
    for plane in planes[-2::-1]:
        state = reach_plane * state + plane[...]
    states = [state]
    for end in ends[:-1]:
        states.append(reach * states[-1] + end)
    for out_ref, value in zip(outs, by_seat(seat, states)):
        out_ref[...] = value


def state_call(body, name, seat, steps, ends, arrays, out_count):
    modes, quarter = arrays[0].shape

    def owned(_, s):
        return (0, s[0])

    own = pl.BlockSpec((modes, quarter), owned)
    whole = pl.BlockSpec((modes, quarter), lambda _, s: (0, 0))
    shape = jax.ShapeDtypeStruct((modes, quarter), F32)
    return pl.pallas_call(
        body,
        grid_spec=pltpu.PrefetchScalarGridSpec(
            num_scalar_prefetch=1,
            grid=(1,),
            in_specs=[own, own] + [whole] * len(arrays),
            out_specs=[whole] * out_count,
        ),
        out_shape=[shape] * out_count,
        name=name,
    )(seat.reshape(1), steps, ends, *arrays)


def product_kernel(relayed_count, token_count, pick_ref, *refs):
    refs = list(refs)
    relayed = [refs.pop(0) for _ in range(relayed_count)]
    gathered_ref = None if relayed else refs.pop(0)
    tokens = [refs.pop(0) for _ in range(token_count)]
    kept_ref, sent_ref, total = refs[:3]
    step = pl.program_id(0)

    @pl.when(step == 0)
    def _():
        total[...] = jnp.zeros_like(total)

    if relayed:
        joined = refs[3]
        feat = relayed[0].shape[0]
        for plane in range(PLANES):
            for here in range(PLANES):

                @pl.when(pick_ref[1] == here)
                def _():
                    source = relayed[PLANES - 1 + here - plane]
                    joined[plane * feat : (plane + 1) * feat, :] = source[...]

        weights = joined[...]
    else:
        planes, feat, width = gathered_ref.shape
        weights = gathered_ref[...].reshape(planes * feat, width)
    for j, token in enumerate(tokens):
        total[j] += lax.dot_general(
            weights, token[...], (((1,), (1,)), ((), ())), preferred_element_type=F32
        )

    @pl.when(step == pl.num_programs(0) - 1)
    def _():
        middle = total.shape[1] // 2
        for side, outs in ((0, (kept_ref, sent_ref)), (1, (sent_ref, kept_ref))):

            @pl.when(pick_ref[0] == side)
            def _():
                outs[0][...] = total[:, :middle, :].astype(BF16)
                outs[1][...] = total[:, middle:, :].astype(BF16)


def project(picks, weights, tokens):
    rows, depth = tokens[0].shape
    width = 1024 if depth % 1024 == 0 else LANES
    relayed = weights if isinstance(weights, list) else []
    scratch = []
    if relayed:
        feat = relayed[0].shape[0]
        specs = [pl.BlockSpec((feat, width), lambda c, _: (0, c)) for _ in relayed]
        scratch = [pltpu.VMEM((PLANES * feat, width), BF16)]
    else:
        feat = weights.shape[1]
        specs = [pl.BlockSpec((PLANES, feat, width), lambda c, _: (0, 0, c))]
        weights = [weights]
    shape = (len(tokens), PLANES * feat // 2, rows)
    return pl.pallas_call(
        functools.partial(product_kernel, len(relayed), len(tokens)),
        grid_spec=pltpu.PrefetchScalarGridSpec(
            num_scalar_prefetch=1,
            grid=(depth // width,),
            in_specs=specs + [pl.BlockSpec((rows, width), lambda c, _: (0, c)) for _ in tokens],
            out_specs=[pl.BlockSpec(shape, lambda c, _: (0, 0, 0))] * 2,
            scratch_shapes=[pltpu.VMEM((len(tokens), PLANES * feat, rows), F32)] + scratch,
        ),
        out_shape=[jax.ShapeDtypeStruct(shape, BF16)] * 2,
        compiler_params=pltpu.CompilerParams(vmem_limit_bytes=VMEM_GRANT),
        cost_estimate=pl.CostEstimate(
            flops=1, bytes_accessed=4 * len(tokens) * rows * depth * 2 if relayed else 1,
            transcendentals=0,
        ),
        name="project",
    )(picks, *weights, *tokens)


def assemble_kernel(seat_ref, *refs):
    pieces, out_ref = refs[:-1], refs[-1]
    halves = PLANES // 2
    block = out_ref.shape[0] // halves
    feat = block // CREW
    for j in range(CREW):
        begin = 0
        for piece in pieces[j::CREW]:
            size = piece.shape[0] // halves
            for half in range(halves):
                at = half * block + (seat_ref[0] ^ j) * feat + begin
                at = pl.multiple_of(at, math.gcd(size, begin) if begin else size)
                out_ref[pl.ds(at, size), :] = piece[half * size : (half + 1) * size, :]
            begin += size


def assemble(seat, pieces):
    rows = pieces[0].shape[1]
    vmem = pl.BlockSpec(memory_space=pltpu.VMEM)
    return pl.pallas_call(
        assemble_kernel,
        in_specs=[pl.BlockSpec(memory_space=pltpu.SMEM)] + [vmem] * len(pieces),
        out_specs=vmem,
        out_shape=jax.ShapeDtypeStruct((sum(p.shape[0] for p in pieces), rows), BF16),
        compiler_params=pltpu.CompilerParams(vmem_limit_bytes=VMEM_GRANT),
        name="assemble",
    )(seat.reshape(1), *pieces)


def tails_kernel(q_ref, k_ref, v_ref, out_ref):
    lead = LEAD
    for which, ref in enumerate((q_ref, k_ref, v_ref)):
        rows = ref[...].astype(F32)
        out_ref[which * lead : (which + 1) * lead, :] = rows[rows.shape[0] - lead :]
    out_ref[3 * lead :, :] = jnp.zeros((out_ref.shape[0] - 3 * lead, out_ref.shape[1]), F32)


def gather_rims(q_proj, k_proj, v_proj):
    size = lax.axis_size("context")
    rows, chan_count = q_proj.shape
    last = pl.BlockSpec((16, chan_count), lambda i: (rows // 16 - 1, 0))
    tails = pl.pallas_call(
        tails_kernel,
        grid=(1,),
        in_specs=[last] * 3,
        out_specs=pl.BlockSpec((SEGS, chan_count), lambda i: (0, 0)),
        out_shape=jax.ShapeDtypeStruct((SEGS, chan_count), F32),
        compiler_params=pltpu.CompilerParams(vmem_limit_bytes=VMEM_GRANT),
        name="tails",
    )(q_proj, k_proj, v_proj)
    return lax.ppermute(tails, "context", [(i, i + 1) for i in range(size - 1)])


def per_device(q_proj, k_proj, v_proj, short_filter, residue, decay_rate, out_weight):
    place, size = lax.axis_index("context"), lax.axis_size("context")

    rows = q_proj.shape[0]
    rims = gather_rims(q_proj, k_proj, v_proj)
    q_feat, y_local, carry, ends = local_rows(
        q_proj, k_proj, v_proj, rims, short_filter, residue, decay_rate
    )
    gathered = lax.all_gather(ends, "context")
    gaps = (place - 1 - jnp.arange(size))[:, None, None]
    reach = jnp.exp(-(decay_rate / float(rows * size))[None] * (gaps * rows).astype(F32))
    incoming = jnp.sum(jnp.where(gaps >= 0, reach * gathered, 0.0), axis=0)
    gated = gate_rows(
        q_feat, y_local, carry, incoming[None], decay_rate, residue, jnp.int32(0)
    )
    partial_terms = lax.dot_general(
        lax.all_gather(out_weight, "context", axis=0, tiled=True),
        gated,
        (((1,), (1,)), ((), ())),
        preferred_element_type=F32,
    )
    return lax.psum_scatter(
        partial_terms.astype(BF16), "tensor", scatter_dimension=0, tiled=True
    )


def swap(block, mask):
    size = lax.axis_size("context")
    return lax.ppermute(block, "context", [(i, i ^ mask) for i in range(size)])


def shift(block, distance):
    size = lax.axis_size("context")
    moves = [(i, i + distance) for i in range(size) if 0 <= i + distance < size]
    return lax.ppermute(block, "context", moves)


def per_device_planes(q_proj, k_proj, v_proj, short_filter, residue, decay_rate, out_weight):
    size = lax.axis_size("context")
    seat = lax.axis_index("context") % CREW
    side = lax.axis_index("tensor")
    rows, feat = q_proj.shape[0], out_weight.shape[0]
    quarter = q_proj.shape[1] // CREW
    span = float(rows)
    steps = decay_rate / (span * size)
    columns = [[p * CREW + s for p in range(PLANES)] for s in range(CREW)]
    cut = feat * 3 // 4
    most, k_proj = lax.optimization_barrier((out_weight[:cut], k_proj))
    gathered = lax.all_gather(most, "context", axis_index_groups=columns)
    picks = jnp.stack([side, lax.axis_index("context") // CREW]).astype(jnp.int32)

    def hops(block, moves):
        return lax.ppermute(
            block, "context",
            [(a * CREW + s, b * CREW + s) for a, b in moves for s in range(CREW)],
        )

    rims = gather_rims(q_proj, k_proj, v_proj)
    q_feat, y_local, carry, ends = local_rows(
        q_proj, k_proj, v_proj, rims, short_filter, residue, decay_rate
    )
    blocks = [
        swap(lax.dynamic_slice_in_dim(ends, (seat ^ j) * quarter, quarter, 1), j)
        for j in range(1, CREW)
    ]
    total = state_call(
        functools.partial(plane_kernel, span), "plane_state", seat, steps, ends, blocks, 1
    )[0]
    planes = [shift(total, hop * CREW) for hop in range(1, PLANES)]
    planes, own = lax.optimization_barrier((planes, out_weight[cut:]))
    up1, down1 = shift(own, CREW), shift(own, -CREW)
    mine = state_call(
        functools.partial(incoming_kernel, span), "incoming_state",
        seat, steps, ends, blocks + planes, CREW,
    )
    incoming = jnp.stack([mine[0]] + [swap(mine[j], j) for j in range(1, CREW)])
    gated = gate_rows(q_feat, y_local, carry, incoming, decay_rate, residue, seat)
    beside = swap(gated, 1)
    far, up1, down1 = lax.optimization_barrier((swap(gated, 2), up1, down1))
    up2, down2 = hops(up1, [(1, 2), (2, 3)]), hops(down1, [(2, 1), (1, 0)])

    def added(kept, arrived):
        return [
            (kept[at].astype(F32) + arrived[at].astype(F32)).astype(BF16)
            for at in range(kept.shape[0])
        ]

    def deal(parts, members):
        return [swap(part, j) if j else part for part, j in zip(parts, members)]

    def finish(kept, arrived, members):
        return deal(added(kept, arrived), members)

    near, beyond = [gated, beside], [far, swap(far, 1)]
    kept, sent = project(picks, gathered, beyond)
    kept, near[0], up2, down2 = lax.optimization_barrier((kept, near[0], up2, down2))
    up3, down3 = hops(up2, [(2, 3)]), hops(down2, [(1, 0)])
    far_kept, far_arrived = kept, lax.ppermute(sent, "tensor", [(0, 1), (1, 0)])
    near_kept, sent = project(picks, gathered, near)
    near_arrived = lax.ppermute(sent, "tensor", [(0, 1), (1, 0)])
    near_kept, up3, down3, far_arrived = lax.optimization_barrier(
        (near_kept, up3, down3, far_arrived)
    )
    far_pieces = added(far_kept, far_arrived)
    up3, down3, far_pieces = lax.optimization_barrier((up3, down3, far_pieces))
    relayed = [down3, down2, down1, own, up1, up2, up3]
    last_kept, last_sent = project(picks, relayed, near + beyond)
    last_kept, near_arrived = lax.optimization_barrier((last_kept, near_arrived))
    last_arrived = lax.ppermute(last_sent, "tensor", [(0, 1), (1, 0)])
    pieces = finish(near_kept, near_arrived, (0, 1)) + deal(far_pieces, (2, 3))
    pieces += finish(last_kept, last_arrived, (0, 1, 2, 3))
    return assemble(seat, pieces)


def solution(mesh):
    planes = mesh.shape["tensor"] == 2 and mesh.shape["context"] == CREW * PLANES
    return jax.shard_map(
        per_device_planes if planes else per_device,
        mesh=mesh,
        in_specs=(
            P("context", "tensor"),
            P("context", "tensor"),
            P("context", "tensor"),
            P(None, None, "tensor"),
            P(None, "tensor"),
            P(None, "tensor"),
            P("context", "tensor"),
        ),
        out_specs=P("tensor", "context"),
        check_vma=False,
    )
```

```python
import functools
import math

import jax
import jax.numpy as jnp
from jax import lax
from jax.experimental import pallas as pl
from jax.experimental.pallas import tpu as pltpu
from jax.sharding import PartitionSpec as P

LANES = 128
SEGS = 8
CREW = 4
LEAD = 2
PLANES = 4
VMEM_GRANT = 56 * 2**20
F32 = jnp.float32
BF16 = jnp.bfloat16


def lane_block(chan_count):
    for width in (1024, 512):
        if chan_count % (CREW * width) == 0:
            return width
    return LANES


def tree_sum(terms):
    terms = list(terms)
    while len(terms) > 1:
        paired = [terms[i] + terms[i + 1] for i in range(0, len(terms) - 1, 2)]
        if len(terms) % 2:
            paired.append(terms[-1])
        terms = paired
    return terms[0]


def spread(row):
    return jnp.broadcast_to(row, (SEGS, LANES))


def local_kernel(
    total, q_ref, k_ref, v_ref, rim_ref, filter_ref, decay_ref, residue_ref,
    qf_ref, y_ref, carry_ref, end_ref, shifted, signal,
):
    rows, width = q_ref.shape
    modes = decay_ref.shape[0]
    length = rows // SEGS
    kinds, tap_count, groups = filter_ref.shape
    group_width = pl.num_programs(0) * width // groups
    begin, count = 0, groups
    if groups % LANES == 0 and LANES * group_width % width == 0:
        begin, count = pl.program_id(0) * width // (LANES * group_width) * LANES, LANES
        begin = pl.multiple_of(begin, LANES)
    chan = pl.program_id(0) * width + lax.broadcasted_iota(jnp.int32, (count, width), 1)
    first = (begin + lax.broadcasted_iota(jnp.int32, (count, width), 0)) * group_width
    member = ((chan >= first) & (chan < first + group_width)).astype(BF16)
    filters = [filter_ref[kind, :, pl.ds(begin, count)].astype(F32) for kind in range(kinds)]
    taps = jnp.dot(
        jnp.concatenate(filters, axis=0).astype(BF16), member, preferred_element_type=F32
    )
    lead = LEAD

    def short_pass(which, ref, lanes):
        pad = shifted.at[which]
        pad[SEGS : SEGS + rows, :] = ref[:, lanes].astype(F32)
        pad[SEGS - lead : SEGS, :] = rim_ref[which * lead : (which + 1) * lead, lanes]
        running = None
        for offset in range(tap_count):
            row = which * tap_count + offset
            tap = taps[row : row + 1, lanes]
            term = tap * pad[SEGS - offset : SEGS - offset + rows, :]
            running = term if running is None else running + term
        return running.astype(BF16)

    for block in range(width // LANES):
        lanes = slice(block * LANES, (block + 1) * LANES)
        qf_ref[:, lanes] = short_pass(0, q_ref, lanes)
        k_feat = short_pass(1, k_ref, lanes).astype(F32)
        v_feat = short_pass(2, v_ref, lanes).astype(F32)
        signal[block] = (k_feat * v_feat).astype(BF16).astype(F32)

    seg = lax.broadcasted_iota(jnp.int32, (SEGS, LANES), 0)
    for block in range(width // LANES):
        lanes = slice(block * LANES, (block + 1) * LANES)
        steps = decay_ref[:, lanes] / total
        decays = jnp.exp(-steps)
        scales = residue_ref[:, lanes] * jnp.sqrt(2.0 * steps)
        decay = [spread(decays[m : m + 1]) for m in range(modes)]
        scale = [spread(scales[m : m + 1]) for m in range(modes)]

        def advance(i, state):
            x = signal[block, pl.ds(i, SEGS, stride=length), :]
            state = tuple(d * s + x for d, s in zip(decay, state))
            y_ref[i, :, lanes] = tree_sum(c * s for c, s in zip(scale, state))
            return state

        zero = jnp.zeros((SEGS, LANES), F32)
        state = lax.fori_loop(0, length, advance, (zero,) * modes, unroll=4)
        for m in range(modes):
            ends = state[m]
            for hop in (1, 2, 4):
                factor = spread(jnp.exp(-steps[m : m + 1] * float(length * hop)))
                ends = ends + factor * jnp.where(seg >= hop, pltpu.roll(ends, hop, 0), 0.0)
            end_ref[m : m + 1, lanes] = ends[SEGS - 1 : SEGS]
            carry_ref[m, :, lanes] = jnp.where(seg >= 1, pltpu.roll(ends, 1, 0), 0.0)


def gate_kernel(
    total, per_part, seat_ref, qf_ref, y_ref, carry_ref, decay_ref, residue_ref, *refs
):
    parts, (out_ref, mixed) = refs[:-2], refs[-2:]
    wanted = seat_ref[0] ^ (pl.program_id(0) // per_part)
    incoming = parts[0][...]
    for at in range(1, len(parts)):
        incoming = jnp.where(wanted == at, parts[at][...], incoming)

    rows, width = qf_ref.shape
    modes = decay_ref.shape[0]
    length = rows // SEGS
    begin = (lax.broadcasted_iota(jnp.int32, (SEGS, LANES), 0) * length).astype(F32)
    for block in range(width // LANES):
        lanes = slice(block * LANES, (block + 1) * LANES)
        steps = decay_ref[:, lanes] / total
        decays = jnp.exp(-steps)
        weights = residue_ref[:, lanes] * jnp.sqrt(2.0 * steps) * decays
        decay = [spread(decays[m : m + 1]) for m in range(modes)]
        tail = []
        for m in range(modes):
            reach = jnp.exp(-spread(steps[m : m + 1]) * begin)
            held = carry_ref[m, :, lanes] + reach * spread(incoming[m : m + 1, lanes])
            tail.append(spread(weights[m : m + 1]) * held)

        def advance(i, tail):
            mixed[block, pl.ds(i, SEGS, stride=length), :] = y_ref[i, :, lanes] + tree_sum(tail)
            return tuple(d * s for d, s in zip(decay, tail))

        lax.fori_loop(0, length, advance, tuple(tail), unroll=4)
    for block in range(width // LANES):
        lanes = slice(block * LANES, (block + 1) * LANES)
        out_ref[:, lanes] = (qf_ref[:, lanes].astype(F32) * mixed[block]).astype(BF16)


def column_call(body, name, arrays, outs, scratch, width, chan_count):
    def spec(shape):
        if shape[-1] != chan_count:
            return pl.BlockSpec(shape, lambda c: (0,) * len(shape))
        return pl.BlockSpec(shape[:-1] + (width,), lambda c: (0,) * (len(shape) - 1) + (c,))

    return pl.pallas_call(
        body,
        grid=(chan_count // width,),
        in_specs=[spec(a.shape) for a in arrays],
        out_specs=[spec(o.shape) for o in outs],
        out_shape=outs,
        scratch_shapes=scratch,
        compiler_params=pltpu.CompilerParams(vmem_limit_bytes=VMEM_GRANT),
        name=name,
    )(*arrays)


def local_rows(q_proj, k_proj, v_proj, rims, short_filter, residue, decay_rate):
    rows, chan_count = q_proj.shape
    modes = decay_rate.shape[0]
    total = float(rows * lax.axis_size("context"))
    width = lane_block(chan_count)
    return column_call(
        functools.partial(local_kernel, total), "local_pass",
        (q_proj, k_proj, v_proj, rims, short_filter, decay_rate, residue),
        [
            jax.ShapeDtypeStruct((rows, chan_count), BF16),
            jax.ShapeDtypeStruct((rows // SEGS, SEGS, chan_count), F32),
            jax.ShapeDtypeStruct((modes, SEGS, chan_count), F32),
            jax.ShapeDtypeStruct((modes, chan_count), F32),
        ],
        [
            pltpu.VMEM((3, rows + SEGS, LANES), F32),
            pltpu.VMEM((width // LANES, rows, LANES), F32),
        ],
        width, chan_count,
    )


def gate_rows(q_feat, y_local, carry, incoming, decay_rate, residue, seat):
    rows, chan_count = q_feat.shape
    modes = decay_rate.shape[0]
    total = float(rows * lax.axis_size("context"))
    width = lane_block(chan_count)
    per_part = incoming[0].shape[1] // width

    def cols(height):
        return pl.BlockSpec((height, width), lambda c, s: (0, c))

    return pl.pallas_call(
        functools.partial(gate_kernel, total, per_part),
        grid_spec=pltpu.PrefetchScalarGridSpec(
            num_scalar_prefetch=1,
            grid=(chan_count // width,),
            in_specs=[
                cols(rows),
                pl.BlockSpec((rows // SEGS, SEGS, width), lambda c, s: (0, 0, c)),
                pl.BlockSpec((modes, SEGS, width), lambda c, s: (0, 0, c)),
                cols(modes),
                cols(modes),
            ]
            + [pl.BlockSpec((modes, width), lambda c, s: (0, c % per_part)) for _ in incoming],
            out_specs=cols(rows),
            scratch_shapes=[pltpu.VMEM((width // LANES, rows, LANES), F32)],
        ),
        out_shape=jax.ShapeDtypeStruct((rows, chan_count), BF16),
        compiler_params=pltpu.CompilerParams(vmem_limit_bytes=VMEM_GRANT),
        name="gate_pass",
    )(seat.reshape(1), q_feat, y_local, carry, decay_rate, residue, *incoming)


def by_seat(seat, blocks):
    ordered = []
    for k in range(CREW):
        value = blocks[0]
        for j in range(1, CREW):
            value = jnp.where((seat ^ k) == j, blocks[j], value)
        ordered.append(value)
    return ordered


def plane_kernel(span, total, seat_ref, decay_ref, *refs):
    blocks, out_ref = refs[:CREW], refs[CREW]
    reach = jnp.exp(-(decay_ref[...] / total) * span)
    ends = by_seat(seat_ref[0], [b[...] for b in blocks])
    state = ends[0]
    for end in ends[1:]:
        state = reach * state + end
    out_ref[...] = state


def incoming_kernel(span, total, seat_ref, decay_ref, *refs):
    blocks, planes = refs[:CREW], refs[CREW : CREW + PLANES - 1]
    outs = refs[CREW + PLANES - 1 :]
    steps, seat = decay_ref[...] / total, seat_ref[0]
    ends = by_seat(seat, [b[...] for b in blocks])
    reach, reach_plane = jnp.exp(-steps * span), jnp.exp(-steps * (span * CREW))
    state = planes[-1][...]
    for plane in planes[-2::-1]:
        state = reach_plane * state + plane[...]
    states = [state]
    for end in ends[:-1]:
        states.append(reach * states[-1] + end)
    for out_ref, value in zip(outs, by_seat(seat, states)):
        out_ref[...] = value


def state_call(body, name, seat, steps, ends, arrays, out_count):
    modes, quarter = arrays[0].shape

    def owned(_, s):
        return (0, s[0])

    own = pl.BlockSpec((modes, quarter), owned)
    whole = pl.BlockSpec((modes, quarter), lambda _, s: (0, 0))
    shape = jax.ShapeDtypeStruct((modes, quarter), F32)
    return pl.pallas_call(
        body,
        grid_spec=pltpu.PrefetchScalarGridSpec(
            num_scalar_prefetch=1,
            grid=(1,),
            in_specs=[own, own] + [whole] * len(arrays),
            out_specs=[whole] * out_count,
        ),
        out_shape=[shape] * out_count,
        name=name,
    )(seat.reshape(1), steps, ends, *arrays)


def product_kernel(relayed_count, token_count, pick_ref, *refs):
    refs = list(refs)
    relayed = [refs.pop(0) for _ in range(relayed_count)]
    gathered_ref = None if relayed else refs.pop(0)
    tokens = [refs.pop(0) for _ in range(token_count)]
    kept_ref, sent_ref, total = refs[:3]
    step = pl.program_id(0)

    @pl.when(step == 0)
    def _():
        total[...] = jnp.zeros_like(total)

    if relayed:
        joined = refs[3]
        feat = relayed[0].shape[0]
        for plane in range(PLANES):
            for here in range(PLANES):

                @pl.when(pick_ref[1] == here)
                def _():
                    source = relayed[PLANES - 1 + here - plane]
                    joined[plane * feat : (plane + 1) * feat, :] = source[...]

        weights = joined[...]
    else:
        planes, feat, width = gathered_ref.shape
        weights = gathered_ref[...].reshape(planes * feat, width)
    for j, token in enumerate(tokens):
        total[j] += lax.dot_general(
            weights, token[...], (((1,), (1,)), ((), ())), preferred_element_type=F32
        )

    @pl.when(step == pl.num_programs(0) - 1)
    def _():
        middle = total.shape[1] // 2
        for side, outs in ((0, (kept_ref, sent_ref)), (1, (sent_ref, kept_ref))):

            @pl.when(pick_ref[0] == side)
            def _():
                outs[0][...] = total[:, :middle, :].astype(BF16)
                outs[1][...] = total[:, middle:, :].astype(BF16)


def project(picks, weights, tokens):
    rows, depth = tokens[0].shape
    width = 1024 if depth % 1024 == 0 else LANES
    relayed = weights if isinstance(weights, list) else []
    scratch = []
    if relayed:
        feat = relayed[0].shape[0]
        specs = [pl.BlockSpec((feat, width), lambda c, _: (0, c)) for _ in relayed]
        scratch = [pltpu.VMEM((PLANES * feat, width), BF16)]
    else:
        feat = weights.shape[1]
        specs = [pl.BlockSpec((PLANES, feat, width), lambda c, _: (0, 0, c))]
        weights = [weights]
    shape = (len(tokens), PLANES * feat // 2, rows)
    return pl.pallas_call(
        functools.partial(product_kernel, len(relayed), len(tokens)),
        grid_spec=pltpu.PrefetchScalarGridSpec(
            num_scalar_prefetch=1,
            grid=(depth // width,),
            in_specs=specs + [pl.BlockSpec((rows, width), lambda c, _: (0, c)) for _ in tokens],
            out_specs=[pl.BlockSpec(shape, lambda c, _: (0, 0, 0))] * 2,
            scratch_shapes=[pltpu.VMEM((len(tokens), PLANES * feat, rows), F32)] + scratch,
        ),
        out_shape=[jax.ShapeDtypeStruct(shape, BF16)] * 2,
        compiler_params=pltpu.CompilerParams(vmem_limit_bytes=VMEM_GRANT),
        cost_estimate=pl.CostEstimate(
            flops=1, bytes_accessed=4 * len(tokens) * rows * depth * 2 if relayed else 1,
            transcendentals=0,
        ),
        name="project",
    )(picks, *weights, *tokens)


def assemble_kernel(seat_ref, *refs):
    pieces, out_ref = refs[:-1], refs[-1]
    halves = PLANES // 2
    block = out_ref.shape[0] // halves
    feat = block // CREW
    for j in range(CREW):
        begin = 0
        for piece in pieces[j::CREW]:
            size = piece.shape[0] // halves
            for half in range(halves):
                at = half * block + (seat_ref[0] ^ j) * feat + begin
                at = pl.multiple_of(at, math.gcd(size, begin) if begin else size)
                out_ref[pl.ds(at, size), :] = piece[half * size : (half + 1) * size, :]
            begin += size


def assemble(seat, pieces):
    rows = pieces[0].shape[1]
    vmem = pl.BlockSpec(memory_space=pltpu.VMEM)
    return pl.pallas_call(
        assemble_kernel,
        in_specs=[pl.BlockSpec(memory_space=pltpu.SMEM)] + [vmem] * len(pieces),
        out_specs=vmem,
        out_shape=jax.ShapeDtypeStruct((sum(p.shape[0] for p in pieces), rows), BF16),
        compiler_params=pltpu.CompilerParams(vmem_limit_bytes=VMEM_GRANT),
        name="assemble",
    )(seat.reshape(1), *pieces)


def tails_kernel(q_ref, k_ref, v_ref, out_ref):
    lead = LEAD
    for which, ref in enumerate((q_ref, k_ref, v_ref)):
        rows = ref[...].astype(F32)
        out_ref[which * lead : (which + 1) * lead, :] = rows[rows.shape[0] - lead :]
    out_ref[3 * lead :, :] = jnp.zeros((out_ref.shape[0] - 3 * lead, out_ref.shape[1]), F32)


def gather_rims(q_proj, k_proj, v_proj):
    size = lax.axis_size("context")
    rows, chan_count = q_proj.shape
    last = pl.BlockSpec((16, chan_count), lambda i: (rows // 16 - 1, 0))
    tails = pl.pallas_call(
        tails_kernel,
        grid=(1,),
        in_specs=[last] * 3,
        out_specs=pl.BlockSpec((SEGS, chan_count), lambda i: (0, 0)),
        out_shape=jax.ShapeDtypeStruct((SEGS, chan_count), F32),
        compiler_params=pltpu.CompilerParams(vmem_limit_bytes=VMEM_GRANT),
        name="tails",
    )(q_proj, k_proj, v_proj)
    return lax.ppermute(tails, "context", [(i, i + 1) for i in range(size - 1)])


def per_device(q_proj, k_proj, v_proj, short_filter, residue, decay_rate, out_weight):
    place, size = lax.axis_index("context"), lax.axis_size("context")

    rows = q_proj.shape[0]
    rims = gather_rims(q_proj, k_proj, v_proj)
    q_feat, y_local, carry, ends = local_rows(
        q_proj, k_proj, v_proj, rims, short_filter, residue, decay_rate
    )
    gathered = lax.all_gather(ends, "context")
    gaps = (place - 1 - jnp.arange(size))[:, None, None]
    reach = jnp.exp(-(decay_rate / float(rows * size))[None] * (gaps * rows).astype(F32))
    incoming = jnp.sum(jnp.where(gaps >= 0, reach * gathered, 0.0), axis=0)
    gated = gate_rows(
        q_feat, y_local, carry, [incoming], decay_rate, residue, jnp.int32(0)
    )
    partial_terms = lax.dot_general(
        lax.all_gather(out_weight, "context", axis=0, tiled=True),
        gated,
        (((1,), (1,)), ((), ())),
        preferred_element_type=F32,
    )
    return lax.psum_scatter(
        partial_terms.astype(BF16), "tensor", scatter_dimension=0, tiled=True
    )


def swap(block, mask):
    size = lax.axis_size("context")
    return lax.ppermute(block, "context", [(i, i ^ mask) for i in range(size)])


def shift(block, distance):
    size = lax.axis_size("context")
    moves = [(i, i + distance) for i in range(size) if 0 <= i + distance < size]
    return lax.ppermute(block, "context", moves)


def per_device_planes(q_proj, k_proj, v_proj, short_filter, residue, decay_rate, out_weight):
    size = lax.axis_size("context")
    seat = lax.axis_index("context") % CREW
    side = lax.axis_index("tensor")
    rows, feat = q_proj.shape[0], out_weight.shape[0]
    quarter = q_proj.shape[1] // CREW
    span = float(rows)
    spans = (span, span * size)
    columns = [[p * CREW + s for p in range(PLANES)] for s in range(CREW)]
    cut = feat * 3 // 4
    most, k_proj = lax.optimization_barrier((out_weight[:cut], k_proj))
    gathered = lax.all_gather(most, "context", axis_index_groups=columns)
    picks = jnp.stack([side, lax.axis_index("context") // CREW]).astype(jnp.int32)

    def hops(block, moves):
        return lax.ppermute(
            block, "context",
            [(a * CREW + s, b * CREW + s) for a, b in moves for s in range(CREW)],
        )

    rims = gather_rims(q_proj, k_proj, v_proj)
    q_feat, y_local, carry, ends = local_rows(
        q_proj, k_proj, v_proj, rims, short_filter, residue, decay_rate
    )
    blocks = [
        swap(lax.dynamic_slice_in_dim(ends, (seat ^ j) * quarter, quarter, 1), j)
        for j in range(1, CREW)
    ]
    total = state_call(
        functools.partial(plane_kernel, *spans), "plane_state", seat, decay_rate, ends, blocks, 1
    )[0]
    planes = [shift(total, hop * CREW) for hop in range(1, PLANES)]
    planes, own = lax.optimization_barrier((planes, out_weight[cut:]))
    up1, down1 = shift(own, CREW), shift(own, -CREW)
    mine = state_call(
        functools.partial(incoming_kernel, *spans), "incoming_state",
        seat, decay_rate, ends, blocks + planes, CREW,
    )
    incoming = [mine[0]] + [swap(mine[j], j) for j in range(1, CREW)]
    gated = gate_rows(q_feat, y_local, carry, incoming, decay_rate, residue, seat)
    beside = swap(gated, 1)
    far, up1, down1 = lax.optimization_barrier((swap(gated, 2), up1, down1))
    up2, down2 = hops(up1, [(1, 2), (2, 3)]), hops(down1, [(2, 1), (1, 0)])

    def added(kept, arrived):
        return [
            (kept[at].astype(F32) + arrived[at].astype(F32)).astype(BF16)
            for at in range(kept.shape[0])
        ]

    def deal(parts, members):
        return [swap(part, j) if j else part for part, j in zip(parts, members)]

    def finish(kept, arrived, members):
        return deal(added(kept, arrived), members)

    near, beyond = [gated, beside], [far, swap(far, 1)]
    kept, sent = project(picks, gathered, beyond)
    kept, near[0], up2, down2 = lax.optimization_barrier((kept, near[0], up2, down2))
    up3, down3 = hops(up2, [(2, 3)]), hops(down2, [(1, 0)])
    far_kept, far_arrived = kept, lax.ppermute(sent, "tensor", [(0, 1), (1, 0)])
    near_kept, sent = project(picks, gathered, near)
    near_arrived = lax.ppermute(sent, "tensor", [(0, 1), (1, 0)])
    near_kept, up3, down3, far_arrived = lax.optimization_barrier(
        (near_kept, up3, down3, far_arrived)
    )
    far_pieces = added(far_kept, far_arrived)
    up3, down3, far_pieces = lax.optimization_barrier((up3, down3, far_pieces))
    relayed = [down3, down2, down1, own, up1, up2, up3]
    last_kept, last_sent = project(picks, relayed, near + beyond)
    last_kept, near_arrived, far_pieces = lax.optimization_barrier(
        (last_kept, near_arrived, deal(far_pieces, (2, 3)))
    )
    last_arrived = lax.ppermute(last_sent, "tensor", [(0, 1), (1, 0)])
    pieces = finish(near_kept, near_arrived, (0, 1)) + far_pieces
    pieces += finish(last_kept, last_arrived, (0, 1, 2, 3))
    return assemble(seat, pieces)


def solution(mesh):
    planes = mesh.shape["tensor"] == 2 and mesh.shape["context"] == CREW * PLANES
    return jax.shard_map(
        per_device_planes if planes else per_device,
        mesh=mesh,
        in_specs=(
            P("context", "tensor"),
            P("context", "tensor"),
            P("context", "tensor"),
            P(None, None, "tensor"),
            P(None, "tensor"),
            P(None, "tensor"),
            P("context", "tensor"),
        ),
        out_specs=P("tensor", "context"),
        check_vma=False,
    )
```

```python
import functools
import math

import jax
import jax.numpy as jnp
from jax import lax
from jax.experimental import pallas as pl
from jax.experimental.pallas import tpu as pltpu
from jax.sharding import PartitionSpec as P

LANES = 128
SEGS = 8
CREW = 4
LEAD = 2
PLANES = 4
VMEM_GRANT = 56 * 2**20
F32 = jnp.float32
BF16 = jnp.bfloat16


def lane_block(chan_count):
    for width in (1024, 512):
        if chan_count % (CREW * width) == 0:
            return width
    return LANES


def tree_sum(terms):
    terms = list(terms)
    while len(terms) > 1:
        paired = [terms[i] + terms[i + 1] for i in range(0, len(terms) - 1, 2)]
        if len(terms) % 2:
            paired.append(terms[-1])
        terms = paired
    return terms[0]


def spread(row):
    return jnp.broadcast_to(row, (SEGS, LANES))


def local_kernel(
    total, q_ref, k_ref, v_ref, rim_ref, filter_ref, decay_ref, residue_ref,
    qf_ref, y_ref, carry_ref, end_ref, shifted, signal,
):
    rows, width = q_ref.shape
    modes = decay_ref.shape[0]
    length = rows // SEGS
    kinds, tap_count, groups = filter_ref.shape
    group_width = pl.num_programs(0) * width // groups
    begin, count = 0, groups
    if groups % LANES == 0 and LANES * group_width % width == 0:
        begin, count = pl.program_id(0) * width // (LANES * group_width) * LANES, LANES
        begin = pl.multiple_of(begin, LANES)
    chan = pl.program_id(0) * width + lax.broadcasted_iota(jnp.int32, (count, width), 1)
    first = (begin + lax.broadcasted_iota(jnp.int32, (count, width), 0)) * group_width
    member = ((chan >= first) & (chan < first + group_width)).astype(BF16)
    filters = [filter_ref[kind, :, pl.ds(begin, count)].astype(F32) for kind in range(kinds)]
    taps = jnp.dot(
        jnp.concatenate(filters, axis=0).astype(BF16), member, preferred_element_type=F32
    )
    lead = LEAD

    def short_pass(which, ref, lanes):
        pad = shifted.at[which]
        pad[SEGS : SEGS + rows, :] = ref[:, lanes].astype(F32)
        pad[SEGS - lead : SEGS, :] = rim_ref[which * lead : (which + 1) * lead, lanes]
        running = None
        for offset in range(tap_count):
            row = which * tap_count + offset
            tap = taps[row : row + 1, lanes]
            term = tap * pad[SEGS - offset : SEGS - offset + rows, :]
            running = term if running is None else running + term
        return running.astype(BF16)

    for block in range(width // LANES):
        lanes = slice(block * LANES, (block + 1) * LANES)
        qf_ref[:, lanes] = short_pass(0, q_ref, lanes)
        k_feat = short_pass(1, k_ref, lanes).astype(F32)
        v_feat = short_pass(2, v_ref, lanes).astype(F32)
        signal[block] = (k_feat * v_feat).astype(BF16).astype(F32)

    seg = lax.broadcasted_iota(jnp.int32, (SEGS, LANES), 0)
    for block in range(width // LANES):
        lanes = slice(block * LANES, (block + 1) * LANES)
        steps = decay_ref[:, lanes] / total
        decays = jnp.exp(-steps)
        scales = residue_ref[:, lanes] * jnp.sqrt(2.0 * steps)
        decay = [spread(decays[m : m + 1]) for m in range(modes)]
        scale = [spread(scales[m : m + 1]) for m in range(modes)]

        def advance(i, state):
            x = signal[block, pl.ds(i, SEGS, stride=length), :]
            state = tuple(d * s + x for d, s in zip(decay, state))
            y_ref[i, :, lanes] = tree_sum(c * s for c, s in zip(scale, state))
            return state

        zero = jnp.zeros((SEGS, LANES), F32)
        state = lax.fori_loop(0, length, advance, (zero,) * modes, unroll=4)
        for m in range(modes):
            ends = state[m]
            for hop in (1, 2, 4):
                factor = spread(jnp.exp(-steps[m : m + 1] * float(length * hop)))
                ends = ends + factor * jnp.where(seg >= hop, pltpu.roll(ends, hop, 0), 0.0)
            end_ref[m : m + 1, lanes] = ends[SEGS - 1 : SEGS]
            carry_ref[m, :, lanes] = jnp.where(seg >= 1, pltpu.roll(ends, 1, 0), 0.0)


def gate_kernel(
    total, per_part, seat_ref, qf_ref, y_ref, carry_ref, decay_ref, residue_ref, *refs
):
    parts, (out_ref, mixed) = refs[:-2], refs[-2:]
    wanted = seat_ref[0] ^ (pl.program_id(0) // per_part)
    incoming = parts[0][...]
    for at in range(1, len(parts)):
        incoming = jnp.where(wanted == at, parts[at][...], incoming)

    rows, width = qf_ref.shape
    modes = decay_ref.shape[0]
    length = rows // SEGS
    begin = (lax.broadcasted_iota(jnp.int32, (SEGS, LANES), 0) * length).astype(F32)
    for block in range(width // LANES):
        lanes = slice(block * LANES, (block + 1) * LANES)
        steps = decay_ref[:, lanes] / total
        decays = jnp.exp(-steps)
        weights = residue_ref[:, lanes] * jnp.sqrt(2.0 * steps) * decays
        decay = [spread(decays[m : m + 1]) for m in range(modes)]
        tail = []
        for m in range(modes):
            reach = jnp.exp(-spread(steps[m : m + 1]) * begin)
            held = carry_ref[m, :, lanes] + reach * spread(incoming[m : m + 1, lanes])
            tail.append(spread(weights[m : m + 1]) * held)

        def advance(i, tail):
            mixed[block, pl.ds(i, SEGS, stride=length), :] = y_ref[i, :, lanes] + tree_sum(tail)
            return tuple(d * s for d, s in zip(decay, tail))

        lax.fori_loop(0, length, advance, tuple(tail), unroll=4)
    for block in range(width // LANES):
        lanes = slice(block * LANES, (block + 1) * LANES)
        out_ref[:, lanes] = (qf_ref[:, lanes].astype(F32) * mixed[block]).astype(BF16)


def column_call(body, name, arrays, outs, scratch, width, chan_count):
    def spec(shape):
        if shape[-1] != chan_count:
            return pl.BlockSpec(shape, lambda c: (0,) * len(shape))
        return pl.BlockSpec(shape[:-1] + (width,), lambda c: (0,) * (len(shape) - 1) + (c,))

    return pl.pallas_call(
        body,
        grid=(chan_count // width,),
        in_specs=[spec(a.shape) for a in arrays],
        out_specs=[spec(o.shape) for o in outs],
        out_shape=outs,
        scratch_shapes=scratch,
        compiler_params=pltpu.CompilerParams(vmem_limit_bytes=VMEM_GRANT),
        name=name,
    )(*arrays)


def local_rows(q_proj, k_proj, v_proj, rims, short_filter, residue, decay_rate):
    rows, chan_count = q_proj.shape
    modes = decay_rate.shape[0]
    total = float(rows * lax.axis_size("context"))
    width = lane_block(chan_count)
    return column_call(
        functools.partial(local_kernel, total), "local_pass",
        (q_proj, k_proj, v_proj, rims, short_filter, decay_rate, residue),
        [
            jax.ShapeDtypeStruct((rows, chan_count), BF16),
            jax.ShapeDtypeStruct((rows // SEGS, SEGS, chan_count), F32),
            jax.ShapeDtypeStruct((modes, SEGS, chan_count), F32),
            jax.ShapeDtypeStruct((modes, chan_count), F32),
        ],
        [
            pltpu.VMEM((3, rows + SEGS, LANES), F32),
            pltpu.VMEM((width // LANES, rows, LANES), F32),
        ],
        width, chan_count,
    )


def gate_rows(q_feat, y_local, carry, incoming, decay_rate, residue, seat):
    rows, chan_count = q_feat.shape
    modes = decay_rate.shape[0]
    total = float(rows * lax.axis_size("context"))
    width = lane_block(chan_count)
    per_part = incoming[0].shape[1] // width

    def cols(height):
        return pl.BlockSpec((height, width), lambda c, s: (0, c))

    return pl.pallas_call(
        functools.partial(gate_kernel, total, per_part),
        grid_spec=pltpu.PrefetchScalarGridSpec(
            num_scalar_prefetch=1,
            grid=(chan_count // width,),
            in_specs=[
                cols(rows),
                pl.BlockSpec((rows // SEGS, SEGS, width), lambda c, s: (0, 0, c)),
                pl.BlockSpec((modes, SEGS, width), lambda c, s: (0, 0, c)),
                cols(modes),
                cols(modes),
            ]
            + [pl.BlockSpec((modes, width), lambda c, s: (0, c % per_part)) for _ in incoming],
            out_specs=cols(rows),
            scratch_shapes=[pltpu.VMEM((width // LANES, rows, LANES), F32)],
        ),
        out_shape=jax.ShapeDtypeStruct((rows, chan_count), BF16),
        compiler_params=pltpu.CompilerParams(vmem_limit_bytes=VMEM_GRANT),
        name="gate_pass",
    )(seat.reshape(1), q_feat, y_local, carry, decay_rate, residue, *incoming)


def by_seat(seat, blocks):
    ordered = []
    for k in range(CREW):
        value = blocks[0]
        for j in range(1, CREW):
            value = jnp.where((seat ^ k) == j, blocks[j], value)
        ordered.append(value)
    return ordered


def plane_kernel(span, total, seat_ref, decay_ref, *refs):
    blocks, out_ref = refs[:CREW], refs[CREW]
    reach = jnp.exp(-(decay_ref[...] / total) * span)
    ends = by_seat(seat_ref[0], [b[...] for b in blocks])
    state = ends[0]
    for end in ends[1:]:
        state = reach * state + end
    out_ref[...] = state


def incoming_kernel(span, total, seat_ref, decay_ref, *refs):
    blocks, planes = refs[:CREW], refs[CREW : CREW + PLANES - 1]
    outs = refs[CREW + PLANES - 1 :]
    steps, seat = decay_ref[...] / total, seat_ref[0]
    ends = by_seat(seat, [b[...] for b in blocks])
    reach, reach_plane = jnp.exp(-steps * span), jnp.exp(-steps * (span * CREW))
    state = planes[-1][...]
    for plane in planes[-2::-1]:
        state = reach_plane * state + plane[...]
    states = [state]
    for end in ends[:-1]:
        states.append(reach * states[-1] + end)
    for out_ref, value in zip(outs, by_seat(seat, states)):
        out_ref[...] = value


def state_call(body, name, seat, steps, ends, arrays, out_count):
    modes, quarter = arrays[0].shape

    def owned(_, s):
        return (0, s[0])

    own = pl.BlockSpec((modes, quarter), owned)
    whole = pl.BlockSpec((modes, quarter), lambda _, s: (0, 0))
    shape = jax.ShapeDtypeStruct((modes, quarter), F32)
    return pl.pallas_call(
        body,
        grid_spec=pltpu.PrefetchScalarGridSpec(
            num_scalar_prefetch=1,
            grid=(1,),
            in_specs=[own, own] + [whole] * len(arrays),
            out_specs=[whole] * out_count,
        ),
        out_shape=[shape] * out_count,
        name=name,
    )(seat.reshape(1), steps, ends, *arrays)


def product_kernel(relayed_count, token_count, pick_ref, *refs):
    refs = list(refs)
    relayed = [refs.pop(0) for _ in range(relayed_count)]
    gathered_ref = None if relayed else refs.pop(0)
    tokens = [refs.pop(0) for _ in range(token_count)]
    kept_ref, sent_ref, total = refs[:3]
    step = pl.program_id(0)

    @pl.when(step == 0)
    def _():
        total[...] = jnp.zeros_like(total)

    if relayed:
        joined = refs[3]
        feat = relayed[0].shape[0]
        for plane in range(PLANES):
            for here in range(PLANES):

                @pl.when(pick_ref[1] == here)
                def _():
                    source = relayed[PLANES - 1 + here - plane]
                    joined[plane * feat : (plane + 1) * feat, :] = source[...]

        weights = joined[...]
    else:
        planes, feat, width = gathered_ref.shape
        weights = gathered_ref[...].reshape(planes * feat, width)
    for j, token in enumerate(tokens):
        total[j] += lax.dot_general(
            weights, token[...], (((1,), (1,)), ((), ())), preferred_element_type=F32
        )

    @pl.when(step == pl.num_programs(0) - 1)
    def _():
        middle = total.shape[1] // 2
        for side, outs in ((0, (kept_ref, sent_ref)), (1, (sent_ref, kept_ref))):

            @pl.when(pick_ref[0] == side)
            def _():
                outs[0][...] = total[:, :middle, :].astype(BF16)
                outs[1][...] = total[:, middle:, :].astype(BF16)


def project(picks, weights, tokens):
    rows, depth = tokens[0].shape
    width = 1024 if depth % 1024 == 0 else LANES
    relayed = weights if isinstance(weights, list) else []
    scratch = []
    if relayed:
        feat = relayed[0].shape[0]
        specs = [pl.BlockSpec((feat, width), lambda c, _: (0, c)) for _ in relayed]
        scratch = [pltpu.VMEM((PLANES * feat, width), BF16)]
    else:
        feat = weights.shape[1]
        specs = [pl.BlockSpec((PLANES, feat, width), lambda c, _: (0, 0, c))]
        weights = [weights]
    shape = (len(tokens), PLANES * feat // 2, rows)
    return pl.pallas_call(
        functools.partial(product_kernel, len(relayed), len(tokens)),
        grid_spec=pltpu.PrefetchScalarGridSpec(
            num_scalar_prefetch=1,
            grid=(depth // width,),
            in_specs=specs + [pl.BlockSpec((rows, width), lambda c, _: (0, c)) for _ in tokens],
            out_specs=[pl.BlockSpec(shape, lambda c, _: (0, 0, 0))] * 2,
            scratch_shapes=[pltpu.VMEM((len(tokens), PLANES * feat, rows), F32)] + scratch,
        ),
        out_shape=[jax.ShapeDtypeStruct(shape, BF16)] * 2,
        compiler_params=pltpu.CompilerParams(vmem_limit_bytes=VMEM_GRANT),
        cost_estimate=pl.CostEstimate(
            flops=1, bytes_accessed=4 * len(tokens) * rows * depth * 2 if relayed else 1,
            transcendentals=0,
        ),
        name="project",
    )(picks, *weights, *tokens)


def assemble_kernel(seat_ref, *refs):
    pieces, out_ref = refs[:-1], refs[-1]
    halves = PLANES // 2
    block = out_ref.shape[0] // halves
    feat = block // CREW
    for j in range(CREW):
        begin = 0
        for piece in pieces[j::CREW]:
            size = piece.shape[0] // halves
            for half in range(halves):
                at = half * block + (seat_ref[0] ^ j) * feat + begin
                at = pl.multiple_of(at, math.gcd(size, begin) if begin else size)
                out_ref[pl.ds(at, size), :] = piece[half * size : (half + 1) * size, :]
            begin += size


def assemble(seat, pieces):
    rows = pieces[0].shape[1]
    vmem = pl.BlockSpec(memory_space=pltpu.VMEM)
    return pl.pallas_call(
        assemble_kernel,
        in_specs=[pl.BlockSpec(memory_space=pltpu.SMEM)] + [vmem] * len(pieces),
        out_specs=vmem,
        out_shape=jax.ShapeDtypeStruct((sum(p.shape[0] for p in pieces), rows), BF16),
        compiler_params=pltpu.CompilerParams(vmem_limit_bytes=VMEM_GRANT),
        name="assemble",
    )(seat.reshape(1), *pieces)


def tails_kernel(q_ref, k_ref, v_ref, out_ref):
    lead = LEAD
    for which, ref in enumerate((q_ref, k_ref, v_ref)):
        rows = ref[...].astype(F32)
        out_ref[which * lead : (which + 1) * lead, :] = rows[rows.shape[0] - lead :]
    out_ref[3 * lead :, :] = jnp.zeros((out_ref.shape[0] - 3 * lead, out_ref.shape[1]), F32)


def gather_rims(q_proj, k_proj, v_proj):
    size = lax.axis_size("context")
    rows, chan_count = q_proj.shape
    last = pl.BlockSpec((16, chan_count), lambda i: (rows // 16 - 1, 0))
    tails = pl.pallas_call(
        tails_kernel,
        grid=(1,),
        in_specs=[last] * 3,
        out_specs=pl.BlockSpec((SEGS, chan_count), lambda i: (0, 0)),
        out_shape=jax.ShapeDtypeStruct((SEGS, chan_count), F32),
        compiler_params=pltpu.CompilerParams(vmem_limit_bytes=VMEM_GRANT),
        name="tails",
    )(q_proj, k_proj, v_proj)
    return lax.ppermute(tails, "context", [(i, i + 1) for i in range(size - 1)])


def per_device(q_proj, k_proj, v_proj, short_filter, residue, decay_rate, out_weight):
    place, size = lax.axis_index("context"), lax.axis_size("context")

    rows = q_proj.shape[0]
    rims = gather_rims(q_proj, k_proj, v_proj)
    q_feat, y_local, carry, ends = local_rows(
        q_proj, k_proj, v_proj, rims, short_filter, residue, decay_rate
    )
    gathered = lax.all_gather(ends, "context")
    gaps = (place - 1 - jnp.arange(size))[:, None, None]
    reach = jnp.exp(-(decay_rate / float(rows * size))[None] * (gaps * rows).astype(F32))
    incoming = jnp.sum(jnp.where(gaps >= 0, reach * gathered, 0.0), axis=0)
    gated = gate_rows(
        q_feat, y_local, carry, [incoming], decay_rate, residue, jnp.int32(0)
    )
    partial_terms = lax.dot_general(
        lax.all_gather(out_weight, "context", axis=0, tiled=True),
        gated,
        (((1,), (1,)), ((), ())),
        preferred_element_type=F32,
    )
    return lax.psum_scatter(
        partial_terms.astype(BF16), "tensor", scatter_dimension=0, tiled=True
    )


def swap(block, mask):
    size = lax.axis_size("context")
    return lax.ppermute(block, "context", [(i, i ^ mask) for i in range(size)])


def shift(block, distance):
    size = lax.axis_size("context")
    moves = [(i, i + distance) for i in range(size) if 0 <= i + distance < size]
    return lax.ppermute(block, "context", moves)


def per_device_planes(q_proj, k_proj, v_proj, short_filter, residue, decay_rate, out_weight):
    size = lax.axis_size("context")
    seat = lax.axis_index("context") % CREW
    side = lax.axis_index("tensor")
    rows, feat = q_proj.shape[0], out_weight.shape[0]
    quarter = q_proj.shape[1] // CREW
    span = float(rows)
    spans = (span, span * size)
    columns = [[p * CREW + s for p in range(PLANES)] for s in range(CREW)]
    cut = feat * 3 // 4
    most, k_proj = lax.optimization_barrier((out_weight[:cut], k_proj))
    gathered = lax.all_gather(most, "context", axis_index_groups=columns)
    picks = jnp.stack([side, lax.axis_index("context") // CREW]).astype(jnp.int32)

    def hops(block, moves):
        return lax.ppermute(
            block, "context",
            [(a * CREW + s, b * CREW + s) for a, b in moves for s in range(CREW)],
        )

    rims = gather_rims(q_proj, k_proj, v_proj)
    q_feat, y_local, carry, ends = local_rows(
        q_proj, k_proj, v_proj, rims, short_filter, residue, decay_rate
    )
    blocks = [
        swap(lax.dynamic_slice_in_dim(ends, (seat ^ j) * quarter, quarter, 1), j)
        for j in range(1, CREW)
    ]
    total = state_call(
        functools.partial(plane_kernel, *spans), "plane_state", seat, decay_rate, ends, blocks, 1
    )[0]
    planes = [shift(total, hop * CREW) for hop in range(1, PLANES)]
    planes, own = lax.optimization_barrier((planes, out_weight[cut:]))
    up1, down1 = shift(own, CREW), shift(own, -CREW)
    mine = state_call(
        functools.partial(incoming_kernel, *spans), "incoming_state",
        seat, decay_rate, ends, blocks + planes, CREW,
    )
    incoming = [mine[0]] + [swap(mine[j], j) for j in range(1, CREW)]
    gated = gate_rows(q_feat, y_local, carry, incoming, decay_rate, residue, seat)
    beside = swap(gated, 1)
    far = swap(gated, 2)
    up2, down2 = hops(up1, [(1, 2), (2, 3)]), hops(down1, [(2, 1), (1, 0)])

    def added(kept, arrived):
        return [
            (kept[at].astype(F32) + arrived[at].astype(F32)).astype(BF16)
            for at in range(kept.shape[0])
        ]

    def deal(parts, members):
        return [swap(part, j) if j else part for part, j in zip(parts, members)]

    def finish(kept, arrived, members):
        return deal(added(kept, arrived), members)

    near = [gated, beside]
    near_kept, sent = project(picks, gathered, near)
    near_kept, far, last_up, last_down = lax.optimization_barrier((near_kept, far, up2, down2))
    near_arrived = lax.ppermute(sent, "tensor", [(0, 1), (1, 0)])
    up3, down3 = hops(last_up, [(2, 3)]), hops(last_down, [(1, 0)])
    beyond = [far, swap(far, 1)]
    far_kept, sent = project(picks, gathered, beyond)
    far_arrived = lax.ppermute(sent, "tensor", [(0, 1), (1, 0)])
    far_kept, up3, down3 = lax.optimization_barrier((far_kept, up3, down3))
    relayed = [down3, down2, down1, own, up1, up2, up3]
    last_kept, last_sent = project(picks, relayed, near + beyond)
    last_kept, near_arrived = lax.optimization_barrier((last_kept, near_arrived))
    far_pieces = deal(added(far_kept, far_arrived), (2, 3))
    last_arrived = lax.ppermute(last_sent, "tensor", [(0, 1), (1, 0)])
    pieces = finish(near_kept, near_arrived, (0, 1)) + far_pieces
    pieces += finish(last_kept, last_arrived, (0, 1, 2, 3))
    return assemble(seat, pieces)


def solution(mesh):
    planes = mesh.shape["tensor"] == 2 and mesh.shape["context"] == CREW * PLANES
    return jax.shard_map(
        per_device_planes if planes else per_device,
        mesh=mesh,
        in_specs=(
            P("context", "tensor"),
            P("context", "tensor"),
            P("context", "tensor"),
            P(None, None, "tensor"),
            P(None, "tensor"),
            P(None, "tensor"),
            P("context", "tensor"),
        ),
        out_specs=P("tensor", "context"),
        check_vma=False,
    )
```

```python
import functools
import math

import jax
import jax.numpy as jnp
from jax import lax
from jax.experimental import pallas as pl
from jax.experimental.pallas import tpu as pltpu
from jax.sharding import PartitionSpec as P

LANES = 128
SEGS = 8
CREW = 4
LEAD = 2
PLANES = 4
VMEM_GRANT = 56 * 2**20
F32 = jnp.float32
BF16 = jnp.bfloat16


def lane_block(chan_count):
    for width in (1024, 512):
        if chan_count % (CREW * width) == 0:
            return width
    return LANES


def tree_sum(terms):
    terms = list(terms)
    while len(terms) > 1:
        paired = [terms[i] + terms[i + 1] for i in range(0, len(terms) - 1, 2)]
        if len(terms) % 2:
            paired.append(terms[-1])
        terms = paired
    return terms[0]


def spread(row):
    return jnp.broadcast_to(row, (SEGS, LANES))


def local_kernel(
    total, q_ref, k_ref, v_ref, rim_ref, filter_ref, decay_ref, residue_ref,
    qf_ref, y_ref, carry_ref, end_ref, shifted, signal,
):
    rows, width = q_ref.shape
    modes = decay_ref.shape[0]
    length = rows // SEGS
    kinds, tap_count, groups = filter_ref.shape
    group_width = pl.num_programs(0) * width // groups
    begin, count = 0, groups
    if groups % LANES == 0 and LANES * group_width % width == 0:
        begin, count = pl.program_id(0) * width // (LANES * group_width) * LANES, LANES
        begin = pl.multiple_of(begin, LANES)
    chan = pl.program_id(0) * width + lax.broadcasted_iota(jnp.int32, (count, width), 1)
    first = (begin + lax.broadcasted_iota(jnp.int32, (count, width), 0)) * group_width
    member = ((chan >= first) & (chan < first + group_width)).astype(BF16)
    filters = [filter_ref[kind, :, pl.ds(begin, count)].astype(F32) for kind in range(kinds)]
    taps = jnp.dot(
        jnp.concatenate(filters, axis=0).astype(BF16), member, preferred_element_type=F32
    )
    lead = LEAD

    def short_pass(which, ref, lanes):
        pad = shifted.at[which]
        pad[SEGS : SEGS + rows, :] = ref[:, lanes].astype(F32)
        pad[SEGS - lead : SEGS, :] = rim_ref[which * lead : (which + 1) * lead, lanes]
        running = None
        for offset in range(tap_count):
            row = which * tap_count + offset
            tap = taps[row : row + 1, lanes]
            term = tap * pad[SEGS - offset : SEGS - offset + rows, :]
            running = term if running is None else running + term
        return running.astype(BF16)

    for block in range(width // LANES):
        lanes = slice(block * LANES, (block + 1) * LANES)
        qf_ref[:, lanes] = short_pass(0, q_ref, lanes)
        k_feat = short_pass(1, k_ref, lanes).astype(F32)
        v_feat = short_pass(2, v_ref, lanes).astype(F32)
        signal[block] = (k_feat * v_feat).astype(BF16).astype(F32)

    seg = lax.broadcasted_iota(jnp.int32, (SEGS, LANES), 0)
    for block in range(width // LANES):
        lanes = slice(block * LANES, (block + 1) * LANES)
        steps = decay_ref[:, lanes] / total
        decays = jnp.exp(-steps)
        scales = residue_ref[:, lanes] * jnp.sqrt(2.0 * steps)
        decay = [spread(decays[m : m + 1]) for m in range(modes)]
        scale = [spread(scales[m : m + 1]) for m in range(modes)]

        def advance(i, state):
            x = signal[block, pl.ds(i, SEGS, stride=length), :]
            state = tuple(d * s + x for d, s in zip(decay, state))
            y_ref[i, :, lanes] = tree_sum(c * s for c, s in zip(scale, state))
            return state

        zero = jnp.zeros((SEGS, LANES), F32)
        state = lax.fori_loop(0, length, advance, (zero,) * modes, unroll=4)
        for m in range(modes):
            ends = state[m]
            for hop in (1, 2, 4):
                factor = spread(jnp.exp(-steps[m : m + 1] * float(length * hop)))
                ends = ends + factor * jnp.where(seg >= hop, pltpu.roll(ends, hop, 0), 0.0)
            end_ref[m : m + 1, lanes] = ends[SEGS - 1 : SEGS]
            carry_ref[m, :, lanes] = jnp.where(seg >= 1, pltpu.roll(ends, 1, 0), 0.0)


def gate_kernel(
    total, per_part, seat_ref, qf_ref, y_ref, carry_ref, decay_ref, residue_ref, *refs
):
    parts, (out_ref, mixed) = refs[:-2], refs[-2:]
    wanted = seat_ref[0] ^ (pl.program_id(0) // per_part)
    incoming = parts[0][...]
    for at in range(1, len(parts)):
        incoming = jnp.where(wanted == at, parts[at][...], incoming)

    rows, width = qf_ref.shape
    modes = decay_ref.shape[0]
    length = rows // SEGS
    begin = (lax.broadcasted_iota(jnp.int32, (SEGS, LANES), 0) * length).astype(F32)
    for block in range(width // LANES):
        lanes = slice(block * LANES, (block + 1) * LANES)
        steps = decay_ref[:, lanes] / total
        decays = jnp.exp(-steps)
        weights = residue_ref[:, lanes] * jnp.sqrt(2.0 * steps) * decays
        decay = [spread(decays[m : m + 1]) for m in range(modes)]
        tail = []
        for m in range(modes):
            reach = jnp.exp(-spread(steps[m : m + 1]) * begin)
            held = carry_ref[m, :, lanes] + reach * spread(incoming[m : m + 1, lanes])
            tail.append(spread(weights[m : m + 1]) * held)

        def advance(i, tail):
            mixed[block, pl.ds(i, SEGS, stride=length), :] = y_ref[i, :, lanes] + tree_sum(tail)
            return tuple(d * s for d, s in zip(decay, tail))

        lax.fori_loop(0, length, advance, tuple(tail), unroll=4)
    for block in range(width // LANES):
        lanes = slice(block * LANES, (block + 1) * LANES)
        out_ref[:, lanes] = (qf_ref[:, lanes].astype(F32) * mixed[block]).astype(BF16)


def column_call(body, name, arrays, outs, scratch, width, chan_count):
    def spec(shape):
        if shape[-1] != chan_count:
            return pl.BlockSpec(shape, lambda c: (0,) * len(shape))
        return pl.BlockSpec(shape[:-1] + (width,), lambda c: (0,) * (len(shape) - 1) + (c,))

    return pl.pallas_call(
        body,
        grid=(chan_count // width,),
        in_specs=[spec(a.shape) for a in arrays],
        out_specs=[spec(o.shape) for o in outs],
        out_shape=outs,
        scratch_shapes=scratch,
        compiler_params=pltpu.CompilerParams(vmem_limit_bytes=VMEM_GRANT),
        name=name,
    )(*arrays)


def local_rows(q_proj, k_proj, v_proj, rims, short_filter, residue, decay_rate):
    rows, chan_count = q_proj.shape
    modes = decay_rate.shape[0]
    total = float(rows * lax.axis_size("context"))
    width = lane_block(chan_count)
    return column_call(
        functools.partial(local_kernel, total), "local_pass",
        (q_proj, k_proj, v_proj, rims, short_filter, decay_rate, residue),
        [
            jax.ShapeDtypeStruct((rows, chan_count), BF16),
            jax.ShapeDtypeStruct((rows // SEGS, SEGS, chan_count), F32),
            jax.ShapeDtypeStruct((modes, SEGS, chan_count), F32),
            jax.ShapeDtypeStruct((modes, chan_count), F32),
        ],
        [
            pltpu.VMEM((3, rows + SEGS, LANES), F32),
            pltpu.VMEM((width // LANES, rows, LANES), F32),
        ],
        width, chan_count,
    )


def gate_rows(q_feat, y_local, carry, incoming, decay_rate, residue, seat):
    rows, chan_count = q_feat.shape
    modes = decay_rate.shape[0]
    total = float(rows * lax.axis_size("context"))
    width = lane_block(chan_count)
    per_part = incoming[0].shape[1] // width

    def cols(height):
        return pl.BlockSpec((height, width), lambda c, s: (0, c))

    return pl.pallas_call(
        functools.partial(gate_kernel, total, per_part),
        grid_spec=pltpu.PrefetchScalarGridSpec(
            num_scalar_prefetch=1,
            grid=(chan_count // width,),
            in_specs=[
                cols(rows),
                pl.BlockSpec((rows // SEGS, SEGS, width), lambda c, s: (0, 0, c)),
                pl.BlockSpec((modes, SEGS, width), lambda c, s: (0, 0, c)),
                cols(modes),
                cols(modes),
            ]
            + [pl.BlockSpec((modes, width), lambda c, s: (0, c % per_part)) for _ in incoming],
            out_specs=cols(rows),
            scratch_shapes=[pltpu.VMEM((width // LANES, rows, LANES), F32)],
        ),
        out_shape=jax.ShapeDtypeStruct((rows, chan_count), BF16),
        compiler_params=pltpu.CompilerParams(vmem_limit_bytes=VMEM_GRANT),
        name="gate_pass",
    )(seat.reshape(1), q_feat, y_local, carry, decay_rate, residue, *incoming)


def by_seat(seat, blocks):
    ordered = []
    for k in range(CREW):
        value = blocks[0]
        for j in range(1, CREW):
            value = jnp.where((seat ^ k) == j, blocks[j], value)
        ordered.append(value)
    return ordered


def plane_kernel(span, total, seat_ref, decay_ref, *refs):
    blocks, out_ref = refs[:CREW], refs[CREW]
    reach = jnp.exp(-(decay_ref[...] / total) * span)
    ends = by_seat(seat_ref[0], [b[...] for b in blocks])
    state = ends[0]
    for end in ends[1:]:
        state = reach * state + end
    out_ref[...] = state


def incoming_kernel(span, total, seat_ref, decay_ref, *refs):
    blocks, planes = refs[:CREW], refs[CREW : CREW + PLANES - 1]
    outs = refs[CREW + PLANES - 1 :]
    steps, seat = decay_ref[...] / total, seat_ref[0]
    ends = by_seat(seat, [b[...] for b in blocks])
    reach, reach_plane = jnp.exp(-steps * span), jnp.exp(-steps * (span * CREW))
    state = planes[-1][...]
    for plane in planes[-2::-1]:
        state = reach_plane * state + plane[...]
    states = [state]
    for end in ends[:-1]:
        states.append(reach * states[-1] + end)
    for out_ref, value in zip(outs, by_seat(seat, states)):
        out_ref[...] = value


def state_call(body, name, seat, steps, ends, arrays, out_count):
    modes, quarter = arrays[0].shape

    def owned(_, s):
        return (0, s[0])

    own = pl.BlockSpec((modes, quarter), owned)
    whole = pl.BlockSpec((modes, quarter), lambda _, s: (0, 0))
    shape = jax.ShapeDtypeStruct((modes, quarter), F32)
    return pl.pallas_call(
        body,
        grid_spec=pltpu.PrefetchScalarGridSpec(
            num_scalar_prefetch=1,
            grid=(1,),
            in_specs=[own, own] + [whole] * len(arrays),
            out_specs=[whole] * out_count,
        ),
        out_shape=[shape] * out_count,
        name=name,
    )(seat.reshape(1), steps, ends, *arrays)


def product_kernel(relayed_count, token_count, pick_ref, *refs):
    refs = list(refs)
    relayed = [refs.pop(0) for _ in range(relayed_count)]
    gathered_ref = None if relayed else refs.pop(0)
    tokens = [refs.pop(0) for _ in range(token_count)]
    kept_ref, sent_ref, total = refs[:3]
    step = pl.program_id(0)

    @pl.when(step == 0)
    def _():
        total[...] = jnp.zeros_like(total)

    if relayed:
        joined = refs[3]
        feat = relayed[0].shape[0]
        for plane in range(PLANES):
            for here in range(PLANES):

                @pl.when(pick_ref[1] == here)
                def _():
                    source = relayed[plane ^ here]
                    joined[plane * feat : (plane + 1) * feat, :] = source[...]

        weights = joined[...]
    else:
        planes, feat, width = gathered_ref.shape
        weights = gathered_ref[...].reshape(planes * feat, width)
    for j, token in enumerate(tokens):
        total[j] += lax.dot_general(
            weights, token[...], (((1,), (1,)), ((), ())), preferred_element_type=F32
        )

    @pl.when(step == pl.num_programs(0) - 1)
    def _():
        middle = total.shape[1] // 2
        for side, outs in ((0, (kept_ref, sent_ref)), (1, (sent_ref, kept_ref))):

            @pl.when(pick_ref[0] == side)
            def _():
                outs[0][...] = total[:, :middle, :].astype(BF16)
                outs[1][...] = total[:, middle:, :].astype(BF16)


def project(picks, weights, tokens):
    rows, depth = tokens[0].shape
    width = 1024 if depth % 1024 == 0 else LANES
    relayed = weights if isinstance(weights, list) else []
    scratch = []
    if relayed:
        feat = relayed[0].shape[0]
        specs = [pl.BlockSpec((feat, width), lambda c, _: (0, c)) for _ in relayed]
        scratch = [pltpu.VMEM((PLANES * feat, width), BF16)]
    else:
        feat = weights.shape[1]
        specs = [pl.BlockSpec((PLANES, feat, width), lambda c, _: (0, 0, c))]
        weights = [weights]
    shape = (len(tokens), PLANES * feat // 2, rows)
    return pl.pallas_call(
        functools.partial(product_kernel, len(relayed), len(tokens)),
        grid_spec=pltpu.PrefetchScalarGridSpec(
            num_scalar_prefetch=1,
            grid=(depth // width,),
            in_specs=specs + [pl.BlockSpec((rows, width), lambda c, _: (0, c)) for _ in tokens],
            out_specs=[pl.BlockSpec(shape, lambda c, _: (0, 0, 0))] * 2,
            scratch_shapes=[pltpu.VMEM((len(tokens), PLANES * feat, rows), F32)] + scratch,
        ),
        out_shape=[jax.ShapeDtypeStruct(shape, BF16)] * 2,
        compiler_params=pltpu.CompilerParams(vmem_limit_bytes=VMEM_GRANT),
        cost_estimate=pl.CostEstimate(
            flops=1, bytes_accessed=4 * len(tokens) * rows * depth * 2 if relayed else 1,
            transcendentals=0,
        ),
        name="project",
    )(picks, *weights, *tokens)


def assemble_kernel(seat_ref, *refs):
    pieces, out_ref = refs[:-1], refs[-1]
    halves = PLANES // 2
    block = out_ref.shape[0] // halves
    feat = block // CREW
    for j in range(CREW):
        begin = 0
        for piece in pieces[j::CREW]:
            size = piece.shape[0] // halves
            for half in range(halves):
                at = half * block + (seat_ref[0] ^ j) * feat + begin
                at = pl.multiple_of(at, math.gcd(size, begin) if begin else size)
                out_ref[pl.ds(at, size), :] = piece[half * size : (half + 1) * size, :]
            begin += size


def assemble(seat, pieces):
    rows = pieces[0].shape[1]
    vmem = pl.BlockSpec(memory_space=pltpu.VMEM)
    return pl.pallas_call(
        assemble_kernel,
        in_specs=[pl.BlockSpec(memory_space=pltpu.SMEM)] + [vmem] * len(pieces),
        out_specs=vmem,
        out_shape=jax.ShapeDtypeStruct((sum(p.shape[0] for p in pieces), rows), BF16),
        compiler_params=pltpu.CompilerParams(vmem_limit_bytes=VMEM_GRANT),
        name="assemble",
    )(seat.reshape(1), *pieces)


def tails_kernel(q_ref, k_ref, v_ref, out_ref):
    lead = LEAD
    for which, ref in enumerate((q_ref, k_ref, v_ref)):
        rows = ref[...].astype(F32)
        out_ref[which * lead : (which + 1) * lead, :] = rows[rows.shape[0] - lead :]
    out_ref[3 * lead :, :] = jnp.zeros((out_ref.shape[0] - 3 * lead, out_ref.shape[1]), F32)


def gather_rims(q_proj, k_proj, v_proj):
    size = lax.axis_size("context")
    rows, chan_count = q_proj.shape
    last = pl.BlockSpec((16, chan_count), lambda i: (rows // 16 - 1, 0))
    tails = pl.pallas_call(
        tails_kernel,
        grid=(1,),
        in_specs=[last] * 3,
        out_specs=pl.BlockSpec((SEGS, chan_count), lambda i: (0, 0)),
        out_shape=jax.ShapeDtypeStruct((SEGS, chan_count), F32),
        compiler_params=pltpu.CompilerParams(vmem_limit_bytes=VMEM_GRANT),
        name="tails",
    )(q_proj, k_proj, v_proj)
    return lax.ppermute(tails, "context", [(i, i + 1) for i in range(size - 1)])


def per_device(q_proj, k_proj, v_proj, short_filter, residue, decay_rate, out_weight):
    place, size = lax.axis_index("context"), lax.axis_size("context")

    rows = q_proj.shape[0]
    rims = gather_rims(q_proj, k_proj, v_proj)
    q_feat, y_local, carry, ends = local_rows(
        q_proj, k_proj, v_proj, rims, short_filter, residue, decay_rate
    )
    gathered = lax.all_gather(ends, "context")
    gaps = (place - 1 - jnp.arange(size))[:, None, None]
    reach = jnp.exp(-(decay_rate / float(rows * size))[None] * (gaps * rows).astype(F32))
    incoming = jnp.sum(jnp.where(gaps >= 0, reach * gathered, 0.0), axis=0)
    gated = gate_rows(
        q_feat, y_local, carry, [incoming], decay_rate, residue, jnp.int32(0)
    )
    partial_terms = lax.dot_general(
        lax.all_gather(out_weight, "context", axis=0, tiled=True),
        gated,
        (((1,), (1,)), ((), ())),
        preferred_element_type=F32,
    )
    return lax.psum_scatter(
        partial_terms.astype(BF16), "tensor", scatter_dimension=0, tiled=True
    )


def swap(block, mask):
    size = lax.axis_size("context")
    return lax.ppermute(block, "context", [(i, i ^ mask) for i in range(size)])


def shift(block, distance):
    size = lax.axis_size("context")
    moves = [(i, i + distance) for i in range(size) if 0 <= i + distance < size]
    return lax.ppermute(block, "context", moves)


def per_device_planes(q_proj, k_proj, v_proj, short_filter, residue, decay_rate, out_weight):
    size = lax.axis_size("context")
    seat = lax.axis_index("context") % CREW
    side = lax.axis_index("tensor")
    rows, feat = q_proj.shape[0], out_weight.shape[0]
    quarter = q_proj.shape[1] // CREW
    span = float(rows)
    spans = (span, span * size)
    columns = [[p * CREW + s for p in range(PLANES)] for s in range(CREW)]
    cut = feat * 3 // 4
    most, k_proj = lax.optimization_barrier((out_weight[:cut], k_proj))
    gathered = lax.all_gather(most, "context", axis_index_groups=columns)
    picks = jnp.stack([side, lax.axis_index("context") // CREW]).astype(jnp.int32)

    rims = gather_rims(q_proj, k_proj, v_proj)
    q_feat, y_local, carry, ends = local_rows(
        q_proj, k_proj, v_proj, rims, short_filter, residue, decay_rate
    )
    blocks = [
        swap(lax.dynamic_slice_in_dim(ends, (seat ^ j) * quarter, quarter, 1), j)
        for j in range(1, CREW)
    ]
    total = state_call(
        functools.partial(plane_kernel, *spans), "plane_state", seat, decay_rate, ends, blocks, 1
    )[0]
    planes = [shift(total, hop * CREW) for hop in range(1, PLANES)]
    planes, own = lax.optimization_barrier((planes, out_weight[cut:]))
    mine = state_call(
        functools.partial(incoming_kernel, *spans), "incoming_state",
        seat, decay_rate, ends, blocks + planes, CREW,
    )
    incoming = [mine[0]] + [swap(mine[j], j) for j in range(1, CREW)]
    gated = gate_rows(q_feat, y_local, carry, incoming, decay_rate, residue, seat)
    beside = swap(gated, 1)
    far = swap(gated, 2)
    direct = [swap(own, mask * CREW) for mask in range(1, PLANES)]

    def added(kept, arrived):
        return [
            (kept[at].astype(F32) + arrived[at].astype(F32)).astype(BF16)
            for at in range(kept.shape[0])
        ]

    def deal(parts, members):
        return [swap(part, j) if j else part for part, j in zip(parts, members)]

    def finish(kept, arrived, members):
        return deal(added(kept, arrived), members)

    near = [gated, beside]
    near_kept, sent = project(picks, gathered, near)
    near_kept, far = lax.optimization_barrier((near_kept, far))
    near_arrived = lax.ppermute(sent, "tensor", [(0, 1), (1, 0)])

    def start_far(far):
        beyond = [far, swap(far, 1)]
        return (*project(picks, gathered, beyond), beyond[1])

    def no_far(far):
        empty = jnp.zeros((2, PLANES * cut // 2, rows), BF16)
        return empty, empty, far

    place = lax.axis_index("context")
    far_kept, sent, last_token = lax.cond(place < size, start_far, no_far, far)
    beyond = [far, last_token]
    far_arrived = lax.ppermute(sent, "tensor", [(0, 1), (1, 0)])
    far_kept, direct = lax.optimization_barrier((far_kept, direct))
    relayed = [own] + direct
    last_kept, last_sent = project(picks, relayed, near + beyond)
    last_kept, near_arrived = lax.optimization_barrier((last_kept, near_arrived))
    far_pieces = deal(added(far_kept, far_arrived), (2, 3))
    last_arrived = lax.ppermute(last_sent, "tensor", [(0, 1), (1, 0)])
    pieces = finish(near_kept, near_arrived, (0, 1)) + far_pieces
    pieces += finish(last_kept, last_arrived, (0, 1, 2, 3))
    return assemble(seat, pieces)


def solution(mesh):
    planes = mesh.shape["tensor"] == 2 and mesh.shape["context"] == CREW * PLANES
    return jax.shard_map(
        per_device_planes if planes else per_device,
        mesh=mesh,
        in_specs=(
            P("context", "tensor"),
            P("context", "tensor"),
            P("context", "tensor"),
            P(None, None, "tensor"),
            P(None, "tensor"),
            P(None, "tensor"),
            P("context", "tensor"),
        ),
        out_specs=P("tensor", "context"),
        check_vma=False,
    )
```

```python
import functools
import math

import jax
import jax.numpy as jnp
from jax import lax
from jax.experimental import pallas as pl
from jax.experimental.pallas import tpu as pltpu
from jax.sharding import PartitionSpec as P

LANES = 128
SEGS = 8
CREW = 4
LEAD = 2
PLANES = 4
VMEM_GRANT = 56 * 2**20
F32 = jnp.float32
BF16 = jnp.bfloat16


def lane_block(chan_count):
    for width in (1024, 512):
        if chan_count % (CREW * width) == 0:
            return width
    return LANES


def tree_sum(terms):
    terms = list(terms)
    while len(terms) > 1:
        paired = [terms[i] + terms[i + 1] for i in range(0, len(terms) - 1, 2)]
        if len(terms) % 2:
            paired.append(terms[-1])
        terms = paired
    return terms[0]


def spread(row):
    return jnp.broadcast_to(row, (SEGS, LANES))


def local_kernel(
    total, q_ref, k_ref, v_ref, rim_ref, filter_ref, decay_ref, residue_ref,
    qf_ref, y_ref, carry_ref, end_ref, shifted, signal,
):
    rows, width = q_ref.shape
    modes = decay_ref.shape[0]
    length = rows // SEGS
    kinds, tap_count, groups = filter_ref.shape
    group_width = pl.num_programs(0) * width // groups
    begin, count = 0, groups
    if groups % LANES == 0 and LANES * group_width % width == 0:
        begin, count = pl.program_id(0) * width // (LANES * group_width) * LANES, LANES
        begin = pl.multiple_of(begin, LANES)
    chan = pl.program_id(0) * width + lax.broadcasted_iota(jnp.int32, (count, width), 1)
    first = (begin + lax.broadcasted_iota(jnp.int32, (count, width), 0)) * group_width
    member = ((chan >= first) & (chan < first + group_width)).astype(BF16)
    filters = [filter_ref[kind, :, pl.ds(begin, count)].astype(F32) for kind in range(kinds)]
    taps = jnp.dot(
        jnp.concatenate(filters, axis=0).astype(BF16), member, preferred_element_type=F32
    )
    lead = LEAD

    def short_pass(which, ref, lanes):
        pad = shifted.at[which]
        pad[SEGS : SEGS + rows, :] = ref[:, lanes].astype(F32)
        pad[SEGS - lead : SEGS, :] = rim_ref[which * lead : (which + 1) * lead, lanes]
        running = None
        for offset in range(tap_count):
            row = which * tap_count + offset
            tap = taps[row : row + 1, lanes]
            term = tap * pad[SEGS - offset : SEGS - offset + rows, :]
            running = term if running is None else running + term
        return running.astype(BF16)

    for block in range(width // LANES):
        lanes = slice(block * LANES, (block + 1) * LANES)
        qf_ref[:, lanes] = short_pass(0, q_ref, lanes)
        k_feat = short_pass(1, k_ref, lanes).astype(F32)
        v_feat = short_pass(2, v_ref, lanes).astype(F32)
        signal[block] = (k_feat * v_feat).astype(BF16).astype(F32)

    seg = lax.broadcasted_iota(jnp.int32, (SEGS, LANES), 0)
    for block in range(width // LANES):
        lanes = slice(block * LANES, (block + 1) * LANES)
        steps = decay_ref[:, lanes] / total
        decays = jnp.exp(-steps)
        scales = residue_ref[:, lanes] * jnp.sqrt(2.0 * steps)
        decay = [spread(decays[m : m + 1]) for m in range(modes)]
        scale = [spread(scales[m : m + 1]) for m in range(modes)]

        def advance(i, state):
            x = signal[block, pl.ds(i, SEGS, stride=length), :]
            state = tuple(d * s + x for d, s in zip(decay, state))
            y_ref[i, :, lanes] = tree_sum(c * s for c, s in zip(scale, state))
            return state

        zero = jnp.zeros((SEGS, LANES), F32)
        state = lax.fori_loop(0, length, advance, (zero,) * modes, unroll=4)
        for m in range(modes):
            ends = state[m]
            for hop in (1, 2, 4):
                factor = spread(jnp.exp(-steps[m : m + 1] * float(length * hop)))
                ends = ends + factor * jnp.where(seg >= hop, pltpu.roll(ends, hop, 0), 0.0)
            end_ref[m : m + 1, lanes] = ends[SEGS - 1 : SEGS]
            carry_ref[m, :, lanes] = jnp.where(seg >= 1, pltpu.roll(ends, 1, 0), 0.0)


def gate_kernel(
    total, per_part, seat_ref, qf_ref, y_ref, carry_ref, decay_ref, residue_ref, *refs
):
    parts, (out_ref, mixed) = refs[:-2], refs[-2:]
    wanted = seat_ref[0] ^ (pl.program_id(0) // per_part)
    incoming = parts[0][...]
    for at in range(1, len(parts)):
        incoming = jnp.where(wanted == at, parts[at][...], incoming)

    rows, width = qf_ref.shape
    modes = decay_ref.shape[0]
    length = rows // SEGS
    begin = (lax.broadcasted_iota(jnp.int32, (SEGS, LANES), 0) * length).astype(F32)
    for block in range(width // LANES):
        lanes = slice(block * LANES, (block + 1) * LANES)
        steps = decay_ref[:, lanes] / total
        decays = jnp.exp(-steps)
        weights = residue_ref[:, lanes] * jnp.sqrt(2.0 * steps) * decays
        decay = [spread(decays[m : m + 1]) for m in range(modes)]
        tail = []
        for m in range(modes):
            reach = jnp.exp(-spread(steps[m : m + 1]) * begin)
            held = carry_ref[m, :, lanes] + reach * spread(incoming[m : m + 1, lanes])
            tail.append(spread(weights[m : m + 1]) * held)

        def advance(i, tail):
            mixed[block, pl.ds(i, SEGS, stride=length), :] = y_ref[i, :, lanes] + tree_sum(tail)
            return tuple(d * s for d, s in zip(decay, tail))

        lax.fori_loop(0, length, advance, tuple(tail), unroll=4)
    for block in range(width // LANES):
        lanes = slice(block * LANES, (block + 1) * LANES)
        out_ref[:, lanes] = (qf_ref[:, lanes].astype(F32) * mixed[block]).astype(BF16)


def column_call(body, name, arrays, outs, scratch, width, chan_count):
    def spec(shape):
        if shape[-1] != chan_count:
            return pl.BlockSpec(shape, lambda c: (0,) * len(shape))
        return pl.BlockSpec(shape[:-1] + (width,), lambda c: (0,) * (len(shape) - 1) + (c,))

    return pl.pallas_call(
        body,
        grid=(chan_count // width,),
        in_specs=[spec(a.shape) for a in arrays],
        out_specs=[spec(o.shape) for o in outs],
        out_shape=outs,
        scratch_shapes=scratch,
        compiler_params=pltpu.CompilerParams(vmem_limit_bytes=VMEM_GRANT),
        name=name,
    )(*arrays)


def local_rows(q_proj, k_proj, v_proj, rims, short_filter, residue, decay_rate):
    rows, chan_count = q_proj.shape
    modes = decay_rate.shape[0]
    total = float(rows * lax.axis_size("context"))
    width = lane_block(chan_count)
    return column_call(
        functools.partial(local_kernel, total), "local_pass",
        (q_proj, k_proj, v_proj, rims, short_filter, decay_rate, residue),
        [
            jax.ShapeDtypeStruct((rows, chan_count), BF16),
            jax.ShapeDtypeStruct((rows // SEGS, SEGS, chan_count), F32),
            jax.ShapeDtypeStruct((modes, SEGS, chan_count), F32),
            jax.ShapeDtypeStruct((modes, chan_count), F32),
        ],
        [
            pltpu.VMEM((3, rows + SEGS, LANES), F32),
            pltpu.VMEM((width // LANES, rows, LANES), F32),
        ],
        width, chan_count,
    )


def gate_rows(q_feat, y_local, carry, incoming, decay_rate, residue, seat):
    rows, chan_count = q_feat.shape
    modes = decay_rate.shape[0]
    total = float(rows * lax.axis_size("context"))
    width = lane_block(chan_count)
    per_part = incoming[0].shape[1] // width

    def cols(height):
        return pl.BlockSpec((height, width), lambda c, s: (0, c))

    return pl.pallas_call(
        functools.partial(gate_kernel, total, per_part),
        grid_spec=pltpu.PrefetchScalarGridSpec(
            num_scalar_prefetch=1,
            grid=(chan_count // width,),
            in_specs=[
                cols(rows),
                pl.BlockSpec((rows // SEGS, SEGS, width), lambda c, s: (0, 0, c)),
                pl.BlockSpec((modes, SEGS, width), lambda c, s: (0, 0, c)),
                cols(modes),
                cols(modes),
            ]
            + [pl.BlockSpec((modes, width), lambda c, s: (0, c % per_part)) for _ in incoming],
            out_specs=cols(rows),
            scratch_shapes=[pltpu.VMEM((width // LANES, rows, LANES), F32)],
        ),
        out_shape=jax.ShapeDtypeStruct((rows, chan_count), BF16),
        compiler_params=pltpu.CompilerParams(vmem_limit_bytes=VMEM_GRANT),
        name="gate_pass",
    )(seat.reshape(1), q_feat, y_local, carry, decay_rate, residue, *incoming)


def by_seat(seat, blocks):
    ordered = []
    for k in range(CREW):
        value = blocks[0]
        for j in range(1, CREW):
            value = jnp.where((seat ^ k) == j, blocks[j], value)
        ordered.append(value)
    return ordered


def plane_kernel(span, total, seat_ref, decay_ref, *refs):
    blocks, out_ref = refs[:CREW], refs[CREW]
    reach = jnp.exp(-(decay_ref[...] / total) * span)
    ends = by_seat(seat_ref[0], [b[...] for b in blocks])
    state = ends[0]
    for end in ends[1:]:
        state = reach * state + end
    out_ref[...] = state


def incoming_kernel(span, total, seat_ref, decay_ref, *refs):
    blocks, planes = refs[:CREW], refs[CREW : CREW + PLANES - 1]
    outs = refs[CREW + PLANES - 1 :]
    steps, seat = decay_ref[...] / total, seat_ref[0]
    ends = by_seat(seat, [b[...] for b in blocks])
    reach, reach_plane = jnp.exp(-steps * span), jnp.exp(-steps * (span * CREW))
    state = planes[-1][...]
    for plane in planes[-2::-1]:
        state = reach_plane * state + plane[...]
    states = [state]
    for end in ends[:-1]:
        states.append(reach * states[-1] + end)
    for out_ref, value in zip(outs, by_seat(seat, states)):
        out_ref[...] = value


def state_call(body, name, seat, steps, ends, arrays, out_count):
    modes, quarter = arrays[0].shape

    def owned(_, s):
        return (0, s[0])

    own = pl.BlockSpec((modes, quarter), owned)
    whole = pl.BlockSpec((modes, quarter), lambda _, s: (0, 0))
    shape = jax.ShapeDtypeStruct((modes, quarter), F32)
    return pl.pallas_call(
        body,
        grid_spec=pltpu.PrefetchScalarGridSpec(
            num_scalar_prefetch=1,
            grid=(1,),
            in_specs=[own, own] + [whole] * len(arrays),
            out_specs=[whole] * out_count,
        ),
        out_shape=[shape] * out_count,
        name=name,
    )(seat.reshape(1), steps, ends, *arrays)


def product_kernel(relayed_count, token_count, pick_ref, *refs):
    refs = list(refs)
    relayed = [refs.pop(0) for _ in range(relayed_count)]
    gathered_ref = None if relayed else refs.pop(0)
    tokens = [refs.pop(0) for _ in range(token_count)]
    kept_ref, sent_ref, total = refs[:3]
    step = pl.program_id(0)

    @pl.when(step == 0)
    def _():
        total[...] = jnp.zeros_like(total)

    if relayed:
        joined = refs[3]
        feat = relayed[0].shape[0]
        for plane in range(PLANES):
            for here in range(PLANES):

                @pl.when(pick_ref[1] == here)
                def _():
                    source = relayed[PLANES - 1 + here - plane]
                    joined[plane * feat : (plane + 1) * feat, :] = source[...]

        weights = joined[...]
    else:
        planes, feat, width = gathered_ref.shape
        weights = gathered_ref[...].reshape(planes * feat, width)
    for j, token in enumerate(tokens):
        total[j] += lax.dot_general(
            weights, token[...], (((1,), (1,)), ((), ())), preferred_element_type=F32
        )

    @pl.when(step == pl.num_programs(0) - 1)
    def _():
        middle = total.shape[1] // 2
        for side, outs in ((0, (kept_ref, sent_ref)), (1, (sent_ref, kept_ref))):

            @pl.when(pick_ref[0] == side)
            def _():
                outs[0][...] = total[:, :middle, :].astype(BF16)
                outs[1][...] = total[:, middle:, :].astype(BF16)


def project(picks, weights, tokens):
    rows, depth = tokens[0].shape
    width = 1024 if depth % 1024 == 0 else LANES
    relayed = weights if isinstance(weights, list) else []
    scratch = []
    if relayed:
        feat = relayed[0].shape[0]
        specs = [pl.BlockSpec((feat, width), lambda c, _: (0, c)) for _ in relayed]
        scratch = [pltpu.VMEM((PLANES * feat, width), BF16)]
    else:
        feat = weights.shape[1]
        specs = [pl.BlockSpec((PLANES, feat, width), lambda c, _: (0, 0, c))]
        weights = [weights]
    shape = (len(tokens), PLANES * feat // 2, rows)
    return pl.pallas_call(
        functools.partial(product_kernel, len(relayed), len(tokens)),
        grid_spec=pltpu.PrefetchScalarGridSpec(
            num_scalar_prefetch=1,
            grid=(depth // width,),
            in_specs=specs + [pl.BlockSpec((rows, width), lambda c, _: (0, c)) for _ in tokens],
            out_specs=[pl.BlockSpec(shape, lambda c, _: (0, 0, 0))] * 2,
            scratch_shapes=[pltpu.VMEM((len(tokens), PLANES * feat, rows), F32)] + scratch,
        ),
        out_shape=[jax.ShapeDtypeStruct(shape, BF16)] * 2,
        compiler_params=pltpu.CompilerParams(vmem_limit_bytes=VMEM_GRANT),
        cost_estimate=pl.CostEstimate(
            flops=1, bytes_accessed=4 * len(tokens) * rows * depth * 2 if relayed else 1,
            transcendentals=0,
        ),
        name="project",
    )(picks, *weights, *tokens)


def assemble_kernel(seat_ref, *refs):
    pieces, out_ref = refs[:-1], refs[-1]
    halves = PLANES // 2
    block = out_ref.shape[0] // halves
    feat = block // CREW
    for j in range(CREW):
        begin = 0
        for piece in pieces[j::CREW]:
            size = piece.shape[0] // halves
            for half in range(halves):
                at = half * block + (seat_ref[0] ^ j) * feat + begin
                at = pl.multiple_of(at, math.gcd(size, begin) if begin else size)
                out_ref[pl.ds(at, size), :] = piece[half * size : (half + 1) * size, :]
            begin += size


def assemble(seat, pieces):
    rows = pieces[0].shape[1]
    vmem = pl.BlockSpec(memory_space=pltpu.VMEM)
    return pl.pallas_call(
        assemble_kernel,
        in_specs=[pl.BlockSpec(memory_space=pltpu.SMEM)] + [vmem] * len(pieces),
        out_specs=vmem,
        out_shape=jax.ShapeDtypeStruct((sum(p.shape[0] for p in pieces), rows), BF16),
        compiler_params=pltpu.CompilerParams(vmem_limit_bytes=VMEM_GRANT),
        name="assemble",
    )(seat.reshape(1), *pieces)


def tails_kernel(q_ref, k_ref, v_ref, out_ref):
    lead = LEAD
    for which, ref in enumerate((q_ref, k_ref, v_ref)):
        rows = ref[...].astype(F32)
        out_ref[which * lead : (which + 1) * lead, :] = rows[rows.shape[0] - lead :]
    out_ref[3 * lead :, :] = jnp.zeros((out_ref.shape[0] - 3 * lead, out_ref.shape[1]), F32)


def gather_rims(q_proj, k_proj, v_proj):
    size = lax.axis_size("context")
    rows, chan_count = q_proj.shape
    last = pl.BlockSpec((16, chan_count), lambda i: (rows // 16 - 1, 0))
    tails = pl.pallas_call(
        tails_kernel,
        grid=(1,),
        in_specs=[last] * 3,
        out_specs=pl.BlockSpec((SEGS, chan_count), lambda i: (0, 0)),
        out_shape=jax.ShapeDtypeStruct((SEGS, chan_count), F32),
        compiler_params=pltpu.CompilerParams(vmem_limit_bytes=VMEM_GRANT),
        name="tails",
    )(q_proj, k_proj, v_proj)
    return lax.ppermute(tails, "context", [(i, i + 1) for i in range(size - 1)])


def per_device(q_proj, k_proj, v_proj, short_filter, residue, decay_rate, out_weight):
    place, size = lax.axis_index("context"), lax.axis_size("context")

    rows = q_proj.shape[0]
    rims = gather_rims(q_proj, k_proj, v_proj)
    q_feat, y_local, carry, ends = local_rows(
        q_proj, k_proj, v_proj, rims, short_filter, residue, decay_rate
    )
    gathered = lax.all_gather(ends, "context")
    gaps = (place - 1 - jnp.arange(size))[:, None, None]
    reach = jnp.exp(-(decay_rate / float(rows * size))[None] * (gaps * rows).astype(F32))
    incoming = jnp.sum(jnp.where(gaps >= 0, reach * gathered, 0.0), axis=0)
    gated = gate_rows(
        q_feat, y_local, carry, [incoming], decay_rate, residue, jnp.int32(0)
    )
    partial_terms = lax.dot_general(
        lax.all_gather(out_weight, "context", axis=0, tiled=True),
        gated,
        (((1,), (1,)), ((), ())),
        preferred_element_type=F32,
    )
    return lax.psum_scatter(
        partial_terms.astype(BF16), "tensor", scatter_dimension=0, tiled=True
    )


def swap(block, mask):
    size = lax.axis_size("context")
    return lax.ppermute(block, "context", [(i, i ^ mask) for i in range(size)])


def shift(block, distance):
    size = lax.axis_size("context")
    moves = [(i, i + distance) for i in range(size) if 0 <= i + distance < size]
    return lax.ppermute(block, "context", moves)


def per_device_planes(q_proj, k_proj, v_proj, short_filter, residue, decay_rate, out_weight):
    size = lax.axis_size("context")
    seat = lax.axis_index("context") % CREW
    side = lax.axis_index("tensor")
    rows, feat = q_proj.shape[0], out_weight.shape[0]
    quarter = q_proj.shape[1] // CREW
    span = float(rows)
    spans = (span, span * size)
    columns = [[p * CREW + s for p in range(PLANES)] for s in range(CREW)]
    cut = feat * 3 // 4
    most, k_proj = lax.optimization_barrier((out_weight[:cut], k_proj))
    gathered = lax.all_gather(most, "context", axis_index_groups=columns)
    picks = jnp.stack([side, lax.axis_index("context") // CREW]).astype(jnp.int32)

    def hops(block, moves):
        return lax.ppermute(
            block, "context",
            [(a * CREW + s, b * CREW + s) for a, b in moves for s in range(CREW)],
        )

    rims = gather_rims(q_proj, k_proj, v_proj)
    q_feat, y_local, carry, ends = local_rows(
        q_proj, k_proj, v_proj, rims, short_filter, residue, decay_rate
    )
    blocks = [
        swap(lax.dynamic_slice_in_dim(ends, (seat ^ j) * quarter, quarter, 1), j)
        for j in range(1, CREW)
    ]
    total = state_call(
        functools.partial(plane_kernel, *spans), "plane_state", seat, decay_rate, ends, blocks, 1
    )[0]
    planes = [shift(total, hop * CREW) for hop in range(1, PLANES)]
    planes, own = lax.optimization_barrier((planes, out_weight[cut:]))
    mine = state_call(
        functools.partial(incoming_kernel, *spans), "incoming_state",
        seat, decay_rate, ends, blocks + planes, CREW,
    )
    incoming = [mine[0]] + [swap(mine[j], j) for j in range(1, CREW)]
    gated = gate_rows(q_feat, y_local, carry, incoming, decay_rate, residue, seat)
    beside = swap(gated, 1)
    far = swap(gated, 2)
    up1, down1 = shift(own, CREW), shift(own, -CREW)
    up1, down1, outward = lax.optimization_barrier((up1, down1, own))
    direct = [
        hops(up1, [(1, 2), (2, 3)]), hops(down1, [(2, 1), (1, 0)]), hops(outward, [(0, 3), (3, 0)])
    ]

    def added(kept, arrived):
        return [
            (kept[at].astype(F32) + arrived[at].astype(F32)).astype(BF16)
            for at in range(kept.shape[0])
        ]

    def deal(parts, members):
        return [swap(part, j) if j else part for part, j in zip(parts, members)]

    def finish(kept, arrived, members):
        return deal(added(kept, arrived), members)

    near = [gated, beside]
    near_kept, sent = project(picks, gathered, near)
    near_kept, far = lax.optimization_barrier((near_kept, far))
    near_arrived = lax.ppermute(sent, "tensor", [(0, 1), (1, 0)])

    def start_far(far):
        beyond = [far, swap(far, 1)]
        return (*project(picks, gathered, beyond), beyond[1])

    def no_far(far):
        empty = jnp.zeros((2, PLANES * cut // 2, rows), BF16)
        return empty, empty, far

    place = lax.axis_index("context")
    far_kept, sent, last_token = lax.cond(place < size, start_far, no_far, far)
    beyond = [far, last_token]
    far_arrived = lax.ppermute(sent, "tensor", [(0, 1), (1, 0)])
    far_kept, direct = lax.optimization_barrier((far_kept, direct))
    up2, down2, ends = direct
    relayed = [ends, down2, down1, own, up1, up2, ends]
    last_kept, last_sent = project(picks, relayed, near + beyond)
    last_kept, near_arrived = lax.optimization_barrier((last_kept, near_arrived))
    far_pieces = deal(added(far_kept, far_arrived), (2, 3))
    last_arrived = lax.ppermute(last_sent, "tensor", [(0, 1), (1, 0)])
    pieces = finish(near_kept, near_arrived, (0, 1)) + far_pieces
    pieces += finish(last_kept, last_arrived, (0, 1, 2, 3))
    return assemble(seat, pieces)


def solution(mesh):
    planes = mesh.shape["tensor"] == 2 and mesh.shape["context"] == CREW * PLANES
    return jax.shard_map(
        per_device_planes if planes else per_device,
        mesh=mesh,
        in_specs=(
            P("context", "tensor"),
            P("context", "tensor"),
            P("context", "tensor"),
            P(None, None, "tensor"),
            P(None, "tensor"),
            P(None, "tensor"),
            P("context", "tensor"),
        ),
        out_specs=P("tensor", "context"),
        check_vma=False,
    )
```
